256 devices in a mesh: comp: 2 (over core), aa: 8 (over z_hi, y), ba: 16 (over x, z_lo).
Axes of the slice: x: 4, y: 4, z: 8 (z_hi: 2, z_lo: 4; z = z_hi * 4 + z_lo), core: 2. Of those that a mesh axis runs over, the one named last changes fastest.
Arguments:
- legendre: bfloat16 [640, 32, 1280], P('aa'), may hold values from -0.15625 to 0.15625
- coefficients: bfloat16 [2, 640, 2, 64, 1280], P('comp', 'aa', None, 'ba'), may hold values from -0.1796875 to 0.1796875
- cycle_points: int32 [32], replicated, may hold values from 1024 to 4096, as said below
- spectra: float32 [128, 512, 1296], P('aa', 'ba', 'comp'), may hold values from 0.05 to 2
- sea_mask: int32 [128, 512], P('aa', 'ba'), may hold values 0 or 1
- wind_column: int32 [128, 512], P('aa'), may hold values from 0 to 4095, as said below
- roughness_source: int32 [32, 4096], P('aa', 'ba'), may hold values from 0 to 8191, as said below
Outputs:
- grid_winds: bfloat16 [2, 32, 64, 4096], P('comp', 'aa', None, 'ba')
- wave_spectra: float32 [128, 512, 1296], P('aa', 'ba', 'comp')
- charnock: float32 [32, 4096], P('aa', 'ba')
The draws below stay inside these ranges and needn't reach their ends.
Inputs may be any that keep to these rules, and one draw needn't show every extreme that they name: `cycle_points`: at least a quarter of 4096; one cycle has exactly 4096 points. `wind_column`: each value is below the point count of cycle row // 4. `roughness_source`: the row within the band is one of the 4 rows (l mod 4) * 4 onward.
All inputs are finite; a program needn't handle non-finite values. No bound on the sum of `sea_mask` on one device may be relied on, other than what follows from the above.
Results may differ from the reference program's by a relative error of at most 0.0046.
The reference program's roundings to bfloat16 on the way count: a program that leaves them out, or rounds other values in their place, can miss the bound.
Values may be sent and summed in bfloat16 or wider, within the bound.
A program may use at most 64 MiB of HBM per device.

```python
import math
import jax
import jax.numpy as jnp
from jax import lax

MW = 640
NT = 1280
LEV = 64
LON = 4096
LAT_DEV = 4
CYCLE_ROWS = 4
NDIR = 36
NFREQ = 36
WSTEPS = 2
LAT = 32
WLAT_DEV = 16
WLAT = 128
WLON = 512
BINS = 1296
N_AA = 8


def point_counts(key):
    subkey = jax.random.fold_in(key, 17)
    drawn = jax.random.randint(jax.random.fold_in(subkey, 1), (LAT,), LON // 4, LON + 1)
    fullest = jax.random.randint(jax.random.fold_in(subkey, 2), (), 0, LAT)
    return jnp.where(jnp.arange(LAT) == fullest, LON, drawn).astype(jnp.int32)


def draw_cycle_points(key, part):
    return point_counts(key)


def draw_wind_column(key, part):
    counts = point_counts(key)
    row_cycles = jnp.arange(WLAT) // CYCLE_ROWS
    per_row = counts[row_cycles][:, None]
    columns = jnp.arange(WLON)[None, :]
    centred = (2 * columns + 1) * per_row // (2 * WLON)
    jitter = jax.random.randint(jax.random.fold_in(key, 23), (WLAT, WLON), -2, 3)
    return ((centred + jitter + per_row) % per_row).astype(jnp.int32)


def draw_roughness_source(key, part):
    counts = point_counts(key)[:, None]
    cycles = jnp.arange(LAT)[:, None]
    slot_index = jnp.arange(LON)[None, :]
    row_pick = cycles % LAT_DEV * CYCLE_ROWS + jax.random.randint(jax.random.fold_in(key, 29), (LAT, LON), 0, CYCLE_ROWS)
    column = (2 * slot_index + 1) * WLON // (2 * counts)
    column = column + jax.random.randint(jax.random.fold_in(key, 31), (LAT, LON), -1, 2)
    column = jnp.clip(column, 0, WLON - 1)
    return (row_pick * WLON + column).astype(jnp.int32)


def place_ends(array, own_key, smallest, top_value):
    spot = [jax.random.randint(jax.random.fold_in(own_key, axis), (), 0, length) for axis, length in enumerate(array.shape)]
    widest = array.shape.index(max(array.shape))
    next_to = spot[:widest] + [(spot[widest] + 1) % array.shape[widest]] + spot[widest + 1:]
    return array.at[tuple(spot)].set(smallest).at[tuple(next_to)].set(top_value)


def levels(stream_key, dims, cuts, low, largest):
    loudness = 1.0
    for position, parts in cuts:
        heights = jax.random.uniform(jax.random.fold_in(jax.random.fold_in(stream_key, 6), position), (parts,), jnp.float32, low / len(cuts), largest / len(cuts))
        loudness = loudness * jnp.repeat(jnp.exp(heights), dims[position] // parts).reshape((-1,) + (1,) * (len(dims) - 1 - position))
    return loudness


def bell_draw(stream_key, extent, spread, most, split=(), kind=jnp.bfloat16):
    array = spread * jax.random.normal(stream_key, extent, jnp.float32)
    if split:
        array = array * levels(stream_key, extent, split, -0.22, 0.18)
    return jnp.clip(array, -most, most).astype(kind)


def setup_inputs(seed: int = 0) -> dict:
    seeds = jax.random.split(jax.random.key(seed), 8)
    return {
        "legendre": bell_draw(seeds[0], (MW, LAT, NT), NT ** -0.5, 0.15625, ((0, 8),)),
        "coefficients": bell_draw(seeds[1], (2, MW, 2, LEV, NT), 0.03, 0.1796875, ((0, 2), (1, 8), (3, 16))),
        "cycle_points": draw_cycle_points(jax.random.fold_in(seeds[7], 71), 0),
        "spectra": jnp.clip(jnp.exp(math.log(2.0) - 3.6888794 * jax.random.uniform(seeds[3], (WLAT, WLON, BINS), jnp.float32) ** levels(seeds[3], (WLAT, WLON, BINS), ((0, 8), (1, 16), (2, 2)), -0.2, 0.2)), 0.05, 2.0),
        "sea_mask": place_ends((jax.random.randint(seeds[4], (WLAT, WLON), 0, 3) < 2).astype(jnp.int32), jax.random.fold_in(seeds[4], 1), 0, 1),
        "wind_column": draw_wind_column(jax.random.fold_in(seeds[7], 71), 0),
        "roughness_source": draw_roughness_source(jax.random.fold_in(seeds[7], 71), 0),
    }


two_pi = 2.0 * math.pi
gravity = 9.81
base_freq = 0.04177
courant = 0.45
wind_scale = 10.0
growth = 0.05
dissipation = 0.5
energy_ref = 8.0
mid_freq = 0.2
stress_coef = 0.03
drag_coef = 0.0012
stress_floor = 0.02

def cycle_tables(cycle_counts, slot_index, wave_count):
    orders = jnp.arange(wave_count, dtype=jnp.int32)
    remain = orders[None, :, None] * slot_index[None, None, :] % cycle_counts[:, None, None]
    phases = two_pi * remain.astype(jnp.float32) / cycle_counts.astype(jnp.float32)[:, None, None]
    weight = jnp.where(orders == 0, 1.0, 2.0).astype(jnp.float32)[None, :, None]
    active = slot_index[None, None, :] < cycle_counts[:, None, None]
    cosine_part = jnp.where(active, weight * jnp.cos(phases), 0.0)
    sine_part = jnp.where(active, -weight * jnp.sin(phases), 0.0)
    return jnp.stack([cosine_part, sine_part], axis=1).astype(jnp.bfloat16)

def bin_constants(directions, freq_index):
    heading = two_pi * (directions.astype(jnp.float32) + 0.5) / NDIR
    freq_step = 35.0 / (NFREQ - 1)
    period_ratio = jnp.exp(-math.log(1.1) * freq_step * freq_index.astype(jnp.float32))
    frequency = base_freq / period_ratio
    cosine_dir = jnp.cos(heading)
    sine_dir = jnp.sin(heading)
    drift_east = courant * period_ratio * cosine_dir
    drift_north = courant * period_ratio * sine_dir
    inverse_speed = two_pi * frequency / gravity
    bin_width = 0.1 * frequency * (two_pi / NDIR)
    return (frequency, cosine_dir, sine_dir, drift_east, drift_north, inverse_speed, bin_width)

def advect(padded, drift_east, drift_north):
    centre = padded[1:-1, 1:-1]
    western = padded[1:-1, :-2]
    eastern = padded[1:-1, 2:]
    southern = padded[:-2, 1:-1]
    northern = padded[2:, 1:-1]
    east_pos = jnp.maximum(drift_east, 0.0)
    east_neg = jnp.minimum(drift_east, 0.0)
    north_pos = jnp.maximum(drift_north, 0.0)
    north_neg = jnp.minimum(drift_north, 0.0)
    return centre - east_pos * (centre - western) - east_neg * (eastern - centre) - north_pos * (centre - southern) - north_neg * (northern - centre)

def wind_terms(density, east_wind, north_wind, cosine_dir, sine_dir, inverse_speed, bin_width):
    alignment = (east_wind[..., None] * cosine_dir + north_wind[..., None] * sine_dir) * inverse_speed
    wind_gain = growth * jnp.maximum(alignment - 1.0, 0.0)
    energy_part = lax.optimization_barrier(jnp.sum(density * bin_width, axis=-1))
    stress_part = lax.optimization_barrier(jnp.sum(wind_gain * density * alignment * bin_width, axis=-1))
    return (wind_gain, energy_part, stress_part)

def finish(density, wind_gain, energy, stress, east_wind, north_wind, frequency):
    decay_rate = dissipation * (frequency / mid_freq) * jnp.square(energy / energy_ref)[..., None]
    spectra_after = density * (1.0 + wind_gain) / (1.0 + decay_rate)
    air_stress = drag_coef * (east_wind * east_wind + north_wind * north_wind) + stress_floor
    roughness = jnp.sqrt(1.0 + stress_coef * stress / air_stress)
    return (spectra_after, roughness)

def reference(legendre, coefficients, cycle_points, spectra, sea_mask, wind_column, roughness_source):
    degrees = jnp.arange(NT, dtype=jnp.int32)

    def legendre_order(order_index):
        legendre_row = lax.dynamic_index_in_dim(legendre, order_index, 0, keepdims=False)
        legendre_row = jnp.where(degrees[None, :] >= order_index, legendre_row, jnp.zeros((), jnp.bfloat16))
        coeff_block = lax.dynamic_index_in_dim(coefficients, order_index, 1, keepdims=False)
        return jnp.einsum('ln,spcn->lspc', legendre_row.astype(jnp.float32), coeff_block.astype(jnp.float32))
    fourier = lax.map(legendre_order, jnp.arange(MW, dtype=jnp.int32)).astype(jnp.bfloat16)
    slot_index = jnp.arange(LON, dtype=jnp.int32)

    def synthesize(cycle_index):
        cycle_count = lax.dynamic_slice_in_dim(cycle_points, cycle_index, 1)
        tables = cycle_tables(cycle_count, slot_index, MW)[0]
        cycle_block = lax.dynamic_index_in_dim(fourier, cycle_index, 1, keepdims=False)
        grid_field = jnp.einsum('mspc,pmk->sck', cycle_block.astype(jnp.float32), tables.astype(jnp.float32))
        return grid_field.astype(jnp.bfloat16)
    grid_field = lax.map(synthesize, jnp.arange(LAT, dtype=jnp.int32))
    grid_winds = jnp.transpose(grid_field, (1, 0, 2, 3))
    bin_index = jnp.arange(NDIR * NFREQ, dtype=jnp.int32)
    frequency, cosine_dir, sine_dir, drift_east, drift_north, inverse_speed, bin_width = bin_constants(bin_index // NFREQ, bin_index % NFREQ)
    sea_float = sea_mask.astype(jnp.float32)[:, :, None]
    density = spectra * sea_float
    for substep in range(WSTEPS):
        padded = jnp.pad(density, ((1, 1), (1, 1), (0, 0)))
        density = advect(padded, drift_east, drift_north) * sea_float
    lowest = grid_winds[:, :, 0, :].astype(jnp.float32)
    repeated = jnp.repeat(lowest, CYCLE_ROWS, axis=1)
    picked = jnp.take_along_axis(repeated, jnp.broadcast_to(wind_column[None], (2, WLAT, WLON)), axis=2)
    east_wind = wind_scale * picked[0]
    north_wind = wind_scale * picked[1]
    wind_gain, energy, stress = wind_terms(density, east_wind, north_wind, cosine_dir, sine_dir, inverse_speed, bin_width)
    wave_spectra, roughness = finish(density, wind_gain, energy, stress, east_wind, north_wind, frequency)
    band_ratio = roughness.reshape(N_AA, WLAT_DEV * WLON)
    per_cycle = jnp.repeat(band_ratio, LAT_DEV, axis=0)
    values = jnp.take_along_axis(per_cycle, roughness_source, axis=1)
    active = slot_index[None, :] < cycle_points[:, None]
    charnock = jnp.where(active, values, 0.0)
    return (grid_winds, wave_spectra, charnock)
```

```python
import functools
import math

import numpy as np

import jax
import jax.numpy as jnp
from jax import lax
from jax.experimental import pallas as pl
from jax.experimental.pallas import tpu as pltpu
from jax.sharding import PartitionSpec as P

LON = 4096
NDIR = 36
NFREQ = 36
F32 = jnp.float32
BF16 = jnp.bfloat16
MESH = pl.DeviceIdType.MESH

N_A = 8
N_B = 16
N_X = 4
N_Z = 4
WAVES = 640
BLOCK = WAVES // N_A
CYCLES = 4
SLOTS = LON // N_B
ROWS = 16
COLS = 32
HALF = NDIR * NFREQ // 2
POINTS = 128
TILES = [(j, min(128, HALF - j)) for j in range(0, HALF, 128)]


def bin_table():
    b = np.arange(NDIR * NFREQ)
    theta = 2 * np.pi * (b // NFREQ + 0.5) / NDIR
    ratio = np.exp(-math.log(1.1) * (b % NFREQ))
    freq = 0.04177 / ratio
    east = 0.45 * ratio * np.cos(theta)
    north = 0.45 * ratio * np.sin(theta)
    q = 2 * np.pi * freq / 9.81
    width = 0.1 * freq * (2 * np.pi / NDIR)
    rows = [
        np.abs(east),
        np.abs(north),
        1.0 - np.abs(east) - np.abs(north),
        np.sign(east),
        np.sign(north),
        10.0 * q * np.cos(theta),
        10.0 * q * np.sin(theta),
        width,
        0.5 * freq / 0.2,
    ]
    rows += [np.zeros_like(freq)] * (16 - len(rows))
    table = np.stack(rows).astype(np.float32)
    return np.stack([table[:, :HALF], table[:, HALF:]])


AE, AN, CC, SE, SN, QE, QN, WB, DF = range(9)


def poly(y2, coefs):
    acc = jnp.full_like(y2, coefs[-1])
    for c in coefs[-2::-1]:
        acc = acc * y2 + c
    return acc


SIN_C = [(-1.0) ** i / math.factorial(2 * i + 1) for i in range(7)]
COS_C = [(-1.0) ** i / math.factorial(2 * i) for i in range(7)]


def turn(mk, count, inv):
    rest = mk - jnp.floor(mk * inv + 0.5) * count
    y = (rest * inv) * math.pi
    y2 = y * y
    s = y * poly(y2, SIN_C)
    c = poly(y2, COS_C)
    return 1.0 - 2.0 * s * s, 2.0 * s * c


def rcopy(src, dst, send, recv, device):
    return pltpu.make_async_remote_copy(
        src_ref=src, dst_ref=dst, send_sem=send, recv_sem=recv, device_id=device, device_id_type=MESH
    )


def diagonal():
    return lax.broadcasted_iota(jnp.int32, (POINTS, 128), 0) == lax.broadcasted_iota(
        jnp.int32, (POINTS, 128), 1
    )


def spread(row):
    kept = jnp.where(diagonal(), jnp.broadcast_to(row, (POINTS, 128)), 0.0)
    return jnp.broadcast_to(jnp.sum(kept, axis=1, keepdims=True), (POINTS, 128))


def kernel(
    cp_ref, msg_ref, spec_ref, pts_ref, rs_ref, cst_ref,
    gw_ref, ws_ref, ch_ref,
    a2a, gath, gperm, l0, table, ca, sa, buf_a, buf_b, d2, edge, edge_in,
    mask_b, east_b, north_b, en, en_in, stress_b, wind, wind_in, st, st_in, rough,
    a_send, a_recv, g_send, g_recv, l_send, l_recv, h_send, h_recv, c_send, c_recv, r_send, r_recv,
):
    s = lax.axis_index("comp")
    a = lax.axis_index("aa")
    b = lax.axis_index("ba")
    x, z = b // N_Z, b % N_Z
    partner = {"comp": 1 - s}

    barrier = pltpu.get_barrier_semaphore()
    pl.semaphore_signal(barrier, inc=1, device_id=partner, device_id_type=MESH)
    for d in range(1, N_A):
        pl.semaphore_signal(barrier, inc=1, device_id={"aa": lax.rem(a + d, N_A)}, device_id_type=MESH)
    for d in range(1, N_B):
        pl.semaphore_signal(barrier, inc=1, device_id={"ba": lax.rem(b + d, N_B)}, device_id_type=MESH)

    for l in range(CYCLES):
        mask_b[pl.ds(l * POINTS, POINTS), :] = spread(pts_ref[l : l + 1, :].astype(F32))

    def first(r, carry):
        m = mask_b[pl.ds(r * COLS, COLS), :]
        for j, w in TILES:
            v = spec_ref[r, :, j : j + w] * m[:, :w]
            buf_a[r + 1, 8 : 8 + COLS, j : j + w] = v
            edge[0, 0, r, :, j : j + w] = v[0:1, :]
            edge[0, 1, r, :, j : j + w] = v[COLS - 1 : COLS, :]
        return carry

    lax.fori_loop(0, ROWS, first, 0)

    pl.semaphore_wait(barrier, N_A + N_B - 1)

    sent = []
    for d in range(1, N_A):
        t = lax.rem(a + d, N_A)
        c = rcopy(msg_ref.at[t], a2a.at[a], a_send.at[d - 1], a_recv.at[a], {"aa": t})
        c.start()
        sent.append(c)

    def halo(buf, step):
        copies = [
            (a < N_A - 1, a > 0, rcopy(
                buf.at[ROWS, pl.ds(8, COLS)], buf.at[0, pl.ds(8, COLS)],
                h_send.at[step, 0], h_recv.at[step, 0], {"aa": lax.rem(a + 1, N_A)})),
            (a > 0, a < N_A - 1, rcopy(
                buf.at[1, pl.ds(8, COLS)], buf.at[ROWS + 1, pl.ds(8, COLS)],
                h_send.at[step, 1], h_recv.at[step, 1], {"aa": lax.rem(a + N_A - 1, N_A)})),
            (b < N_B - 1, b > 0, rcopy(
                edge.at[step, 1], edge_in.at[step, 0],
                h_send.at[step, 2], h_recv.at[step, 2], {"ba": lax.rem(b + 1, N_B)})),
            (b > 0, b < N_B - 1, rcopy(
                edge.at[step, 0], edge_in.at[step, 1],
                h_send.at[step, 3], h_recv.at[step, 3], {"ba": lax.rem(b + N_B - 1, N_B)})),
        ]
        return copies

    def halo_start(copies):
        for can, _, c in copies:
            pl.when(can)(c.start)

    def halo_land(copies, buf, step):
        for i, (_, comes, c) in enumerate(copies):
            pl.when(comes)(c.wait_recv)

            @pl.when(jnp.logical_not(comes))
            def _():
                if i < 2:
                    buf[0 if i == 0 else ROWS + 1, 8 : 8 + COLS, :] = jnp.zeros((COLS, HALF), F32)
                else:
                    edge_in[step, i - 2] = jnp.zeros((ROWS, 1, HALF), F32)

        def place(r, carry):
            for j, w in TILES:
                buf[r + 1, 7:8, j : j + w] = edge_in[step, 0, r, :, j : j + w]
                buf[r + 1, 8 + COLS : 9 + COLS, j : j + w] = edge_in[step, 1, r, :, j : j + w]
            return carry

        lax.fori_loop(0, ROWS, place, 0)

    def halo_sent(copies):
        for can, _, c in copies:
            pl.when(can)(c.wait_send)

    halo_a = halo(buf_a, 0)
    halo_start(halo_a)
    a2a[a] = msg_ref[a]

    def tables(l, k, active, lane, w):
        count = jnp.full((1, w), cp_ref[a * CYCLES + l], jnp.int32).astype(F32)
        inv = 1.0 / count
        u = lax.broadcasted_iota(jnp.int32, (WAVES // 8, w), 0).astype(F32) * 8.0
        cu, su = turn(u * k, count, inv)
        ca[:, :w] = cu
        sa[:, :w] = su
        v = lax.broadcasted_iota(jnp.int32, (8, w), 0).astype(F32)
        cv, sv = turn(v * k, count, inv)
        cv, sv = cv * active, sv * active

        def block(i, carry):
            near = pl.ds(pl.multiple_of(i * 8, 8), 8)
            c8, s8 = ca[near, :w], sa[near, :w]
            for h in range(4):
                j = i * 4 + h
                cs, ss = [], []
                for o in range(2):
                    c0 = c8[h * 2 + o : h * 2 + o + 1, :]
                    s0 = s8[h * 2 + o : h * 2 + o + 1, :]
                    cs.append(c0 * cv - s0 * sv)
                    ss.append(-(s0 * cv) - c0 * sv)
                at = pl.multiple_of(j * 16, 16)
                table[l, pl.ds(at, 16), lane : lane + w] = jnp.concatenate(cs, axis=0).astype(BF16)
                table[l, pl.ds(WAVES + at, 16), lane : lane + w] = jnp.concatenate(ss, axis=0).astype(BF16)
            return carry

        lax.fori_loop(0, WAVES // 64, block, 0)
        top = table[l, 0:16, lane : lane + w].astype(F32)
        row = lax.broadcasted_iota(jnp.int32, (16, w), 0)
        table[l, 0:16, lane : lane + w] = jnp.where(row == 0, top * 0.5, top).astype(BF16)

    slots = lax.broadcasted_iota(jnp.int32, (1, SLOTS), 1) + b * SLOTS
    for l in range(CYCLES):
        active = jnp.where(slots < cp_ref[a * CYCLES + l], 2.0, 0.0)
        tables(l, slots.astype(F32), active, 0, SLOTS)
        tables(l, pts_ref[4 + l : 5 + l, :].astype(F32), 2.0, SLOTS, POINTS)

    for d in range(1, N_A):
        o = lax.rem(a + N_A - d, N_A)
        rcopy(msg_ref.at[0], a2a.at[o], a_send.at[d - 1], a_recv.at[o], {"aa": o}).wait_recv()
    lane = lax.broadcasted_iota(jnp.int32, (16, 128), 1)
    for p in range(2):
        tiles = [jnp.zeros((16, 128), F32) for _ in range(WAVES // 128)]
        for o in range(N_A):
            t, shift = divmod(o * BLOCK, 128)
            piece = a2a[o, :, p * 128 : p * 128 + 128].astype(F32)
            if shift:
                piece = pltpu.roll(piece, shift, axis=1)
                tiles[t] = tiles[t] + jnp.where(lane >= shift, piece, 0.0)
                if shift + BLOCK > 128:
                    tiles[t + 1] = tiles[t + 1] + jnp.where(lane < shift, piece, 0.0)
            else:
                tiles[t] = tiles[t] + piece
        for t, tile in enumerate(tiles):
            gath[b, :, p * WAVES + t * 128 : p * WAVES + t * 128 + 128] = tile.astype(BF16)

            @pl.when(b == 0)
            def _():
                for l in range(CYCLES):
                    l0[p * 4 + l : p * 4 + l + 1, t * 128 : t * 128 + 128] = tile[4 * l : 4 * l + 1, :]

    low = [
        rcopy(l0, l0, l_send.at[d - 1], l_recv.at[0], {"ba": lax.rem(b + d, N_B)}) for d in range(1, N_B)
    ]

    @pl.when(b == 0)
    def _():
        for c in low:
            c.start()

    gathers = []

    def give(o, device):
        c = rcopy(gath.at[o], gath.at[o], g_send.at[len(gathers)], g_recv.at[o], {"ba": device})
        c.start()
        gathers.append(c)

    def arrived(o):
        rcopy(gath.at[o], gath.at[o], g_send.at[0], g_recv.at[o], {"ba": o}).wait_recv()

    x_peers = [lax.rem(x + d, N_X) * N_Z + z for d in (1, 3, 2)]
    for d in range(1, N_Z):
        give(b, x * N_Z + lax.rem(z + d, N_Z))
    for t in x_peers:
        give(b, t)

    def upwind(buf, r, j, w):
        c = lambda i: cst_ref[s, i : i + 1, j : j + w]
        here = buf[r + 1, 8 : 8 + COLS, j : j + w]
        ux = jnp.where(c(SE) > 0.0, buf[r + 1, 7 : 7 + COLS, j : j + w], buf[r + 1, 9 : 9 + COLS, j : j + w])
        uy = jnp.where(c(SN) > 0.0, buf[r, 8 : 8 + COLS, j : j + w], buf[r + 2, 8 : 8 + COLS, j : j + w])
        return here * c(CC) + ux * c(AE) + uy * c(AN)

    halo_land(halo_a, buf_a, 0)

    def second(r, carry):
        m = mask_b[pl.ds(r * COLS, COLS), :]
        for j, w in TILES:
            v = upwind(buf_a, r, j, w) * m[:, :w]
            buf_b[r + 1, 8 : 8 + COLS, j : j + w] = v
            edge[1, 0, r, :, j : j + w] = v[0:1, :]
            edge[1, 1, r, :, j : j + w] = v[COLS - 1 : COLS, :]
        return carry

    lax.fori_loop(0, ROWS, second, 0)
    halo_b = halo(buf_b, 1)
    halo_start(halo_b)

    for d in range(1, N_Z):
        o = x * N_Z + lax.rem(z + N_Z - d, N_Z)
        arrived(o)
        for t in x_peers:
            give(o, t)

    @pl.when(b > 0)
    def _():
        low[0].wait_recv()

    lowest = l0[...].astype(BF16)
    for l in range(CYCLES):
        pc = jnp.dot(lowest, table[l, 0:WAVES, SLOTS:], preferred_element_type=F32)
        ps = jnp.dot(lowest, table[l, WAVES:, SLOTS:], preferred_element_type=F32)
        value = (pc[l : l + 1, :] + ps[4 + l : 5 + l, :]).astype(BF16).astype(F32)
        wind[l : l + 1, :] = value
        wind[4 + l : 5 + l, :] = value
    wind_copy = rcopy(wind, wind_in, c_send.at[0], c_recv.at[0], partner)
    wind_copy.start()

    halo_land(halo_b, buf_b, 1)

    def third(r, carry):
        m = mask_b[pl.ds(r * COLS, COLS), :]
        total = jnp.zeros((COLS, 128), F32)
        for j, w in TILES:
            v = upwind(buf_b, r, j, w) * m[:, :w]
            d2[r, :, j : j + w] = v
            part = v * cst_ref[s, WB : WB + 1, j : j + w]
            if w == 128:
                total = total + part
            else:
                rest = jnp.sum(part, axis=1, keepdims=True)
        total = jnp.sum(total, axis=1, keepdims=True) + rest
        en[pl.ds(r * COLS, COLS), :] = jnp.broadcast_to(total, (COLS, 128))
        return carry

    lax.fori_loop(0, ROWS, third, 0)
    energy_copy = rcopy(en, en_in, c_send.at[1], c_recv.at[1], partner)
    energy_copy.start()

    wind_copy.wait_recv()
    mine, other = wind[...], wind_in[...]
    east = jnp.where(s == 0, mine, other)
    north = jnp.where(s == 0, other, mine)
    for l in range(CYCLES):
        east_b[pl.ds(l * POINTS, POINTS), :] = spread(east[l : l + 1, :])
        north_b[pl.ds(l * POINTS, POINTS), :] = spread(north[l : l + 1, :])
    air = 0.0012 * (100.0 * (east * east + north * north)) + 0.02

    def gain_of(e, n, r, j, w):
        c = lambda i: cst_ref[s, i : i + 1, j : j + w]
        align = e[:, :w] * c(QE) + n[:, :w] * c(QN)
        grown = 0.05 * jnp.maximum(align - 1.0, 0.0) * d2[r, :, j : j + w]
        return align, grown

    def fourth(r, carry):
        e = east_b[pl.ds(r * COLS, COLS), :]
        n = north_b[pl.ds(r * COLS, COLS), :]
        total = jnp.zeros((COLS, 128), F32)
        for j, w in TILES:
            align, grown = gain_of(e, n, r, j, w)
            part = grown * align * cst_ref[s, WB : WB + 1, j : j + w]
            if w == 128:
                total = total + part
            else:
                rest = jnp.sum(part, axis=1, keepdims=True)
        total = jnp.sum(total, axis=1, keepdims=True) + rest
        stress_b[pl.ds(r * COLS, COLS), :] = jnp.broadcast_to(total, (COLS, 128))
        return carry

    lax.fori_loop(0, ROWS, fourth, 0)
    for l in range(CYCLES):
        block = stress_b[pl.ds(l * POINTS, POINTS), :]
        row = jnp.sum(jnp.where(diagonal(), block, 0.0), axis=0, keepdims=True)
        st[l : l + 1, :] = row
        st[4 + l : 5 + l, :] = row
    stress_copy = rcopy(st, st_in, c_send.at[2], c_recv.at[2], partner)
    stress_copy.start()

    energy_copy.wait_recv()

    def fifth(r, carry):
        at = pl.ds(r * COLS, COLS)
        e, n = east_b[at, :], north_b[at, :]
        level = (en[at, :] + en_in[at, :]) * 0.125
        square = level * level
        for j, w in TILES:
            _, grown = gain_of(e, n, r, j, w)
            decay = square[:, :w] * cst_ref[s, DF : DF + 1, j : j + w]
            ws_ref[r, :, j : j + w] = (d2[r, :, j : j + w] + grown) / (1.0 + decay)
        return carry

    def roughness():
        stress_copy.wait_recv()
        rough[b] = jnp.sqrt(1.0 + 0.03 * (st[...] + st_in[...]) / air)
        copies = []
        for d in range(1, N_B):
            t = lax.rem(b + d, N_B)
            c = rcopy(rough.at[b], rough.at[b], r_send.at[d - 1], r_recv.at[b], {"ba": t})
            c.start()
            copies.append(c)
        return copies

    lax.fori_loop(0, ROWS, fifth, 0)
    rough_copies = roughness()

    for xd in range(1, N_X):
        for zd in range(N_Z):
            arrived(lax.rem(x + N_X - xd, N_X) * N_Z + lax.rem(z + zd, N_Z))
    out_row = lax.broadcasted_iota(jnp.int32, (256, 256), 0)
    in_row = (out_row % 64 // 4) * 16 + out_row // 64 * 4 + out_row % 4
    order = (lax.broadcasted_iota(jnp.int32, (256, 256), 1) == in_row).astype(F32).astype(BF16)
    for k in range(0, 2 * WAVES, 256):
        part = gath[:, :, k : k + 256].reshape(256, 256)
        gperm[:, k : k + 256] = jnp.dot(order, part, preferred_element_type=F32).astype(BF16)
    for l in range(CYCLES):
        gw_ref[0, l] = jnp.dot(
            gperm[l * 64 : l * 64 + 64, :], table[l, :, 0:SLOTS], preferred_element_type=F32
        ).astype(BF16)

    for d in range(1, N_B):
        o = lax.rem(b + N_B - d, N_B)
        rcopy(rough.at[o], rough.at[o], r_send.at[0], r_recv.at[o], {"ba": o}).wait_recv()
    for l in range(CYCLES):
        source = rs_ref[l : l + 1, :]
        low_part = ((source >> 9) & 3) * 32 + (source & 31)
        high_part = (source >> 5) & 15
        pick = (lax.broadcasted_iota(jnp.int32, (128, SLOTS), 0) == low_part).astype(F32).astype(BF16)
        values = rough[:, l, :]
        h0 = values.astype(BF16)
        r1 = values - h0.astype(F32)
        h1 = r1.astype(BF16)
        h2 = (r1 - h1.astype(F32)).astype(BF16)
        got = [jnp.dot(h, pick, preferred_element_type=F32) for h in (h0, h1, h2)]
        got = got[0] + (got[1] + got[2])
        keep = lax.broadcasted_iota(jnp.int32, (N_B, SLOTS), 0) == high_part
        row = jnp.sum(jnp.where(keep, got, 0.0), axis=0, keepdims=True)
        ch_ref[l : l + 1, :] = jnp.where(slots < cp_ref[a * CYCLES + l], row, 0.0)

    for c in sent + gathers + rough_copies + [wind_copy, energy_copy, stress_copy]:
        c.wait_send()
    halo_sent(halo_a)
    halo_sent(halo_b)

    @pl.when(b == 0)
    def _():
        for c in low:
            c.wait_send()


def per_device(legendre, coefficients, cycle_points, spectra, sea_mask, wind_column, roughness_source):
    band = lax.axis_index("aa")
    column = lax.axis_index("ba")
    degrees = jnp.arange(legendre.shape[2], dtype=jnp.int32)
    orders = band * BLOCK + jnp.arange(BLOCK, dtype=jnp.int32)
    masked = jnp.where(
        degrees[None, None, :] >= orders[:, None, None], legendre, jnp.zeros((), BF16)
    )
    fourier = jnp.einsum(
        "mln,mpcn->mlpc", masked, coefficients[0], preferred_element_type=F32
    ).astype(BF16)
    message = jnp.transpose(fourier.reshape(BLOCK, N_A, CYCLES, 2, 4), (1, 2, 4, 3, 0))
    message = jnp.pad(message, ((0, 0),) * 4 + ((0, 128 - BLOCK),)).reshape(N_A, 16, 256)
    own = lax.dynamic_slice_in_dim(wind_column, column * COLS, COLS, 1)
    points = jnp.concatenate([sea_mask.reshape(4, POINTS), own.reshape(4, POINTS)], axis=0)

    vmem = pl.BlockSpec(memory_space=pltpu.VMEM)
    dma = pltpu.SemaphoreType.DMA
    return pl.pallas_call(
        kernel,
        out_shape=(
            jax.ShapeDtypeStruct((1, CYCLES, 64, SLOTS), BF16),
            jax.ShapeDtypeStruct((ROWS, COLS, HALF), F32),
            jax.ShapeDtypeStruct((CYCLES, SLOTS), F32),
        ),
        in_specs=[pl.BlockSpec(memory_space=pltpu.SMEM)] + [vmem] * 5,
        out_specs=(vmem, vmem, vmem),
        scratch_shapes=[
            pltpu.VMEM((N_A, 16, 256), BF16),
            pltpu.VMEM((N_B, 16, 2 * WAVES), BF16),
            pltpu.VMEM((256, 2 * WAVES), BF16),
            pltpu.VMEM((8, WAVES), F32),
            pltpu.VMEM((CYCLES, 2 * WAVES, SLOTS + POINTS), BF16),
            pltpu.VMEM((WAVES // 8, SLOTS), F32),
            pltpu.VMEM((WAVES // 8, SLOTS), F32),
            pltpu.VMEM((ROWS + 2, COLS + 16, HALF), F32),
            pltpu.VMEM((ROWS + 2, COLS + 16, HALF), F32),
            pltpu.VMEM((ROWS, COLS, HALF), F32),
            pltpu.VMEM((2, 2, ROWS, 1, HALF), F32),
            pltpu.VMEM((2, 2, ROWS, 1, HALF), F32),
            pltpu.VMEM((ROWS * COLS, 128), F32),
            pltpu.VMEM((ROWS * COLS, 128), F32),
            pltpu.VMEM((ROWS * COLS, 128), F32),
            pltpu.VMEM((ROWS * COLS, 128), F32),
            pltpu.VMEM((ROWS * COLS, 128), F32),
            pltpu.VMEM((ROWS * COLS, 128), F32),
            pltpu.VMEM((8, 128), F32),
            pltpu.VMEM((8, 128), F32),
            pltpu.VMEM((8, 128), F32),
            pltpu.VMEM((8, 128), F32),
            pltpu.VMEM((N_B, 8, 128), F32),
            dma((N_A - 1,)), dma((N_A,)),
            dma((N_B - 1,)), dma((N_B,)),
            dma((N_B - 1,)), dma((1,)),
            dma((2, 4)), dma((2, 4)),
            dma((3,)), dma((3,)),
            dma((N_B - 1,)), dma((N_B,)),
        ],
        compiler_params=pltpu.CompilerParams(
            collective_id=0, has_side_effects=True, vmem_limit_bytes=48 * 1024 * 1024
        ),
    )(cycle_points, message, spectra, points, roughness_source, jnp.asarray(bin_table()))


def solution(mesh):
    in_specs = (
        P("aa", None, None),
        P("comp", "aa", None, "ba", None),
        P(),
        P("aa", "ba", "comp"),
        P("aa", "ba"),
        P("aa", None),
        P("aa", "ba"),
    )
    out_specs = (P("comp", "aa", None, "ba"), P("aa", "ba", "comp"), P("aa", "ba"))
    return jax.shard_map(
        per_device, mesh=mesh, in_specs=in_specs, out_specs=out_specs, check_vma=False
    )
```

```python
import math

import numpy as np

import jax
import jax.numpy as jnp
from jax import lax
from jax.experimental import pallas as pl
from jax.experimental.pallas import tpu as pltpu
from jax.sharding import PartitionSpec as P

LON = 4096
NDIR = 36
NFREQ = 36
F32 = jnp.float32
BF16 = jnp.bfloat16
MESH = pl.DeviceIdType.MESH

N_A = 8
N_B = 16
N_X = 4
N_Z = 4
WAVES = 640
BLOCK = WAVES // N_A
GROUPS = BLOCK // 8
NT = 1280
CYCLES = 4
SLOTS = LON // N_B
ROWS = 16
COLS = 32
HALF = NDIR * NFREQ // 2
POINTS = 128
TILES = [(j, min(128, HALF - j)) for j in range(0, HALF, 128)]


def bin_table():
    b = np.arange(NDIR * NFREQ)
    theta = 2 * np.pi * (b // NFREQ + 0.5) / NDIR
    ratio = np.exp(-math.log(1.1) * (b % NFREQ))
    freq = 0.04177 / ratio
    east = 0.45 * ratio * np.cos(theta)
    north = 0.45 * ratio * np.sin(theta)
    q = 2 * np.pi * freq / 9.81
    width = 0.1 * freq * (2 * np.pi / NDIR)
    rows = [
        np.abs(east),
        np.abs(north),
        1.0 - np.abs(east) - np.abs(north),
        np.sign(east),
        np.sign(north),
        10.0 * q * np.cos(theta),
        10.0 * q * np.sin(theta),
        width,
        0.5 * freq / 0.2,
    ]
    rows += [np.zeros_like(freq)] * (16 - len(rows))
    table = np.stack(rows).astype(np.float32)
    return np.stack([table[:, :HALF], table[:, HALF:]])


AE, AN, CC, SE, SN, QE, QN, WB, DF = range(9)


def poly(y2, coefs):
    acc = jnp.full_like(y2, coefs[-1])
    for c in coefs[-2::-1]:
        acc = acc * y2 + c
    return acc


SIN_C = [(-1.0) ** i / math.factorial(2 * i + 1) for i in range(7)]
COS_C = [(-1.0) ** i / math.factorial(2 * i) for i in range(7)]


def turn(mk, count, inv):
    rest = mk - jnp.floor(mk * inv + 0.5) * count
    y = (rest * inv) * math.pi
    y2 = y * y
    s = y * poly(y2, SIN_C)
    c = poly(y2, COS_C)
    return 1.0 - 2.0 * s * s, 2.0 * s * c


def rcopy(src, dst, send, recv, device):
    return pltpu.make_async_remote_copy(
        src_ref=src, dst_ref=dst, send_sem=send, recv_sem=recv, device_id=device, device_id_type=MESH
    )


def lanes(rows, width=128):
    return lax.broadcasted_iota(jnp.int32, (rows, width), 1)


def sublanes(rows, width=128):
    return lax.broadcasted_iota(jnp.int32, (rows, width), 0)


def spread(row, n):
    kept = jnp.where(sublanes(n, n) == lanes(n, n), jnp.broadcast_to(row, (n, n)), 0.0)
    return jnp.broadcast_to(jnp.sum(kept, axis=1, keepdims=True), (n, 128))


def one_hot(mask):
    return mask.astype(F32).astype(BF16)


def dot(x, y, dims=((1,), (0,))):
    return lax.dot_general(x, y, (dims, ((), ())), preferred_element_type=F32)


def kernel(
    cp_ref, leg_hbm, coef_hbm, spec_hbm, mask_hbm, wc_hbm, cst_hbm,
    gw_ref, ws_ref, rough,
    leg, coef, spec, mask_in, wc, cst_ref, sall, msg, a2a, a2x, gath, gperm, low_f, l0,
    table, ptable, ca, sa, buf_a, buf_b, d2, edge, edge_in,
    mask_b, east_b, north_b, part, part_in, st, st_in,
    i_sem, leg_sem, a_send, a_recv, x_send, x_recv, g_send, g_recv, l_send, l_recv, h_send, h_recv,
    c_send, c_recv, r_send, r_recv,
):
    s = lax.axis_index("comp")
    a = lax.axis_index("aa")
    b = lax.axis_index("ba")
    x, z = b // N_Z, b % N_Z
    partner = {"comp": 1 - s}

    coef_copy = pltpu.make_async_copy(coef_hbm, coef, i_sem.at[0])
    coef_copy.start()
    leg_copies = lambda g: pltpu.make_async_copy(
        leg_hbm.at[pl.ds(g * 8, 8)], leg.at[pl.ds(g * 8, 8)], leg_sem.at[g]
    )
    for g in range(GROUPS):
        leg_copies(g).start()
    small = [
        pltpu.make_async_copy(mask_hbm, mask_in, i_sem.at[1]),
        pltpu.make_async_copy(wc_hbm, wc, i_sem.at[2]),
        pltpu.make_async_copy(cst_hbm, cst_ref, i_sem.at[3]),
        pltpu.make_async_copy(spec_hbm, spec, i_sem.at[4]),
    ]
    for c in small:
        c.start()

    barrier = pltpu.get_barrier_semaphore()
    pl.semaphore_signal(barrier, inc=1, device_id=partner, device_id_type=MESH)
    for d in range(1, N_A):
        pl.semaphore_signal(barrier, inc=1, device_id={"aa": lax.rem(a + d, N_A)}, device_id_type=MESH)
    for d in range(1, N_B):
        pl.semaphore_signal(barrier, inc=1, device_id={"ba": lax.rem(b + d, N_B)}, device_id_type=MESH)

    @pl.when(b == 0)
    def _():
        for d in range(1, N_A):
            pl.semaphore_signal(
                barrier, inc=1, device_id={"comp": 1 - s, "aa": lax.rem(a + d, N_A)}, device_id_type=MESH
            )

    coef_copy.wait()

    def legendre(g, carry):
        rows = []
        for i in range(8):
            order = a * BLOCK + g * 8 + i
            block = jnp.concatenate([coef[g * 8 + i, p].astype(F32) for p in range(2)], axis=0)
            rows.append(jnp.where(lanes(8, NT) >= order, block, 0.0))
        rows = jnp.concatenate(rows, axis=0).astype(BF16)
        leg_copies(g).wait()
        cross = dot(rows, leg[pl.ds(g * 8, 8)].reshape(256, NT), ((1,), (1,)))
        at = pl.ds(pl.multiple_of(g * 8, 8), 8)
        for t in range(2):
            kept = cross[t * 32 : t * 32 + 8, t * 128 : t * 128 + 128]
            for q in range(1, 4):
                m = t * 4 + q
                kept = jnp.where(lanes(8) >= q * 32, cross[m * 8 : m * 8 + 8, t * 128 : t * 128 + 128], kept)
            sall[at, t * 128 : t * 128 + 128] = kept
        return carry

    lax.fori_loop(0, GROUPS, legendre, 0)

    i, o = sublanes(256, 256), lanes(256, 256)
    moved = dot(sall[...].astype(BF16), one_hot(o == (i & 31) // 4 * 32 + (i // 32) * 4 + (i & 3)))
    turned = {}
    for t in range(N_A):
        for q in range(3):
            acc = jnp.zeros((8, 128), F32)
            for g in range(q * 4, min(q * 4 + 4, GROUPS)):
                shift = 32 * ((g - t) % 4)
                key = (g, t // 4, shift)
                if key not in turned:
                    v = moved[g * 8 : g * 8 + 8, t // 4 * 128 : t // 4 * 128 + 128]
                    turned[key] = pltpu.roll(v, shift, axis=1) if shift else v
                at = lanes(8) // 32 == g % 4
                acc = jnp.where(at, turned[key], acc)
            msg[t, :, q * 128 : q * 128 + 128] = acc

    pl.semaphore_wait(barrier, N_A + N_B - 1 + jnp.where(b == 0, N_A - 1, 0))

    sent = []
    for d in range(1, N_A):
        t = lax.rem(a + d, N_A)
        c = rcopy(msg.at[t], a2a.at[a], a_send.at[d - 1], a_recv.at[a], {"aa": t})
        c.start()
        sent.append(c)
    crossed = []
    for d in range(N_A):
        t = lax.rem(a + d, N_A)
        crossed.append(
            rcopy(msg.at[t], a2x.at[a], x_send.at[d], x_recv.at[a], {"comp": 1 - s, "aa": t})
        )

    @pl.when(b == 0)
    def _():
        for c in crossed:
            c.start()

    a2a[a] = msg[a]

    for c in small:
        c.wait()
    sea = mask_in[...].astype(F32)
    for r in range(ROWS):
        mask_b[r * COLS : (r + 1) * COLS, :] = spread(sea[r : r + 1, :], COLS)

    def first(r, carry):
        m = mask_b[pl.ds(r * COLS, COLS), :]
        for j, w in TILES:
            v = spec[r, :, j : j + w] * m[:, :w]
            buf_a[r + 1, 8 : 8 + COLS, j : j + w] = v
            edge[0, 0, r, :, j : j + w] = v[0:1, :]
            edge[0, 1, r, :, j : j + w] = v[COLS - 1 : COLS, :]
        return carry

    lax.fori_loop(0, ROWS, first, 0)

    def halo(buf, step):
        return [
            (a < N_A - 1, a > 0, rcopy(
                buf.at[ROWS, pl.ds(8, COLS)], buf.at[0, pl.ds(8, COLS)],
                h_send.at[step, 0], h_recv.at[step, 0], {"aa": lax.rem(a + 1, N_A)})),
            (a > 0, a < N_A - 1, rcopy(
                buf.at[1, pl.ds(8, COLS)], buf.at[ROWS + 1, pl.ds(8, COLS)],
                h_send.at[step, 1], h_recv.at[step, 1], {"aa": lax.rem(a + N_A - 1, N_A)})),
            (b < N_B - 1, b > 0, rcopy(
                edge.at[step, 1], edge_in.at[step, 0],
                h_send.at[step, 2], h_recv.at[step, 2], {"ba": lax.rem(b + 1, N_B)})),
            (b > 0, b < N_B - 1, rcopy(
                edge.at[step, 0], edge_in.at[step, 1],
                h_send.at[step, 3], h_recv.at[step, 3], {"ba": lax.rem(b + N_B - 1, N_B)})),
        ]

    def halo_start(copies):
        for can, _, c in copies:
            pl.when(can)(c.start)

    def halo_land(copies, buf, step):
        for i, (_, comes, c) in enumerate(copies):
            pl.when(comes)(c.wait_recv)

            @pl.when(jnp.logical_not(comes))
            def _():
                if i < 2:
                    buf[0 if i == 0 else ROWS + 1, 8 : 8 + COLS, :] = jnp.zeros((COLS, HALF), F32)
                else:
                    edge_in[step, i - 2] = jnp.zeros((ROWS, 1, HALF), F32)

        for r in range(ROWS):
            buf[r + 1, 7:8, :] = edge_in[step, 0, r]
            buf[r + 1, 8 + COLS : 9 + COLS, :] = edge_in[step, 1, r]

    def halo_sent(copies):
        for can, _, c in copies:
            pl.when(can)(c.wait_send)

    halo_a = halo(buf_a, 0)
    halo_start(halo_a)

    def tables(out, l, k, active):
        w = k.shape[1]
        count = jnp.full((1, w), cp_ref[a * CYCLES + l], jnp.int32).astype(F32)
        inv = 1.0 / count
        cu, su = turn(sublanes(WAVES // 8, w).astype(F32) * 8.0 * k, count, inv)
        ca[:, :, :w] = cu.reshape(GROUPS, 8, w)
        sa[:, :, :w] = su.reshape(GROUPS, 8, w)
        cv, sv = turn(sublanes(8, w).astype(F32) * k, count, inv)
        cv, sv = cv * active, sv * active
        minus_c, minus_s = -cv, -sv

        def block(i, carry):
            for h in range(4):
                cs, ss = [], []
                for o in range(h * 2, h * 2 + 2):
                    c0, s0 = ca[i, o : o + 1, :w], sa[i, o : o + 1, :w]
                    cs.append(c0 * cv + s0 * minus_s)
                    ss.append(s0 * minus_c + c0 * minus_s)
                at = pl.multiple_of(i * 64 + h * 16, 16)
                out[l, pl.ds(at, 16), :] = jnp.concatenate(cs, axis=0).astype(BF16)
                out[l, pl.ds(WAVES + at, 16), :] = jnp.concatenate(ss, axis=0).astype(BF16)
            return carry

        lax.fori_loop(0, GROUPS, block, 0)
        top = out[l, 0:16, :].astype(F32)
        out[l, 0:16, :] = jnp.where(sublanes(16, w) == 0, top * 0.5, top).astype(BF16)

    near = wc[:, pl.ds(pl.multiple_of(b // 4 * 128, 128), 128)].astype(F32)
    near = pltpu.roll(near, (4 - b % 4) % 4 * COLS, axis=1)
    near = jnp.where(lanes(ROWS) < COLS, near, 0.0)
    side = near
    for q in range(1, 4):
        side = jnp.where(sublanes(ROWS) % 4 == q, pltpu.roll(near, q * COLS, axis=1), side)
    for l in range(CYCLES):
        tables(ptable, l, jnp.sum(side[l * 4 : l * 4 + 4, :], axis=0, keepdims=True), 2.0)

    i, o = sublanes(384, 512), lanes(384, 512)
    order = one_hot((o == (i & 3) * 128 + i // 4) & (i < BLOCK * 4))

    def compact(landed):
        wide = dot(landed[...].reshape(64, 384).astype(BF16), order)
        out = []
        for l in range(CYCLES):
            tiles = [jnp.zeros((8, 128), F32) for _ in range(WAVES // 128)]
            for c in range(N_A):
                t, shift = divmod(c * BLOCK, 128)
                piece = wide[c * 8 : c * 8 + 8, l * 128 : l * 128 + 128]
                if shift:
                    piece = pltpu.roll(piece, shift, axis=1)
                    tiles[t] = jnp.where(lanes(8) >= shift, piece, tiles[t])
                    if shift + BLOCK > 128:
                        tiles[t + 1] = jnp.where(lanes(8) < shift, piece, tiles[t + 1])
                else:
                    tiles[t] = jnp.where(lanes(8) < BLOCK, piece, tiles[t])
            out.append(tiles)
        return out

    def lowest(blocks, base):
        for l in range(CYCLES):
            for t in range(WAVES // 128):
                for p in range(2):
                    r = base + p * 4 + l
                    low_f[r : r + 1, t * 128 : t * 128 + 128] = blocks[l][t][p * 4 : p * 4 + 1, :]

    for d in range(1, N_A):
        c = lax.rem(a + N_A - d, N_A)
        rcopy(msg.at[0], a2a.at[c], a_send.at[d - 1], a_recv.at[c], {"aa": c}).wait_recv()
    blocks = compact(a2a)
    low = [
        rcopy(l0, l0, l_send.at[d - 1], l_recv.at[0], {"ba": lax.rem(b + d, N_B)}) for d in range(1, N_B)
    ]

    @pl.when(b == 0)
    def _():
        lowest(blocks, 0)
        for d in range(N_A):
            c = lax.rem(a + N_A - d, N_A)
            rcopy(msg.at[0], a2x.at[c], x_send.at[d], x_recv.at[c], {"comp": 1 - s, "aa": c}).wait_recv()
        lowest(compact(a2x), 8)
        l0[...] = low_f[...].astype(BF16)
        for c in low:
            c.start()

    for t in range(WAVES // 128):
        up = [pltpu.roll(blocks[l][t], 4, axis=0) for l in range(CYCLES)]
        own = [blocks[l][t] for l in range(CYCLES)]
        top = sublanes(8) < 4
        for p in range(2):
            pair = [
                jnp.where(top, own[l], up[l + 1]) if p == 0 else jnp.where(top, up[l], own[l + 1])
                for l in (0, 2)
            ]
            at = p * WAVES + t * 128
            gath[b, :, at : at + 128] = jnp.concatenate(pair, axis=0).astype(BF16)

    gathers = []

    def give(o, device):
        c = rcopy(gath.at[o], gath.at[o], g_send.at[len(gathers)], g_recv.at[o], {"ba": device})
        c.start()
        gathers.append(c)

    def arrived(o):
        rcopy(gath.at[o], gath.at[o], g_send.at[0], g_recv.at[o], {"ba": o}).wait_recv()

    x_peers = [lax.rem(x + d, N_X) * N_Z + z for d in (1, 3, 2)]
    for d in range(1, N_Z):
        give(b, x * N_Z + lax.rem(z + d, N_Z))
    for t in x_peers:
        give(b, t)

    def upwind(buf, r, j, w):
        c = lambda i: cst_ref[s, i : i + 1, j : j + w]
        here = buf[r + 1, 8 : 8 + COLS, j : j + w]
        ux = jnp.where(c(SE) > 0.0, buf[r + 1, 7 : 7 + COLS, j : j + w], buf[r + 1, 9 : 9 + COLS, j : j + w])
        uy = jnp.where(c(SN) > 0.0, buf[r, 8 : 8 + COLS, j : j + w], buf[r + 2, 8 : 8 + COLS, j : j + w])
        return here * c(CC) + ux * c(AE) + uy * c(AN)

    halo_land(halo_a, buf_a, 0)

    def second(r, carry):
        m = mask_b[pl.ds(r * COLS, COLS), :]
        for j, w in TILES:
            v = upwind(buf_a, r, j, w) * m[:, :w]
            buf_b[r + 1, 8 : 8 + COLS, j : j + w] = v
            edge[1, 0, r, :, j : j + w] = v[0:1, :]
            edge[1, 1, r, :, j : j + w] = v[COLS - 1 : COLS, :]
        return carry

    lax.fori_loop(0, ROWS, second, 0)
    halo_b = halo(buf_b, 1)
    halo_start(halo_b)

    for d in range(1, N_Z):
        o = x * N_Z + lax.rem(z + N_Z - d, N_Z)
        arrived(o)
        for t in x_peers:
            give(o, t)

    halo_land(halo_b, buf_b, 1)

    def third(r, carry):
        at = pl.ds(r * COLS, COLS)
        m = mask_b[at, :]
        total = jnp.zeros((COLS, 128), F32)
        for j, w in TILES:
            v = upwind(buf_b, r, j, w) * m[:, :w]
            d2[r, :, j : j + w] = v
            term = v * cst_ref[s, WB : WB + 1, j : j + w]
            if w == 128:
                total = total + term
            else:
                part[0, at, :] = total
                part[0, at, :w] = total[:, :w] + term
        return carry

    lax.fori_loop(0, ROWS, third, 0)
    energy_copy = rcopy(part.at[0], part_in, c_send.at[0], c_recv.at[0], partner)
    energy_copy.start()

    @pl.when(b > 0)
    def _():
        low[0].wait_recv()

    own, other = [], []
    for l in range(CYCLES):
        pc = dot(l0[...], ptable[l, 0:WAVES, :])
        ps = dot(l0[...], ptable[l, WAVES:, :])
        own.append((pc[l : l + 1, :] + ps[4 + l : 5 + l, :]).astype(BF16).astype(F32))
        other.append((pc[8 + l : 9 + l, :] + ps[12 + l : 13 + l, :]).astype(BF16).astype(F32))
    east = [jnp.where(s == 0, p, q) for p, q in zip(own, other)]
    north = [jnp.where(s == 0, q, p) for p, q in zip(own, other)]
    for l in range(CYCLES):
        east_b[pl.ds(l * POINTS, POINTS), :] = spread(east[l], POINTS)
        north_b[pl.ds(l * POINTS, POINTS), :] = spread(north[l], POINTS)

    def gain_of(e, n, r, j, w):
        c = lambda i: cst_ref[s, i : i + 1, j : j + w]
        align = e[:, :w] * c(QE) + n[:, :w] * c(QN)
        grown = 0.05 * jnp.maximum(align - 1.0, 0.0) * d2[r, :, j : j + w]
        return align, grown

    def fourth(r, carry):
        at = pl.ds(r * COLS, COLS)
        e, n = east_b[at, :], north_b[at, :]
        total = jnp.zeros((COLS, 128), F32)
        for j, w in TILES:
            align, grown = gain_of(e, n, r, j, w)
            term = grown * align * cst_ref[s, WB : WB + 1, j : j + w]
            if w == 128:
                total = total + term
            else:
                part[1, at, :] = total
                part[1, at, :w] = total[:, :w] + term
        return carry

    lax.fori_loop(0, ROWS, fourth, 0)
    for l in range(CYCLES):
        total = jnp.sum(part[1, pl.ds(l * POINTS, POINTS), :], axis=1, keepdims=True)
        kept = jnp.where(sublanes(POINTS) == lanes(POINTS), jnp.broadcast_to(total, (POINTS, 128)), 0.0)
        row = jnp.sum(kept, axis=0, keepdims=True)
        st[l : l + 1, :] = row
        st[4 + l : 5 + l, :] = row
    stress_copy = rcopy(st, st_in, c_send.at[1], c_recv.at[1], partner)
    stress_copy.start()

    energy_copy.wait_recv()
    for l in range(CYCLES):
        at = pl.ds(l * POINTS, POINTS)
        level = jnp.sum(part[0, at, :] + part_in[at, :], axis=1, keepdims=True) * 0.125
        mask_b[at, :] = jnp.broadcast_to(level * level, (POINTS, 128))

    def fifth(r, carry):
        at = pl.ds(r * COLS, COLS)
        e, n = east_b[at, :], north_b[at, :]
        square = mask_b[at, :]
        for j, w in TILES:
            _, grown = gain_of(e, n, r, j, w)
            decay = square[:, :w] * cst_ref[s, DF : DF + 1, j : j + w]
            ws_ref[r, :, j : j + w] = (d2[r, :, j : j + w] + grown) / (1.0 + decay)
        return carry

    lax.fori_loop(0, ROWS, fifth, 0)

    stress_copy.wait_recv()
    e, n = jnp.concatenate(east * 2, axis=0), jnp.concatenate(north * 2, axis=0)
    air = 0.12 * (e * e + n * n) + 0.02
    rough[b] = jnp.sqrt(1.0 + 0.03 * (st[...] + st_in[...]) / air)
    rough_copies = []
    for d in range(1, N_B):
        t = lax.rem(b + d, N_B)
        c = rcopy(rough.at[b], rough.at[b], r_send.at[d - 1], r_recv.at[b], {"ba": t})
        c.start()
        rough_copies.append(c)

    slots = lanes(1, SLOTS) + b * SLOTS
    for l in range(CYCLES):
        active = jnp.where(slots < cp_ref[a * CYCLES + l], 2.0, 0.0)
        tables(table, l, slots.astype(F32), active)
    for xd in range(1, N_X):
        for zd in range(N_Z):
            arrived(lax.rem(x + N_X - xd, N_X) * N_Z + lax.rem(z + zd, N_Z))
    r = sublanes(256, 256)
    order = one_hot(lanes(256, 256) == (r & 63) // 4 * 16 + r // 64 * 4 + (r & 3))
    for k in range(0, 2 * WAVES, 256):
        gperm[:, k : k + 256] = dot(order, gath[:, :, k : k + 256].reshape(256, 256)).astype(BF16)
    for l in range(CYCLES):
        gw_ref[0, l] = dot(gperm[l * 64 : l * 64 + 64, :], table[l]).astype(BF16)

    for d in range(1, N_B):
        o = lax.rem(b + N_B - d, N_B)
        rcopy(rough.at[o], rough.at[o], r_send.at[0], r_recv.at[o], {"ba": o}).wait_recv()
    for c in sent + gathers + rough_copies + [energy_copy, stress_copy]:
        c.wait_send()
    halo_sent(halo_a)
    halo_sent(halo_b)

    @pl.when(b == 0)
    def _():
        for c in low + crossed:
            c.wait_send()


def last(cp_ref, gw_in, ws_in, rough, rs_ref, gw_ref, ws_ref, ch_ref, sem):
    a = lax.axis_index("aa")
    slots = lanes(1, SLOTS) + lax.axis_index("ba") * SLOTS
    copies = [
        pltpu.make_async_copy(ws_in, ws_ref, sem.at[0]),
        pltpu.make_async_copy(gw_in, gw_ref, sem.at[1]),
    ]
    for c in copies:
        c.start()
    for l in range(CYCLES):
        source = rs_ref[l : l + 1, :]
        low_part = ((source >> 9) & 3) * 32 + (source & 31)
        high_part = (source >> 5) & 15
        pick = one_hot(sublanes(128, SLOTS) == low_part)
        values = rough[:, l, :]
        h0 = values.astype(BF16)
        r1 = values - h0.astype(F32)
        h1 = r1.astype(BF16)
        h2 = (r1 - h1.astype(F32)).astype(BF16)
        got = dot(h0, pick) + (dot(h1, pick) + dot(h2, pick))
        keep = sublanes(N_B, SLOTS) == high_part
        row = jnp.sum(jnp.where(keep, got, 0.0), axis=0, keepdims=True)
        ch_ref[l : l + 1, :] = jnp.where(slots < cp_ref[a * CYCLES + l], row, 0.0)
    for c in copies:
        c.wait()


def per_device(legendre, coefficients, cycle_points, spectra, sea_mask, wind_column, roughness_source):
    vmem = pl.BlockSpec(memory_space=pltpu.VMEM)
    smem = pl.BlockSpec(memory_space=pltpu.SMEM)
    hbm = pl.BlockSpec(memory_space=pl.ANY)
    dma = pltpu.SemaphoreType.DMA
    winds = jax.ShapeDtypeStruct((1, CYCLES, 64, SLOTS), BF16)
    waves = jax.ShapeDtypeStruct((ROWS, COLS, HALF), F32)
    winds_done, waves_done, rough = pl.pallas_call(
        kernel,
        out_shape=(winds, waves, jax.ShapeDtypeStruct((N_B, 8, 128), F32)),
        in_specs=[smem] + [hbm] * 6,
        out_specs=(vmem, vmem, vmem),
        scratch_shapes=[
            pltpu.VMEM((BLOCK, 32, NT), BF16),
            pltpu.VMEM((BLOCK, 2, 4, NT), BF16),
            pltpu.VMEM((ROWS, COLS, HALF), F32),
            pltpu.VMEM((ROWS, COLS), jnp.int32),
            pltpu.VMEM((ROWS, 512), jnp.int32),
            pltpu.VMEM((2, 16, HALF), F32),
            pltpu.VMEM((BLOCK, 256), F32),
            pltpu.VMEM((N_A, 8, 384), F32),
            pltpu.VMEM((N_A, 8, 384), F32),
            pltpu.VMEM((N_A, 8, 384), F32),
            pltpu.VMEM((N_B, 16, 2 * WAVES), BF16),
            pltpu.VMEM((256, 2 * WAVES), BF16),
            pltpu.VMEM((16, WAVES), F32),
            pltpu.VMEM((16, WAVES), BF16),
            pltpu.VMEM((CYCLES, 2 * WAVES, SLOTS), BF16),
            pltpu.VMEM((CYCLES, 2 * WAVES, POINTS), BF16),
            pltpu.VMEM((GROUPS, 8, SLOTS), F32),
            pltpu.VMEM((GROUPS, 8, SLOTS), F32),
            pltpu.VMEM((ROWS + 2, COLS + 16, HALF), F32),
            pltpu.VMEM((ROWS + 2, COLS + 16, HALF), F32),
            pltpu.VMEM((ROWS, COLS, HALF), F32),
            pltpu.VMEM((2, 2, ROWS, 1, HALF), F32),
            pltpu.VMEM((2, 2, ROWS, 1, HALF), F32),
            pltpu.VMEM((ROWS * COLS, 128), F32),
            pltpu.VMEM((ROWS * COLS, 128), F32),
            pltpu.VMEM((ROWS * COLS, 128), F32),
            pltpu.VMEM((2, ROWS * COLS, 128), F32),
            pltpu.VMEM((ROWS * COLS, 128), F32),
            pltpu.VMEM((8, 128), F32),
            pltpu.VMEM((8, 128), F32),
            dma((5,)), dma((GROUPS,)),
            dma((N_A - 1,)), dma((N_A,)),
            dma((N_A,)), dma((N_A,)),
            dma((N_B - 1,)), dma((N_B,)),
            dma((N_B - 1,)), dma((1,)),
            dma((2, 4)), dma((2, 4)),
            dma((2,)), dma((2,)),
            dma((N_B - 1,)), dma((N_B,)),
        ],
        compiler_params=pltpu.CompilerParams(
            collective_id=0, has_side_effects=True, vmem_limit_bytes=50 * 1024 * 1024
        ),
    )(
        cycle_points, legendre, coefficients.reshape(BLOCK, 2, 4, NT), spectra, sea_mask, wind_column,
        jnp.asarray(bin_table()),
    )
    return pl.pallas_call(
        last,
        out_shape=(winds, waves, jax.ShapeDtypeStruct((CYCLES, SLOTS), F32)),
        in_specs=[smem, vmem, vmem, vmem, vmem],
        out_specs=(hbm, hbm, vmem),
        scratch_shapes=[dma((2,))],
    )(cycle_points, winds_done, waves_done, rough, roughness_source)


def solution(mesh):
    in_specs = (
        P("aa", None, None),
        P("comp", "aa", None, "ba", None),
        P(),
        P("aa", "ba", "comp"),
        P("aa", "ba"),
        P("aa", None),
        P("aa", "ba"),
    )
    out_specs = (P("comp", "aa", None, "ba"), P("aa", "ba", "comp"), P("aa", "ba"))
    return jax.shard_map(
        per_device, mesh=mesh, in_specs=in_specs, out_specs=out_specs, check_vma=False
    )
```

```python
import math

import numpy as np

import jax
import jax.numpy as jnp
from jax import lax
from jax.experimental import pallas as pl
from jax.experimental.pallas import tpu as pltpu
from jax.sharding import PartitionSpec as P

LON = 4096
NDIR = 36
NFREQ = 36
F32 = jnp.float32
BF16 = jnp.bfloat16
MESH = pl.DeviceIdType.MESH

N_A = 8
N_B = 16
N_X = 4
N_Z = 4
WAVES = 640
BLOCK = WAVES // N_A
GROUPS = BLOCK // 8
NT = 1280
CYCLES = 4
SLOTS = LON // N_B
ROWS = 16
COLS = 32
VMEM = 64_000_000
HALF = NDIR * NFREQ // 2
POINTS = 128
TILES = [(j, min(128, HALF - j)) for j in range(0, HALF, 128)]


def bin_table():
    b = np.arange(NDIR * NFREQ)
    theta = 2 * np.pi * (b // NFREQ + 0.5) / NDIR
    ratio = np.exp(-math.log(1.1) * (b % NFREQ))
    freq = 0.04177 / ratio
    east = 0.45 * ratio * np.cos(theta)
    north = 0.45 * ratio * np.sin(theta)
    q = 2 * np.pi * freq / 9.81
    width = 0.1 * freq * (2 * np.pi / NDIR)
    rows = [
        np.abs(east),
        np.abs(north),
        1.0 - np.abs(east) - np.abs(north),
        np.sign(east),
        np.sign(north),
        10.0 * q * np.cos(theta),
        10.0 * q * np.sin(theta),
        width,
        0.5 * freq / 0.2,
    ]
    rows += [np.zeros_like(freq)] * (16 - len(rows))
    table = np.stack(rows).astype(np.float32)
    return np.stack([table[:, :HALF], table[:, HALF:]])


AE, AN, CC, SE, SN, QE, QN, WB, DF = range(9)


def poly(y2, coefs):
    acc = jnp.full_like(y2, coefs[-1])
    for c in coefs[-2::-1]:
        acc = acc * y2 + c
    return acc


SIN_C = [(-1.0) ** i / math.factorial(2 * i + 1) for i in range(7)]
COS_C = [(-1.0) ** i / math.factorial(2 * i) for i in range(7)]


def turn(mk, count, inv):
    rest = mk - jnp.floor(mk * inv + 0.5) * count
    y = (rest * inv) * math.pi
    y2 = y * y
    s = y * poly(y2, SIN_C)
    c = poly(y2, COS_C)
    return 1.0 - 2.0 * s * s, 2.0 * s * c


def rcopy(src, dst, send, recv, device):
    return pltpu.make_async_remote_copy(
        src_ref=src, dst_ref=dst, send_sem=send, recv_sem=recv, device_id=device, device_id_type=MESH
    )


def lanes(rows, width=128):
    return lax.broadcasted_iota(jnp.int32, (rows, width), 1)


def sublanes(rows, width=128):
    return lax.broadcasted_iota(jnp.int32, (rows, width), 0)


def spread(row, n):
    kept = jnp.where(sublanes(n, n) == lanes(n, n), jnp.broadcast_to(row, (n, n)), 0.0)
    return jnp.broadcast_to(jnp.sum(kept, axis=1, keepdims=True), (n, 128))


def one_hot(mask):
    return mask.astype(F32).astype(BF16)


def dot(x, y, dims=((1,), (0,))):
    return lax.dot_general(x, y, (dims, ((), ())), preferred_element_type=F32)


def kernel(
    cp_hbm, leg_hbm, coef_hbm, spec_hbm, mask_hbm, wc_hbm, cst_hbm,
    gw_out, ws_out, rough_out,
    gw_ref, ws_ref, rough, cp_ref, leg, coef, spec, mask_in, wc, cst_ref, sall, msg, a2a, a2x, gath, gperm, low_f, l0,
    table, ptable, ca, sa, buf_a, buf_b, d2, edge, edge_in,
    mask_b, east_b, north_b, part, part_in, st, st_in,
    i_sem, leg_sem, a_send, a_recv, x_send, x_recv, g_send, g_recv, l_send, l_recv, h_send, h_recv,
    c_send, c_recv, r_send, r_recv, o_sem,
):
    s = lax.axis_index("comp")
    a = lax.axis_index("aa")
    b = lax.axis_index("ba")
    x, z = b // N_Z, b % N_Z
    partner = {"comp": 1 - s}

    coef_copy = pltpu.make_async_copy(coef_hbm, coef, i_sem.at[0])
    coef_copy.start()
    leg_copies = lambda g: pltpu.make_async_copy(
        leg_hbm.at[pl.ds(g * 8, 8)], leg.at[pl.ds(g * 8, 8)], leg_sem.at[g]
    )
    for g in range(GROUPS):
        leg_copies(g).start()
    small = [
        pltpu.make_async_copy(mask_hbm, mask_in, i_sem.at[1]),
        pltpu.make_async_copy(wc_hbm, wc, i_sem.at[2]),
        pltpu.make_async_copy(cst_hbm, cst_ref, i_sem.at[3]),
        pltpu.make_async_copy(spec_hbm, spec, i_sem.at[4]),
        pltpu.make_async_copy(cp_hbm, cp_ref, i_sem.at[5]),
    ]
    for c in small:
        c.start()

    barrier = pltpu.get_barrier_semaphore()
    pl.semaphore_signal(barrier, inc=1, device_id=partner, device_id_type=MESH)
    for d in range(1, N_A):
        pl.semaphore_signal(barrier, inc=1, device_id={"aa": lax.rem(a + d, N_A)}, device_id_type=MESH)
    for d in range(1, N_B):
        pl.semaphore_signal(barrier, inc=1, device_id={"ba": lax.rem(b + d, N_B)}, device_id_type=MESH)

    @pl.when(b == 0)
    def _():
        for d in range(1, N_A):
            pl.semaphore_signal(
                barrier, inc=1, device_id={"comp": 1 - s, "aa": lax.rem(a + d, N_A)}, device_id_type=MESH
            )

    coef_copy.wait()

    def legendre(g, carry):
        rows = []
        for i in range(8):
            order = a * BLOCK + g * 8 + i
            block = jnp.concatenate([coef[g * 8 + i, p].astype(F32) for p in range(2)], axis=0)
            rows.append(jnp.where(lanes(8, NT) >= order, block, 0.0))
        rows = jnp.concatenate(rows, axis=0).astype(BF16)
        leg_copies(g).wait()
        cross = dot(rows, leg[pl.ds(g * 8, 8)].reshape(256, NT), ((1,), (1,)))
        at = pl.ds(pl.multiple_of(g * 8, 8), 8)
        for t in range(2):
            kept = cross[t * 32 : t * 32 + 8, t * 128 : t * 128 + 128]
            for q in range(1, 4):
                m = t * 4 + q
                kept = jnp.where(lanes(8) >= q * 32, cross[m * 8 : m * 8 + 8, t * 128 : t * 128 + 128], kept)
            sall[at, t * 128 : t * 128 + 128] = kept
        return carry

    lax.fori_loop(0, GROUPS, legendre, 0)

    i, o = sublanes(256, 256), lanes(256, 256)
    moved = dot(sall[...].astype(BF16), one_hot(o == (i & 31) // 4 * 32 + (i // 32) * 4 + (i & 3)))
    turned = {}
    for t in range(N_A):
        for q in range(3):
            acc = jnp.zeros((8, 128), F32)
            for g in range(q * 4, min(q * 4 + 4, GROUPS)):
                shift = 32 * ((g - t) % 4)
                key = (g, t // 4, shift)
                if key not in turned:
                    v = moved[g * 8 : g * 8 + 8, t // 4 * 128 : t // 4 * 128 + 128]
                    turned[key] = pltpu.roll(v, shift, axis=1) if shift else v
                at = lanes(8) // 32 == g % 4
                acc = jnp.where(at, turned[key], acc)
            msg[t, :, q * 128 : q * 128 + 128] = acc

    pl.semaphore_wait(barrier, N_A + N_B - 1 + jnp.where(b == 0, N_A - 1, 0))

    sent = []
    for d in range(1, N_A):
        t = lax.rem(a + d, N_A)
        c = rcopy(msg.at[t], a2a.at[a], a_send.at[d - 1], a_recv.at[a], {"aa": t})
        c.start()
        sent.append(c)
    crossed = []
    for d in range(N_A):
        t = lax.rem(a + d, N_A)
        crossed.append(
            rcopy(msg.at[t], a2x.at[a], x_send.at[d], x_recv.at[a], {"comp": 1 - s, "aa": t})
        )

    @pl.when(b == 0)
    def _():
        for c in crossed:
            c.start()

    a2a[a] = msg[a]

    for c in small:
        c.wait()
    sea = mask_in[...].astype(F32)
    for r in range(ROWS):
        mask_b[r * COLS : (r + 1) * COLS, :] = spread(sea[r : r + 1, :], COLS)

    def first(r, carry):
        m = mask_b[pl.ds(r * COLS, COLS), :]
        for j, w in TILES:
            v = spec[r, :, j : j + w] * m[:, :w]
            buf_a[r + 1, 8 : 8 + COLS, j : j + w] = v
            edge[0, 0, r, :, j : j + w] = v[0:1, :]
            edge[0, 1, r, :, j : j + w] = v[COLS - 1 : COLS, :]
        return carry

    lax.fori_loop(0, ROWS, first, 0)

    def halo(buf, step):
        return [
            (a < N_A - 1, a > 0, rcopy(
                buf.at[ROWS, pl.ds(8, COLS)], buf.at[0, pl.ds(8, COLS)],
                h_send.at[step, 0], h_recv.at[step, 0], {"aa": lax.rem(a + 1, N_A)})),
            (a > 0, a < N_A - 1, rcopy(
                buf.at[1, pl.ds(8, COLS)], buf.at[ROWS + 1, pl.ds(8, COLS)],
                h_send.at[step, 1], h_recv.at[step, 1], {"aa": lax.rem(a + N_A - 1, N_A)})),
            (b < N_B - 1, b > 0, rcopy(
                edge.at[step, 1], edge_in.at[step, 0],
                h_send.at[step, 2], h_recv.at[step, 2], {"ba": lax.rem(b + 1, N_B)})),
            (b > 0, b < N_B - 1, rcopy(
                edge.at[step, 0], edge_in.at[step, 1],
                h_send.at[step, 3], h_recv.at[step, 3], {"ba": lax.rem(b + N_B - 1, N_B)})),
        ]

    def halo_start(copies):
        for can, _, c in copies:
            pl.when(can)(c.start)

    def halo_land(copies, buf, step):
        for i, (_, comes, c) in enumerate(copies):
            pl.when(comes)(c.wait_recv)

            @pl.when(jnp.logical_not(comes))
            def _():
                if i < 2:
                    buf[0 if i == 0 else ROWS + 1, 8 : 8 + COLS, :] = jnp.zeros((COLS, HALF), F32)
                else:
                    edge_in[step, i - 2] = jnp.zeros((ROWS, 1, HALF), F32)

        for r in range(ROWS):
            buf[r + 1, 7:8, :] = edge_in[step, 0, r]
            buf[r + 1, 8 + COLS : 9 + COLS, :] = edge_in[step, 1, r]

    def halo_sent(copies):
        for can, _, c in copies:
            pl.when(can)(c.wait_send)

    halo_a = halo(buf_a, 0)
    halo_start(halo_a)

    def tables(out, l, k, active):
        w = k.shape[1]
        count = jnp.full((1, w), cp_ref[a * CYCLES + l], jnp.int32).astype(F32)
        inv = 1.0 / count
        cu, su = turn(sublanes(WAVES // 8, w).astype(F32) * 8.0 * k, count, inv)
        ca[:, :, :w] = cu.reshape(GROUPS, 8, w)
        sa[:, :, :w] = su.reshape(GROUPS, 8, w)
        cv, sv = turn(sublanes(8, w).astype(F32) * k, count, inv)
        cv, sv = cv * active, sv * active
        minus_c, minus_s = -cv, -sv

        def block(i, carry):
            for h in range(4):
                cs, ss = [], []
                for o in range(h * 2, h * 2 + 2):
                    c0, s0 = ca[i, o : o + 1, :w], sa[i, o : o + 1, :w]
                    cs.append(c0 * cv + s0 * minus_s)
                    ss.append(s0 * minus_c + c0 * minus_s)
                at = pl.multiple_of(i * 64 + h * 16, 16)
                out[l, pl.ds(at, 16), :] = jnp.concatenate(cs, axis=0).astype(BF16)
                out[l, pl.ds(WAVES + at, 16), :] = jnp.concatenate(ss, axis=0).astype(BF16)
            return carry

        lax.fori_loop(0, GROUPS, block, 0)
        top = out[l, 0:16, :].astype(F32)
        out[l, 0:16, :] = jnp.where(sublanes(16, w) == 0, top * 0.5, top).astype(BF16)

    near = wc[:, pl.ds(pl.multiple_of(b // 4 * 128, 128), 128)].astype(F32)
    near = pltpu.roll(near, (4 - b % 4) % 4 * COLS, axis=1)
    near = jnp.where(lanes(ROWS) < COLS, near, 0.0)
    side = near
    for q in range(1, 4):
        side = jnp.where(sublanes(ROWS) % 4 == q, pltpu.roll(near, q * COLS, axis=1), side)
    for l in range(CYCLES):
        tables(ptable, l, jnp.sum(side[l * 4 : l * 4 + 4, :], axis=0, keepdims=True), 2.0)

    i, o = sublanes(384, 512), lanes(384, 512)
    order = one_hot((o == (i & 3) * 128 + i // 4) & (i < BLOCK * 4))

    def compact(landed):
        wide = dot(landed[...].reshape(64, 384).astype(BF16), order)
        out = []
        for l in range(CYCLES):
            tiles = [jnp.zeros((8, 128), F32) for _ in range(WAVES // 128)]
            for c in range(N_A):
                t, shift = divmod(c * BLOCK, 128)
                piece = wide[c * 8 : c * 8 + 8, l * 128 : l * 128 + 128]
                if shift:
                    piece = pltpu.roll(piece, shift, axis=1)
                    tiles[t] = jnp.where(lanes(8) >= shift, piece, tiles[t])
                    if shift + BLOCK > 128:
                        tiles[t + 1] = jnp.where(lanes(8) < shift, piece, tiles[t + 1])
                else:
                    tiles[t] = jnp.where(lanes(8) < BLOCK, piece, tiles[t])
            out.append(tiles)
        return out

    def lowest(blocks, base):
        for l in range(CYCLES):
            for t in range(WAVES // 128):
                for p in range(2):
                    r = base + p * 4 + l
                    low_f[r : r + 1, t * 128 : t * 128 + 128] = blocks[l][t][p * 4 : p * 4 + 1, :]

    for d in range(1, N_A):
        c = lax.rem(a + N_A - d, N_A)
        rcopy(msg.at[0], a2a.at[c], a_send.at[d - 1], a_recv.at[c], {"aa": c}).wait_recv()
    blocks = compact(a2a)
    low = [
        rcopy(l0, l0, l_send.at[d - 1], l_recv.at[0], {"ba": lax.rem(b + d, N_B)}) for d in range(1, N_B)
    ]

    @pl.when(b == 0)
    def _():
        lowest(blocks, 0)
        for d in range(N_A):
            c = lax.rem(a + N_A - d, N_A)
            rcopy(msg.at[0], a2x.at[c], x_send.at[d], x_recv.at[c], {"comp": 1 - s, "aa": c}).wait_recv()
        lowest(compact(a2x), 8)
        l0[...] = low_f[...].astype(BF16)
        for c in low:
            c.start()

    for t in range(WAVES // 128):
        up = [pltpu.roll(blocks[l][t], 4, axis=0) for l in range(CYCLES)]
        own = [blocks[l][t] for l in range(CYCLES)]
        top = sublanes(8) < 4
        for p in range(2):
            pair = [
                jnp.where(top, own[l], up[l + 1]) if p == 0 else jnp.where(top, up[l], own[l + 1])
                for l in (0, 2)
            ]
            at = p * WAVES + t * 128
            gath[b, :, at : at + 128] = jnp.concatenate(pair, axis=0).astype(BF16)

    gathers = []

    def give(o, device):
        c = rcopy(gath.at[o], gath.at[o], g_send.at[len(gathers)], g_recv.at[o], {"ba": device})
        c.start()
        gathers.append(c)

    def arrived(o):
        rcopy(gath.at[o], gath.at[o], g_send.at[0], g_recv.at[o], {"ba": o}).wait_recv()

    x_peers = [lax.rem(x + d, N_X) * N_Z + z for d in (1, 3, 2)]
    for d in range(1, N_Z):
        give(b, x * N_Z + lax.rem(z + d, N_Z))
    for t in x_peers:
        give(b, t)

    def upwind(buf, r, j, w):
        c = lambda i: cst_ref[s, i : i + 1, j : j + w]
        here = buf[r + 1, 8 : 8 + COLS, j : j + w]
        ux = jnp.where(c(SE) > 0.0, buf[r + 1, 7 : 7 + COLS, j : j + w], buf[r + 1, 9 : 9 + COLS, j : j + w])
        uy = jnp.where(c(SN) > 0.0, buf[r, 8 : 8 + COLS, j : j + w], buf[r + 2, 8 : 8 + COLS, j : j + w])
        return here * c(CC) + ux * c(AE) + uy * c(AN)

    halo_land(halo_a, buf_a, 0)

    def second(r, carry):
        m = mask_b[pl.ds(r * COLS, COLS), :]
        for j, w in TILES:
            v = upwind(buf_a, r, j, w) * m[:, :w]
            buf_b[r + 1, 8 : 8 + COLS, j : j + w] = v
            edge[1, 0, r, :, j : j + w] = v[0:1, :]
            edge[1, 1, r, :, j : j + w] = v[COLS - 1 : COLS, :]
        return carry

    lax.fori_loop(0, ROWS, second, 0)
    halo_b = halo(buf_b, 1)
    halo_start(halo_b)

    for d in range(1, N_Z):
        o = x * N_Z + lax.rem(z + N_Z - d, N_Z)
        arrived(o)
        for t in x_peers:
            give(o, t)

    halo_land(halo_b, buf_b, 1)

    def third(r, carry):
        at = pl.ds(r * COLS, COLS)
        m = mask_b[at, :]
        total = jnp.zeros((COLS, 128), F32)
        for j, w in TILES:
            v = upwind(buf_b, r, j, w) * m[:, :w]
            d2[r, :, j : j + w] = v
            term = v * cst_ref[s, WB : WB + 1, j : j + w]
            if w == 128:
                total = total + term
            else:
                part[0, at, :] = total
                part[0, at, :w] = total[:, :w] + term
        return carry

    lax.fori_loop(0, ROWS, third, 0)
    energy_copy = rcopy(part.at[0], part_in, c_send.at[0], c_recv.at[0], partner)
    energy_copy.start()

    @pl.when(b > 0)
    def _():
        low[0].wait_recv()

    own, other = [], []
    for l in range(CYCLES):
        pc = dot(l0[...], ptable[l, 0:WAVES, :])
        ps = dot(l0[...], ptable[l, WAVES:, :])
        own.append((pc[l : l + 1, :] + ps[4 + l : 5 + l, :]).astype(BF16).astype(F32))
        other.append((pc[8 + l : 9 + l, :] + ps[12 + l : 13 + l, :]).astype(BF16).astype(F32))
    east = [jnp.where(s == 0, p, q) for p, q in zip(own, other)]
    north = [jnp.where(s == 0, q, p) for p, q in zip(own, other)]
    for l in range(CYCLES):
        east_b[pl.ds(l * POINTS, POINTS), :] = spread(east[l], POINTS)
        north_b[pl.ds(l * POINTS, POINTS), :] = spread(north[l], POINTS)

    def gain_of(e, n, r, j, w):
        c = lambda i: cst_ref[s, i : i + 1, j : j + w]
        align = e[:, :w] * c(QE) + n[:, :w] * c(QN)
        grown = 0.05 * jnp.maximum(align - 1.0, 0.0) * d2[r, :, j : j + w]
        return align, grown

    def fourth(r, carry):
        at = pl.ds(r * COLS, COLS)
        e, n = east_b[at, :], north_b[at, :]
        total = jnp.zeros((COLS, 128), F32)
        for j, w in TILES:
            align, grown = gain_of(e, n, r, j, w)
            term = grown * align * cst_ref[s, WB : WB + 1, j : j + w]
            if w == 128:
                total = total + term
            else:
                part[1, at, :] = total
                part[1, at, :w] = total[:, :w] + term
        return carry

    lax.fori_loop(0, ROWS, fourth, 0)
    for l in range(CYCLES):
        total = jnp.sum(part[1, pl.ds(l * POINTS, POINTS), :], axis=1, keepdims=True)
        kept = jnp.where(sublanes(POINTS) == lanes(POINTS), jnp.broadcast_to(total, (POINTS, 128)), 0.0)
        row = jnp.sum(kept, axis=0, keepdims=True)
        st[l : l + 1, :] = row
        st[4 + l : 5 + l, :] = row
    stress_copy = rcopy(st, st_in, c_send.at[1], c_recv.at[1], partner)
    stress_copy.start()

    energy_copy.wait_recv()
    for l in range(CYCLES):
        at = pl.ds(l * POINTS, POINTS)
        level = jnp.sum(part[0, at, :] + part_in[at, :], axis=1, keepdims=True) * 0.125
        mask_b[at, :] = jnp.broadcast_to(level * level, (POINTS, 128))

    def fifth(r, carry):
        at = pl.ds(r * COLS, COLS)
        e, n = east_b[at, :], north_b[at, :]
        square = mask_b[at, :]
        for j, w in TILES:
            _, grown = gain_of(e, n, r, j, w)
            decay = square[:, :w] * cst_ref[s, DF : DF + 1, j : j + w]
            ws_ref[r, :, j : j + w] = (d2[r, :, j : j + w] + grown) / (1.0 + decay)
        return carry

    lax.fori_loop(0, ROWS, fifth, 0)
    ws_copy = pltpu.make_async_copy(ws_ref, ws_out, o_sem.at[0])
    ws_copy.start()

    stress_copy.wait_recv()
    e, n = jnp.concatenate(east * 2, axis=0), jnp.concatenate(north * 2, axis=0)
    air = 0.12 * (e * e + n * n) + 0.02
    rough[b] = jnp.sqrt(1.0 + 0.03 * (st[...] + st_in[...]) / air)
    rough_copies = []
    for d in range(1, N_B):
        t = lax.rem(b + d, N_B)
        c = rcopy(rough.at[b], rough.at[b], r_send.at[d - 1], r_recv.at[b], {"ba": t})
        c.start()
        rough_copies.append(c)

    slots = lanes(1, SLOTS) + b * SLOTS
    for l in range(CYCLES):
        active = jnp.where(slots < cp_ref[a * CYCLES + l], 2.0, 0.0)
        tables(table, l, slots.astype(F32), active)
    for xd in range(1, N_X):
        for zd in range(N_Z):
            arrived(lax.rem(x + N_X - xd, N_X) * N_Z + lax.rem(z + zd, N_Z))
    r = sublanes(256, 256)
    order = one_hot(lanes(256, 256) == (r & 63) // 4 * 16 + r // 64 * 4 + (r & 3))
    for k in range(0, 2 * WAVES, 256):
        gperm[:, k : k + 256] = dot(order, gath[:, :, k : k + 256].reshape(256, 256)).astype(BF16)
    for l in range(CYCLES):
        gw_ref[0, l] = dot(gperm[l * 64 : l * 64 + 64, :], table[l]).astype(BF16)
    gw_copy = pltpu.make_async_copy(gw_ref, gw_out, o_sem.at[1])
    gw_copy.start()

    for d in range(1, N_B):
        o = lax.rem(b + N_B - d, N_B)
        rcopy(rough.at[o], rough.at[o], r_send.at[0], r_recv.at[o], {"ba": o}).wait_recv()
    rough_copy = pltpu.make_async_copy(rough, rough_out, o_sem.at[2])
    rough_copy.start()
    for c in sent + gathers + rough_copies + [energy_copy, stress_copy]:
        c.wait_send()
    halo_sent(halo_a)
    halo_sent(halo_b)

    @pl.when(b == 0)
    def _():
        for c in low + crossed:
            c.wait_send()

    for c in (ws_copy, gw_copy, rough_copy):
        c.wait()


def last(cp_hbm, gw_in, ws_in, rough, rs_ref, gw_ref, ws_ref, ch_ref, cp_ref, gw, ws, sem_in, sem_out):
    a = lax.axis_index("aa")
    slots = lanes(1, SLOTS) + lax.axis_index("ba") * SLOTS
    step = ROWS // 4
    blocks = [pl.ds(i * step, step) for i in range(4)]
    counts = pltpu.make_async_copy(cp_hbm, cp_ref, sem_in.at[5])
    come = [pltpu.make_async_copy(ws_in.at[k], ws.at[k], sem_in.at[i]) for i, k in enumerate(blocks)]
    come.append(pltpu.make_async_copy(gw_in, gw, sem_in.at[4]))
    go = [pltpu.make_async_copy(ws.at[k], ws_ref.at[k], sem_out.at[i]) for i, k in enumerate(blocks)]
    go.append(pltpu.make_async_copy(gw, gw_ref, sem_out.at[4]))
    counts.start()
    for c in come:
        c.start()
    for c, d in zip(come, go):
        c.wait()
        d.start()
    counts.wait()
    for l in range(CYCLES):
        source = rs_ref[l : l + 1, :]
        low_part = ((source >> 9) & 3) * 32 + (source & 31)
        high_part = (source >> 5) & 15
        pick = one_hot(sublanes(128, SLOTS) == low_part)
        values = rough[:, l, :]
        h0 = values.astype(BF16)
        r1 = values - h0.astype(F32)
        h1 = r1.astype(BF16)
        h2 = (r1 - h1.astype(F32)).astype(BF16)
        got = dot(h0, pick) + (dot(h1, pick) + dot(h2, pick))
        keep = sublanes(N_B, SLOTS) == high_part
        row = jnp.sum(jnp.where(keep, got, 0.0), axis=0, keepdims=True)
        ch_ref[l : l + 1, :] = jnp.where(slots < cp_ref[a * CYCLES + l], row, 0.0)
    for c in go:
        c.wait()


def per_device(legendre, coefficients, cycle_points, spectra, sea_mask, wind_column, roughness_source):
    vmem = pl.BlockSpec(memory_space=pltpu.VMEM)
    smem = pl.BlockSpec(memory_space=pltpu.SMEM)
    hbm = pl.BlockSpec(memory_space=pltpu.HBM)
    dma = pltpu.SemaphoreType.DMA
    winds = jax.ShapeDtypeStruct((1, CYCLES, 64, SLOTS), BF16)
    waves = jax.ShapeDtypeStruct((ROWS, COLS, HALF), F32)
    winds_done, waves_done, rough = pl.pallas_call(
        kernel,
        out_shape=(winds, waves, jax.ShapeDtypeStruct((N_B, 8, 128), F32)),
        in_specs=[hbm] * 7,
        out_specs=(hbm, hbm, hbm),
        scratch_shapes=[
            pltpu.VMEM((1, CYCLES, 64, SLOTS), BF16),
            pltpu.VMEM((ROWS, COLS, HALF), F32),
            pltpu.VMEM((N_B, 8, 128), F32),
            pltpu.SMEM((32,), jnp.int32),
            pltpu.VMEM((BLOCK, 32, NT), BF16),
            pltpu.VMEM((BLOCK, 2, 4, NT), BF16),
            pltpu.VMEM((ROWS, COLS, HALF), F32),
            pltpu.VMEM((ROWS, COLS), jnp.int32),
            pltpu.VMEM((ROWS, 512), jnp.int32),
            pltpu.VMEM((2, 16, HALF), F32),
            pltpu.VMEM((BLOCK, 256), F32),
            pltpu.VMEM((N_A, 8, 384), F32),
            pltpu.VMEM((N_A, 8, 384), F32),
            pltpu.VMEM((N_A, 8, 384), F32),
            pltpu.VMEM((N_B, 16, 2 * WAVES), BF16),
            pltpu.VMEM((256, 2 * WAVES), BF16),
            pltpu.VMEM((16, WAVES), F32),
            pltpu.VMEM((16, WAVES), BF16),
            pltpu.VMEM((CYCLES, 2 * WAVES, SLOTS), BF16),
            pltpu.VMEM((CYCLES, 2 * WAVES, POINTS), BF16),
            pltpu.VMEM((GROUPS, 8, SLOTS), F32),
            pltpu.VMEM((GROUPS, 8, SLOTS), F32),
            pltpu.VMEM((ROWS + 2, COLS + 16, HALF), F32),
            pltpu.VMEM((ROWS + 2, COLS + 16, HALF), F32),
            pltpu.VMEM((ROWS, COLS, HALF), F32),
            pltpu.VMEM((2, 2, ROWS, 1, HALF), F32),
            pltpu.VMEM((2, 2, ROWS, 1, HALF), F32),
            pltpu.VMEM((ROWS * COLS, 128), F32),
            pltpu.VMEM((ROWS * COLS, 128), F32),
            pltpu.VMEM((ROWS * COLS, 128), F32),
            pltpu.VMEM((2, ROWS * COLS, 128), F32),
            pltpu.VMEM((ROWS * COLS, 128), F32),
            pltpu.VMEM((8, 128), F32),
            pltpu.VMEM((8, 128), F32),
            dma((6,)), dma((GROUPS,)),
            dma((N_A - 1,)), dma((N_A,)),
            dma((N_A,)), dma((N_A,)),
            dma((N_B - 1,)), dma((N_B,)),
            dma((N_B - 1,)), dma((1,)),
            dma((2, 4)), dma((2, 4)),
            dma((2,)), dma((2,)),
            dma((N_B - 1,)), dma((N_B,)),
            dma((3,)),
        ],
        compiler_params=pltpu.CompilerParams(
            collective_id=0, has_side_effects=True, vmem_limit_bytes=VMEM
        ),
    )(
        cycle_points, legendre, coefficients.reshape(BLOCK, 2, 4, NT), spectra, sea_mask, wind_column,
        jnp.asarray(bin_table()),
    )
    return pl.pallas_call(
        last,
        out_shape=(winds, waves, jax.ShapeDtypeStruct((CYCLES, SLOTS), F32)),
        in_specs=[hbm, hbm, hbm, vmem, vmem],
        out_specs=(hbm, hbm, vmem),
        scratch_shapes=[
            pltpu.SMEM((32,), jnp.int32),
            pltpu.VMEM((1, CYCLES, 64, SLOTS), BF16),
            pltpu.VMEM((ROWS, COLS, HALF), F32),
            dma((6,)), dma((5,)),
        ],
        compiler_params=pltpu.CompilerParams(vmem_limit_bytes=VMEM),
    )(cycle_points, winds_done, waves_done, rough, roughness_source)


def solution(mesh):
    in_specs = (
        P("aa", None, None),
        P("comp", "aa", None, "ba", None),
        P(),
        P("aa", "ba", "comp"),
        P("aa", "ba"),
        P("aa", None),
        P("aa", "ba"),
    )
    out_specs = (P("comp", "aa", None, "ba"), P("aa", "ba", "comp"), P("aa", "ba"))
    return jax.shard_map(
        per_device, mesh=mesh, in_specs=in_specs, out_specs=out_specs, check_vma=False
    )
```

```python
import math

import numpy as np

import jax
import jax.numpy as jnp
from jax import lax
from jax.experimental import pallas as pl
from jax.experimental.pallas import tpu as pltpu
from jax.sharding import PartitionSpec as P

LON = 4096
NDIR = 36
NFREQ = 36
F32 = jnp.float32
BF16 = jnp.bfloat16
MESH = pl.DeviceIdType.MESH

N_A = 8
N_B = 16
N_X = 4
N_Z = 4
WAVES = 640
BLOCK = WAVES // N_A
GROUPS = BLOCK // 8
NT = 1280
CYCLES = 4
SLOTS = LON // N_B
ROWS = 16
COLS = 32
VMEM = 64_000_000
HALF = NDIR * NFREQ // 2
POINTS = 128
TILES = [(j, min(128, HALF - j)) for j in range(0, HALF, 128)]


def bin_table():
    b = np.arange(NDIR * NFREQ)
    theta = 2 * np.pi * (b // NFREQ + 0.5) / NDIR
    ratio = np.exp(-math.log(1.1) * (b % NFREQ))
    freq = 0.04177 / ratio
    east = 0.45 * ratio * np.cos(theta)
    north = 0.45 * ratio * np.sin(theta)
    q = 2 * np.pi * freq / 9.81
    width = 0.1 * freq * (2 * np.pi / NDIR)
    rows = [
        np.abs(east),
        np.abs(north),
        1.0 - np.abs(east) - np.abs(north),
        np.sign(east),
        np.sign(north),
        10.0 * q * np.cos(theta),
        10.0 * q * np.sin(theta),
        width,
        0.5 * freq / 0.2,
    ]
    rows += [np.zeros_like(freq)] * (16 - len(rows))
    table = np.stack(rows).astype(np.float32)
    return np.stack([table[:, :HALF], table[:, HALF:]])


AE, AN, CC, SE, SN, QE, QN, WB, DF = range(9)


def poly(y2, coefs):
    acc = jnp.full_like(y2, coefs[-1])
    for c in coefs[-2::-1]:
        acc = acc * y2 + c
    return acc


SIN_C = [(-1.0) ** i / math.factorial(2 * i + 1) for i in range(7)]
COS_C = [(-1.0) ** i / math.factorial(2 * i) for i in range(7)]


def turn(mk, count, inv):
    rest = mk - jnp.floor(mk * inv + 0.5) * count
    y = (rest * inv) * math.pi
    y2 = y * y
    s = y * poly(y2, SIN_C)
    c = poly(y2, COS_C)
    return 1.0 - 2.0 * s * s, 2.0 * s * c


def rcopy(src, dst, send, recv, device):
    return pltpu.make_async_remote_copy(
        src_ref=src, dst_ref=dst, send_sem=send, recv_sem=recv, device_id=device, device_id_type=MESH
    )


def lanes(rows, width=128):
    return lax.broadcasted_iota(jnp.int32, (rows, width), 1)


def sublanes(rows, width=128):
    return lax.broadcasted_iota(jnp.int32, (rows, width), 0)


def spread(row, n):
    kept = jnp.where(sublanes(n, n) == lanes(n, n), jnp.broadcast_to(row, (n, n)), 0.0)
    return jnp.broadcast_to(jnp.sum(kept, axis=1, keepdims=True), (n, 128))


def one_hot(mask):
    return mask.astype(F32).astype(BF16)


def dot(x, y, dims=((1,), (0,))):
    return lax.dot_general(x, y, (dims, ((), ())), preferred_element_type=F32)


def kernel(
    cp_hbm, leg_hbm, coef_hbm, spec_hbm, mask_hbm, wc_hbm, cst_hbm,
    gw_out, ws_out, rough_out,
    gw_ref, ws_ref, rough, cp_ref, leg, coef, spec, mask_in, wc, cst_ref, sall, msg, a2a, a2x, gath, gperm, low_f, l0,
    table, ptable, ca, sa, buf_a, buf_b, d2, edge, edge_in,
    mask_b, east_b, north_b, part, part_in, stress, order_in, order_out,
    i_sem, leg_sem, a_send, a_recv, x_send, x_recv, g_send, g_recv, l_send, l_recv, h_send, h_recv,
    c_send, c_recv, r_send, r_recv, o_sem,
):
    s = lax.axis_index("comp")
    a = lax.axis_index("aa")
    b = lax.axis_index("ba")
    x, z = b // N_Z, b % N_Z
    partner = {"comp": 1 - s}

    coef_copy = pltpu.make_async_copy(coef_hbm, coef, i_sem.at[0])
    coef_copy.start()
    leg_copies = lambda g: pltpu.make_async_copy(
        leg_hbm.at[pl.ds(g * 8, 8)], leg.at[pl.ds(g * 8, 8)], leg_sem.at[g]
    )
    for g in range(GROUPS):
        leg_copies(g).start()
    small = [
        pltpu.make_async_copy(mask_hbm, mask_in, i_sem.at[1]),
        pltpu.make_async_copy(wc_hbm, wc, i_sem.at[2]),
        pltpu.make_async_copy(cst_hbm, cst_ref, i_sem.at[3]),
        pltpu.make_async_copy(spec_hbm, spec, i_sem.at[4]),
        pltpu.make_async_copy(cp_hbm, cp_ref, i_sem.at[5]),
    ]
    for c in small:
        c.start()

    barrier = pltpu.get_barrier_semaphore()
    pl.semaphore_signal(barrier, inc=1, device_id=partner, device_id_type=MESH)
    for d in range(1, N_A):
        pl.semaphore_signal(barrier, inc=1, device_id={"aa": lax.rem(a + d, N_A)}, device_id_type=MESH)
    for d in range(1, N_B):
        pl.semaphore_signal(barrier, inc=1, device_id={"ba": lax.rem(b + d, N_B)}, device_id_type=MESH)

    for d in range(1, N_B):
        pl.semaphore_signal(
            barrier, inc=1, device_id={"comp": 1 - s, "ba": lax.rem(b + d, N_B)}, device_id_type=MESH
        )

    @pl.when(b == 0)
    def _():
        for d in range(1, N_A):
            pl.semaphore_signal(
                barrier, inc=1, device_id={"comp": 1 - s, "aa": lax.rem(a + d, N_A)}, device_id_type=MESH
            )

    coef_copy.wait()

    def legendre(g, carry):
        rows = []
        for i in range(8):
            order = a * BLOCK + g * 8 + i
            block = jnp.concatenate([coef[g * 8 + i, p].astype(F32) for p in range(2)], axis=0)
            rows.append(jnp.where(lanes(8, NT) >= order, block, 0.0))
        rows = jnp.concatenate(rows, axis=0).astype(BF16)
        leg_copies(g).wait()
        cross = dot(rows, leg[pl.ds(g * 8, 8)].reshape(256, NT), ((1,), (1,)))
        at = pl.ds(pl.multiple_of(g * 8, 8), 8)
        for t in range(2):
            kept = cross[t * 32 : t * 32 + 8, t * 128 : t * 128 + 128]
            for q in range(1, 4):
                m = t * 4 + q
                kept = jnp.where(lanes(8) >= q * 32, cross[m * 8 : m * 8 + 8, t * 128 : t * 128 + 128], kept)
            sall[at, t * 128 : t * 128 + 128] = kept
        return carry

    lax.fori_loop(0, GROUPS, legendre, 0)

    i, o = sublanes(256, 256), lanes(256, 256)
    moved = dot(sall[...].astype(BF16), one_hot(o == (i & 31) // 4 * 32 + (i // 32) * 4 + (i & 3)))
    turned = {}
    for t in range(N_A):
        for q in range(3):
            acc = jnp.zeros((8, 128), F32)
            for g in range(q * 4, min(q * 4 + 4, GROUPS)):
                shift = 32 * ((g - t) % 4)
                key = (g, t // 4, shift)
                if key not in turned:
                    v = moved[g * 8 : g * 8 + 8, t // 4 * 128 : t // 4 * 128 + 128]
                    turned[key] = pltpu.roll(v, shift, axis=1) if shift else v
                at = lanes(8) // 32 == g % 4
                acc = jnp.where(at, turned[key], acc)
            msg[t, :, q * 128 : q * 128 + 128] = acc

    pl.semaphore_wait(barrier, N_A + 2 * N_B - 2 + jnp.where(b == 0, N_A - 1, 0))

    sent = []
    for d in range(1, N_A):
        t = lax.rem(a + d, N_A)
        c = rcopy(msg.at[t], a2a.at[a], a_send.at[d - 1], a_recv.at[a], {"aa": t})
        c.start()
        sent.append(c)
    crossed = []
    for d in range(N_A):
        t = lax.rem(a + d, N_A)
        crossed.append(
            rcopy(msg.at[t], a2x.at[a], x_send.at[d], x_recv.at[a], {"comp": 1 - s, "aa": t})
        )

    @pl.when(b == 0)
    def _():
        for c in crossed:
            c.start()

    a2a[a] = msg[a]

    for c in small:
        c.wait()
    sea = mask_in[...].astype(F32)
    for r in range(ROWS):
        mask_b[r * COLS : (r + 1) * COLS, :] = spread(sea[r : r + 1, :], COLS)

    def first(r, carry):
        m = mask_b[pl.ds(r * COLS, COLS), :]
        for j, w in TILES:
            v = spec[r, :, j : j + w] * m[:, :w]
            buf_a[r + 1, 8 : 8 + COLS, j : j + w] = v
            edge[0, 0, r, :, j : j + w] = v[0:1, :]
            edge[0, 1, r, :, j : j + w] = v[COLS - 1 : COLS, :]
        return carry

    lax.fori_loop(0, ROWS, first, 0)

    def halo(buf, step):
        return [
            (a < N_A - 1, a > 0, rcopy(
                buf.at[ROWS, pl.ds(8, COLS)], buf.at[0, pl.ds(8, COLS)],
                h_send.at[step, 0], h_recv.at[step, 0], {"aa": lax.rem(a + 1, N_A)})),
            (a > 0, a < N_A - 1, rcopy(
                buf.at[1, pl.ds(8, COLS)], buf.at[ROWS + 1, pl.ds(8, COLS)],
                h_send.at[step, 1], h_recv.at[step, 1], {"aa": lax.rem(a + N_A - 1, N_A)})),
            (b < N_B - 1, b > 0, rcopy(
                edge.at[step, 1], edge_in.at[step, 0],
                h_send.at[step, 2], h_recv.at[step, 2], {"ba": lax.rem(b + 1, N_B)})),
            (b > 0, b < N_B - 1, rcopy(
                edge.at[step, 0], edge_in.at[step, 1],
                h_send.at[step, 3], h_recv.at[step, 3], {"ba": lax.rem(b + N_B - 1, N_B)})),
        ]

    def halo_start(copies):
        for can, _, c in copies:
            pl.when(can)(c.start)

    def halo_land(copies, buf, step):
        for i, (_, comes, c) in enumerate(copies):
            pl.when(comes)(c.wait_recv)

            @pl.when(jnp.logical_not(comes))
            def _():
                if i < 2:
                    buf[0 if i == 0 else ROWS + 1, 8 : 8 + COLS, :] = jnp.zeros((COLS, HALF), F32)
                else:
                    edge_in[step, i - 2] = jnp.zeros((ROWS, 1, HALF), F32)

        for r in range(ROWS):
            buf[r + 1, 7:8, :] = edge_in[step, 0, r]
            buf[r + 1, 8 + COLS : 9 + COLS, :] = edge_in[step, 1, r]

    def halo_sent(copies):
        for can, _, c in copies:
            pl.when(can)(c.wait_send)

    halo_a = halo(buf_a, 0)
    halo_start(halo_a)

    def tables(out, l, k, active):
        w = k.shape[1]
        count = jnp.full((1, w), cp_ref[a * CYCLES + l], jnp.int32).astype(F32)
        inv = 1.0 / count
        cu, su = turn(sublanes(WAVES // 8, w).astype(F32) * 8.0 * k, count, inv)
        ca[:, :, :w] = cu.reshape(GROUPS, 8, w)
        sa[:, :, :w] = su.reshape(GROUPS, 8, w)
        cv, sv = turn(sublanes(8, w).astype(F32) * k, count, inv)
        cv, sv = cv * active, sv * active
        minus_c, minus_s = -cv, -sv

        def block(i, carry):
            for h in range(4):
                cs, ss = [], []
                for o in range(h * 2, h * 2 + 2):
                    c0, s0 = ca[i, o : o + 1, :w], sa[i, o : o + 1, :w]
                    cs.append(c0 * cv + s0 * minus_s)
                    ss.append(s0 * minus_c + c0 * minus_s)
                at = pl.multiple_of(i * 64 + h * 16, 16)
                out[l, pl.ds(at, 16), :] = jnp.concatenate(cs, axis=0).astype(BF16)
                out[l, pl.ds(WAVES + at, 16), :] = jnp.concatenate(ss, axis=0).astype(BF16)
            return carry

        lax.fori_loop(0, GROUPS, block, 0)
        top = out[l, 0:16, :].astype(F32)
        out[l, 0:16, :] = jnp.where(sublanes(16, w) == 0, top * 0.5, top).astype(BF16)

    near = wc[:, pl.ds(pl.multiple_of(b // 4 * 128, 128), 128)].astype(F32)
    near = pltpu.roll(near, (4 - b % 4) % 4 * COLS, axis=1)
    near = jnp.where(lanes(ROWS) < COLS, near, 0.0)
    side = near
    for q in range(1, 4):
        side = jnp.where(sublanes(ROWS) % 4 == q, pltpu.roll(near, q * COLS, axis=1), side)
    for l in range(CYCLES):
        tables(ptable, l, jnp.sum(side[l * 4 : l * 4 + 4, :], axis=0, keepdims=True), 2.0)

    slots = lanes(1, SLOTS) + b * SLOTS
    for l in range(CYCLES):
        active = jnp.where(slots < cp_ref[a * CYCLES + l], 2.0, 0.0)
        tables(table, l, slots.astype(F32), active)

    i, o = sublanes(384, 512), lanes(384, 512)
    order_in[...] = one_hot((o == (i & 3) * 128 + i // 4) & (i < BLOCK * 4))
    r = sublanes(256, 256)
    order_out[...] = one_hot(lanes(256, 256) == (r & 63) // 4 * 16 + r // 64 * 4 + (r & 3))

    def upwind(buf, r, j, w):
        c = lambda i: cst_ref[s, i : i + 1, j : j + w]
        here = buf[r + 1, 8 : 8 + COLS, j : j + w]
        ux = jnp.where(c(SE) > 0.0, buf[r + 1, 7 : 7 + COLS, j : j + w], buf[r + 1, 9 : 9 + COLS, j : j + w])
        uy = jnp.where(c(SN) > 0.0, buf[r, 8 : 8 + COLS, j : j + w], buf[r + 2, 8 : 8 + COLS, j : j + w])
        return here * c(CC) + ux * c(AE) + uy * c(AN)

    halo_land(halo_a, buf_a, 0)

    def second(r, carry):
        m = mask_b[pl.ds(r * COLS, COLS), :]
        for j, w in TILES:
            v = upwind(buf_a, r, j, w) * m[:, :w]
            buf_b[r + 1, 8 : 8 + COLS, j : j + w] = v
            edge[1, 0, r, :, j : j + w] = v[0:1, :]
            edge[1, 1, r, :, j : j + w] = v[COLS - 1 : COLS, :]
        return carry

    lax.fori_loop(0, ROWS, second, 0)
    halo_b = halo(buf_b, 1)
    halo_start(halo_b)

    def compact(landed):
        wide = dot(landed[...].reshape(64, 384).astype(BF16), order_in[...])
        out = []
        for l in range(CYCLES):
            tiles = [jnp.zeros((8, 128), F32) for _ in range(WAVES // 128)]
            for c in range(N_A):
                t, shift = divmod(c * BLOCK, 128)
                piece = wide[c * 8 : c * 8 + 8, l * 128 : l * 128 + 128]
                if shift:
                    piece = pltpu.roll(piece, shift, axis=1)
                    tiles[t] = jnp.where(lanes(8) >= shift, piece, tiles[t])
                    if shift + BLOCK > 128:
                        tiles[t + 1] = jnp.where(lanes(8) < shift, piece, tiles[t + 1])
                else:
                    tiles[t] = jnp.where(lanes(8) < BLOCK, piece, tiles[t])
            out.append(tiles)
        return out

    def lowest(blocks, base):
        for l in range(CYCLES):
            for t in range(WAVES // 128):
                for p in range(2):
                    r = base + p * 4 + l
                    low_f[r : r + 1, t * 128 : t * 128 + 128] = blocks[l][t][p * 4 : p * 4 + 1, :]

    for d in range(1, N_A):
        c = lax.rem(a + N_A - d, N_A)
        rcopy(msg.at[0], a2a.at[c], a_send.at[d - 1], a_recv.at[c], {"aa": c}).wait_recv()
    blocks = compact(a2a)
    low = [
        rcopy(l0, l0, l_send.at[d - 1], l_recv.at[0], {"ba": lax.rem(b + d, N_B)}) for d in range(1, N_B)
    ]

    @pl.when(b == 0)
    def _():
        lowest(blocks, 0)
        for d in range(N_A):
            c = lax.rem(a + N_A - d, N_A)
            rcopy(msg.at[0], a2x.at[c], x_send.at[d], x_recv.at[c], {"comp": 1 - s, "aa": c}).wait_recv()
        lowest(compact(a2x), 8)
        l0[...] = low_f[...].astype(BF16)
        for c in low:
            c.start()

    for t in range(WAVES // 128):
        up = [pltpu.roll(blocks[l][t], 4, axis=0) for l in range(CYCLES)]
        own = [blocks[l][t] for l in range(CYCLES)]
        top = sublanes(8) < 4
        for p in range(2):
            pair = [
                jnp.where(top, own[l], up[l + 1]) if p == 0 else jnp.where(top, up[l], own[l + 1])
                for l in (0, 2)
            ]
            at = p * WAVES + t * 128
            gath[b, :, at : at + 128] = jnp.concatenate(pair, axis=0).astype(BF16)

    gathers = []

    def give(o, device):
        c = rcopy(gath.at[o], gath.at[o], g_send.at[len(gathers)], g_recv.at[o], {"ba": device})
        c.start()
        gathers.append(c)

    def arrived(o):
        rcopy(gath.at[o], gath.at[o], g_send.at[0], g_recv.at[o], {"ba": o}).wait_recv()

    x_peers = [lax.rem(x + d, N_X) * N_Z + z for d in (1, 3, 2)]
    for d in range(1, N_Z):
        give(b, x * N_Z + lax.rem(z + d, N_Z))
    for t in x_peers:
        give(b, t)

    halo_land(halo_b, buf_b, 1)

    def third(r, carry):
        at = pl.ds(r * COLS, COLS)
        m = mask_b[at, :]
        total = jnp.zeros((COLS, 128), F32)
        for j, w in TILES:
            v = upwind(buf_b, r, j, w) * m[:, :w]
            d2[r, :, j : j + w] = v
            term = v * cst_ref[s, WB : WB + 1, j : j + w]
            if w == 128:
                total = total + term
            else:
                part[0, at, :] = total
                part[0, at, :w] = total[:, :w] + term
        return carry

    lax.fori_loop(0, ROWS, third, 0)
    energy_copy = rcopy(part.at[0], part_in, c_send.at[0], c_recv.at[0], partner)
    energy_copy.start()

    for d in range(1, N_Z):
        o = x * N_Z + lax.rem(z + N_Z - d, N_Z)
        arrived(o)
        for t in x_peers:
            give(o, t)

    @pl.when(b > 0)
    def _():
        low[0].wait_recv()

    own, other = [], []
    for l in range(CYCLES):
        pc = dot(l0[...], ptable[l, 0:WAVES, :])
        ps = dot(l0[...], ptable[l, WAVES:, :])
        own.append((pc[l : l + 1, :] + ps[4 + l : 5 + l, :]).astype(BF16).astype(F32))
        other.append((pc[8 + l : 9 + l, :] + ps[12 + l : 13 + l, :]).astype(BF16).astype(F32))
    east = [jnp.where(s == 0, p, q) for p, q in zip(own, other)]
    north = [jnp.where(s == 0, q, p) for p, q in zip(own, other)]
    for l in range(CYCLES):
        east_b[pl.ds(l * POINTS, POINTS), :] = spread(east[l], POINTS)
        north_b[pl.ds(l * POINTS, POINTS), :] = spread(north[l], POINTS)

    def gain_of(e, n, r, j, w):
        c = lambda i: cst_ref[s, i : i + 1, j : j + w]
        align = e[:, :w] * c(QE) + n[:, :w] * c(QN)
        grown = 0.05 * jnp.maximum(align - 1.0, 0.0) * d2[r, :, j : j + w]
        return align, grown

    def fourth(r, carry):
        at = pl.ds(r * COLS, COLS)
        e, n = east_b[at, :], north_b[at, :]
        total = jnp.zeros((COLS, 128), F32)
        for j, w in TILES:
            align, grown = gain_of(e, n, r, j, w)
            term = grown * align * cst_ref[s, WB : WB + 1, j : j + w]
            if w == 128:
                total = total + term
            else:
                part[1, at, :] = total
                part[1, at, :w] = total[:, :w] + term
        return carry

    lax.fori_loop(0, ROWS, fourth, 0)
    for l in range(CYCLES):
        total = jnp.sum(part[1, pl.ds(l * POINTS, POINTS), :], axis=1, keepdims=True)
        kept = jnp.where(sublanes(POINTS) == lanes(POINTS), jnp.broadcast_to(total, (POINTS, 128)), 0.0)
        row = jnp.sum(kept, axis=0, keepdims=True)
        stress[s, b, l : l + 1, :] = row
        stress[s, b, 4 + l : 5 + l, :] = 0.12 * (east[l] * east[l] + north[l] * north[l]) + 0.02
    band = [(s, lax.rem(b + d, N_B)) for d in range(1, N_B)] + [(1 - s, lax.rem(b + d, N_B)) for d in range(N_B)]
    rough_copies = []
    for n, (c, t) in enumerate(band):
        own_block = stress.at[s, b]
        rough_copies.append(
            rcopy(own_block, own_block, r_send.at[n], r_recv.at[s, b], {"comp": c, "ba": t})
        )
        rough_copies[-1].start()

    energy_copy.wait_recv()
    for l in range(CYCLES):
        at = pl.ds(l * POINTS, POINTS)
        level = jnp.sum(part[0, at, :] + part_in[at, :], axis=1, keepdims=True) * 0.125
        mask_b[at, :] = jnp.broadcast_to(level * level, (POINTS, 128))

    def fifth(r, carry):
        at = pl.ds(r * COLS, COLS)
        e, n = east_b[at, :], north_b[at, :]
        square = mask_b[at, :]
        for j, w in TILES:
            _, grown = gain_of(e, n, r, j, w)
            decay = square[:, :w] * cst_ref[s, DF : DF + 1, j : j + w]
            ws_ref[r, :, j : j + w] = (d2[r, :, j : j + w] + grown) / (1.0 + decay)
        return carry

    lax.fori_loop(0, ROWS, fifth, 0)
    ws_copy = pltpu.make_async_copy(ws_ref, ws_out, o_sem.at[0])
    ws_copy.start()

    for xd in range(1, N_X):
        for zd in range(N_Z):
            arrived(lax.rem(x + N_X - xd, N_X) * N_Z + lax.rem(z + zd, N_Z))
    for k in range(0, 2 * WAVES, 256):
        gperm[:, k : k + 256] = dot(order_out[...], gath[:, :, k : k + 256].reshape(256, 256)).astype(BF16)
    for l in range(CYCLES):
        gw_ref[0, l] = dot(gperm[l * 64 : l * 64 + 64, :], table[l]).astype(BF16)
    gw_copy = pltpu.make_async_copy(gw_ref, gw_out, o_sem.at[1])
    gw_copy.start()

    for n, (c, t) in enumerate(band):
        o = lax.rem(2 * b + N_B - t, N_B)
        rcopy(stress.at[c, o], stress.at[c, o], r_send.at[n], r_recv.at[c, o], {"comp": c, "ba": o}).wait_recv()
    total = stress[0, :, 0:4, :] + stress[1, :, 0:4, :]
    rough[:, 0:4, :] = jnp.sqrt(1.0 + 0.03 * total / stress[0, :, 4:8, :])
    rough[:, 4:8, :] = jnp.zeros((N_B, 4, 128), F32)
    rough_copy = pltpu.make_async_copy(rough, rough_out, o_sem.at[2])
    rough_copy.start()
    for c in sent + gathers + rough_copies + [energy_copy]:
        c.wait_send()
    halo_sent(halo_a)
    halo_sent(halo_b)

    @pl.when(b == 0)
    def _():
        for c in low + crossed:
            c.wait_send()

    for c in (ws_copy, gw_copy, rough_copy):
        c.wait()


def last(
    cp_hbm, gw_in, ws_in, rough_in, rs_hbm, gw_ref, ws_ref, ch_ref, cp_ref, gw, ws, rough, rs_ref, sem_in, sem_out
):
    a = lax.axis_index("aa")
    slots = lanes(1, SLOTS) + lax.axis_index("ba") * SLOTS
    step = ROWS // 4
    blocks = [pl.ds(i * step, step) for i in range(4)]
    come = [pltpu.make_async_copy(ws_in.at[k], ws.at[k], sem_in.at[i]) for i, k in enumerate(blocks)]
    come.append(pltpu.make_async_copy(gw_in, gw, sem_in.at[4]))
    go = [pltpu.make_async_copy(ws.at[k], ws_ref.at[k], sem_out.at[i]) for i, k in enumerate(blocks)]
    go.append(pltpu.make_async_copy(gw, gw_ref, sem_out.at[4]))
    other = [
        pltpu.make_async_copy(rough_in, rough, sem_in.at[5]),
        pltpu.make_async_copy(rs_hbm, rs_ref, sem_in.at[6]),
        pltpu.make_async_copy(cp_hbm, cp_ref, sem_in.at[7]),
    ]
    for c in other + come:
        c.start()
    for c, d in zip(come, go):
        c.wait()
        d.start()
    for c in other:
        c.wait()
    for l in range(CYCLES):
        source = rs_ref[l : l + 1, :]
        low_part = ((source >> 9) & 3) * 32 + (source & 31)
        high_part = (source >> 5) & 15
        pick = one_hot(sublanes(128, SLOTS) == low_part)
        values = rough[:, l, :]
        h0 = values.astype(BF16)
        r1 = values - h0.astype(F32)
        h1 = r1.astype(BF16)
        h2 = (r1 - h1.astype(F32)).astype(BF16)
        got = dot(h0, pick) + (dot(h1, pick) + dot(h2, pick))
        keep = sublanes(N_B, SLOTS) == high_part
        row = jnp.sum(jnp.where(keep, got, 0.0), axis=0, keepdims=True)
        ch_ref[l : l + 1, :] = jnp.where(slots < cp_ref[a * CYCLES + l], row, 0.0)
    for c in go:
        c.wait()


def per_device(legendre, coefficients, cycle_points, spectra, sea_mask, wind_column, roughness_source):
    vmem = pl.BlockSpec(memory_space=pltpu.VMEM)
    smem = pl.BlockSpec(memory_space=pltpu.SMEM)
    hbm = pl.BlockSpec(memory_space=pltpu.HBM)
    dma = pltpu.SemaphoreType.DMA
    winds = jax.ShapeDtypeStruct((1, CYCLES, 64, SLOTS), BF16)
    waves = jax.ShapeDtypeStruct((ROWS, COLS, HALF), F32)
    winds_done, waves_done, rough = pl.pallas_call(
        kernel,
        out_shape=(winds, waves, jax.ShapeDtypeStruct((N_B, 8, 128), F32)),
        in_specs=[hbm] * 7,
        out_specs=(hbm, hbm, hbm),
        scratch_shapes=[
            pltpu.VMEM((1, CYCLES, 64, SLOTS), BF16),
            pltpu.VMEM((ROWS, COLS, HALF), F32),
            pltpu.VMEM((N_B, 8, 128), F32),
            pltpu.SMEM((32,), jnp.int32),
            pltpu.VMEM((BLOCK, 32, NT), BF16),
            pltpu.VMEM((BLOCK, 2, 4, NT), BF16),
            pltpu.VMEM((ROWS, COLS, HALF), F32),
            pltpu.VMEM((ROWS, COLS), jnp.int32),
            pltpu.VMEM((ROWS, 512), jnp.int32),
            pltpu.VMEM((2, 16, HALF), F32),
            pltpu.VMEM((BLOCK, 256), F32),
            pltpu.VMEM((N_A, 8, 384), F32),
            pltpu.VMEM((N_A, 8, 384), F32),
            pltpu.VMEM((N_A, 8, 384), F32),
            pltpu.VMEM((N_B, 16, 2 * WAVES), BF16),
            pltpu.VMEM((256, 2 * WAVES), BF16),
            pltpu.VMEM((16, WAVES), F32),
            pltpu.VMEM((16, WAVES), BF16),
            pltpu.VMEM((CYCLES, 2 * WAVES, SLOTS), BF16),
            pltpu.VMEM((CYCLES, 2 * WAVES, POINTS), BF16),
            pltpu.VMEM((GROUPS, 8, SLOTS), F32),
            pltpu.VMEM((GROUPS, 8, SLOTS), F32),
            pltpu.VMEM((ROWS + 2, COLS + 16, HALF), F32),
            pltpu.VMEM((ROWS + 2, COLS + 16, HALF), F32),
            pltpu.VMEM((ROWS, COLS, HALF), F32),
            pltpu.VMEM((2, 2, ROWS, 1, HALF), F32),
            pltpu.VMEM((2, 2, ROWS, 1, HALF), F32),
            pltpu.VMEM((ROWS * COLS, 128), F32),
            pltpu.VMEM((ROWS * COLS, 128), F32),
            pltpu.VMEM((ROWS * COLS, 128), F32),
            pltpu.VMEM((2, ROWS * COLS, 128), F32),
            pltpu.VMEM((ROWS * COLS, 128), F32),
            pltpu.VMEM((2, N_B, 8, 128), F32),
            pltpu.VMEM((384, 512), BF16),
            pltpu.VMEM((256, 256), BF16),
            dma((6,)), dma((GROUPS,)),
            dma((N_A - 1,)), dma((N_A,)),
            dma((N_A,)), dma((N_A,)),
            dma((N_B - 1,)), dma((N_B,)),
            dma((N_B - 1,)), dma((1,)),
            dma((2, 4)), dma((2, 4)),
            dma((1,)), dma((1,)),
            dma((2 * N_B - 1,)), dma((2, N_B)),
            dma((3,)),
        ],
        compiler_params=pltpu.CompilerParams(
            collective_id=0, has_side_effects=True, vmem_limit_bytes=VMEM
        ),
    )(
        cycle_points, legendre, coefficients.reshape(BLOCK, 2, 4, NT), spectra, sea_mask, wind_column,
        jnp.asarray(bin_table()),
    )
    return pl.pallas_call(
        last,
        out_shape=(winds, waves, jax.ShapeDtypeStruct((CYCLES, SLOTS), F32)),
        in_specs=[hbm] * 5,
        out_specs=(hbm, hbm, vmem),
        scratch_shapes=[
            pltpu.SMEM((32,), jnp.int32),
            pltpu.VMEM((1, CYCLES, 64, SLOTS), BF16),
            pltpu.VMEM((ROWS, COLS, HALF), F32),
            pltpu.VMEM((N_B, 8, 128), F32),
            pltpu.VMEM((CYCLES, SLOTS), jnp.int32),
            dma((8,)), dma((5,)),
        ],
        compiler_params=pltpu.CompilerParams(vmem_limit_bytes=VMEM),
    )(cycle_points, winds_done, waves_done, rough, roughness_source)


def solution(mesh):
    in_specs = (
        P("aa", None, None),
        P("comp", "aa", None, "ba", None),
        P(),
        P("aa", "ba", "comp"),
        P("aa", "ba"),
        P("aa", None),
        P("aa", "ba"),
    )
    out_specs = (P("comp", "aa", None, "ba"), P("aa", "ba", "comp"), P("aa", "ba"))
    return jax.shard_map(
        per_device, mesh=mesh, in_specs=in_specs, out_specs=out_specs, check_vma=False
    )
```

```python
import math

import numpy as np

import jax
import jax.numpy as jnp
from jax import lax
from jax.experimental import pallas as pl
from jax.experimental.pallas import tpu as pltpu
from jax.sharding import PartitionSpec as P

LON = 4096
NDIR = 36
NFREQ = 36
F32 = jnp.float32
BF16 = jnp.bfloat16
MESH = pl.DeviceIdType.MESH

N_A = 8
N_B = 16
N_X = 4
N_Z = 4
WAVES = 640
BLOCK = WAVES // N_A
GROUPS = BLOCK // 8
NT = 1280
CYCLES = 4
SLOTS = LON // N_B
ROWS = 16
COLS = 32
VMEM = 64_000_000
HALF = NDIR * NFREQ // 2
POINTS = 128
TILES = [(j, min(128, HALF - j)) for j in range(0, HALF, 128)]


def bin_table():
    b = np.arange(NDIR * NFREQ)
    theta = 2 * np.pi * (b // NFREQ + 0.5) / NDIR
    ratio = np.exp(-math.log(1.1) * (b % NFREQ))
    freq = 0.04177 / ratio
    east = 0.45 * ratio * np.cos(theta)
    north = 0.45 * ratio * np.sin(theta)
    q = 2 * np.pi * freq / 9.81
    assert (north[:HALF] > 0).all() and (north[HALF:] < 0).all()
    width = 0.1 * freq * (2 * np.pi / NDIR)
    rows = [
        np.abs(east),
        np.abs(north),
        1.0 - np.abs(east) - np.abs(north),
        np.sign(east),
        np.sign(north),
        10.0 * q * np.cos(theta),
        10.0 * q * np.sin(theta),
        width,
        0.5 * freq / 0.2,
    ]
    rows += [np.zeros_like(freq)] * (16 - len(rows))
    table = np.stack(rows).astype(np.float32)
    return np.stack([table[:, :HALF], table[:, HALF:]])


AE, AN, CC, SE, SN, QE, QN, WB, DF = range(9)


def poly(y2, coefs):
    acc = jnp.full_like(y2, coefs[-1])
    for c in coefs[-2::-1]:
        acc = acc * y2 + c
    return acc


SIN_C = [(-1.0) ** i / math.factorial(2 * i + 1) for i in range(7)]
COS_C = [(-1.0) ** i / math.factorial(2 * i) for i in range(7)]


def turn(mk, count, inv):
    rest = mk - jnp.floor(mk * inv + 0.5) * count
    y = (rest * inv) * math.pi
    y2 = y * y
    s = y * poly(y2, SIN_C)
    c = poly(y2, COS_C)
    return 1.0 - 2.0 * s * s, 2.0 * s * c


def rcopy(src, dst, send, recv, device):
    return pltpu.make_async_remote_copy(
        src_ref=src, dst_ref=dst, send_sem=send, recv_sem=recv, device_id=device, device_id_type=MESH
    )


def lanes(rows, width=128):
    return lax.broadcasted_iota(jnp.int32, (rows, width), 1)


def sublanes(rows, width=128):
    return lax.broadcasted_iota(jnp.int32, (rows, width), 0)


def spread(row, n):
    kept = jnp.where(sublanes(n, n) == lanes(n, n), jnp.broadcast_to(row, (n, n)), 0.0)
    return jnp.broadcast_to(jnp.sum(kept, axis=1, keepdims=True), (n, 128))


def one_hot(mask):
    return mask.astype(F32).astype(BF16)


def dot(x, y, dims=((1,), (0,))):
    return lax.dot_general(x, y, (dims, ((), ())), preferred_element_type=F32)


def kernel(
    cp_hbm, leg_hbm, coef_hbm, spec_hbm, mask_hbm, wc_hbm, cst_hbm,
    gw_out, ws_out, rough_out,
    gw_ref, ws_ref, rough, cp_ref, leg, coef, spec, mask_in, wc, cst_ref, sall, msg, a2a, a2x, gath, gperm, low_f, l0,
    table, ptable, ca, sa, buf_a, buf_b, d2, edge, edge_in,
    mask_b, east_b, north_b, part, part_in, stress, order_in, order_out,
    i_sem, leg_sem, a_send, a_recv, x_send, x_recv, g_send, g_recv, l_send, l_recv, h_send, h_recv,
    c_send, c_recv, r_send, r_recv, o_sem,
):
    s = lax.axis_index("comp")
    a = lax.axis_index("aa")
    b = lax.axis_index("ba")
    x, z = b // N_Z, b % N_Z
    partner = {"comp": 1 - s}

    small = [
        pltpu.make_async_copy(mask_hbm, mask_in, i_sem.at[1]),
        pltpu.make_async_copy(wc_hbm, wc, i_sem.at[2]),
        pltpu.make_async_copy(cst_hbm, cst_ref, i_sem.at[3]),
        pltpu.make_async_copy(spec_hbm, spec, i_sem.at[4]),
        pltpu.make_async_copy(cp_hbm, cp_ref, i_sem.at[5]),
    ]
    for c in small:
        c.start()
    coef_copy = pltpu.make_async_copy(coef_hbm, coef, i_sem.at[0])
    coef_copy.start()
    leg_copies = lambda g: pltpu.make_async_copy(
        leg_hbm.at[pl.ds(g * 8, 8)], leg.at[pl.ds(g * 8, 8)], leg_sem.at[g]
    )
    for g in range(GROUPS):
        leg_copies(g).start()
    barrier = pltpu.get_barrier_semaphore()
    pl.semaphore_signal(barrier, inc=1, device_id=partner, device_id_type=MESH)
    for d in range(1, N_A):
        pl.semaphore_signal(barrier, inc=1, device_id={"aa": lax.rem(a + d, N_A)}, device_id_type=MESH)
    for d in range(1, N_B):
        pl.semaphore_signal(barrier, inc=1, device_id={"ba": lax.rem(b + d, N_B)}, device_id_type=MESH)

    for d in range(1, N_B):
        pl.semaphore_signal(
            barrier, inc=1, device_id={"comp": 1 - s, "ba": lax.rem(b + d, N_B)}, device_id_type=MESH
        )

    @pl.when(b == 0)
    def _():
        for d in range(1, N_A):
            pl.semaphore_signal(
                barrier, inc=1, device_id={"comp": 1 - s, "aa": lax.rem(a + d, N_A)}, device_id_type=MESH
            )

    for c in small:
        c.wait()
    sea = mask_in[...].astype(F32)
    for r in range(ROWS):
        mask_b[r * COLS : (r + 1) * COLS, :] = spread(sea[r : r + 1, :], COLS)

    def first(r, carry):
        m = mask_b[pl.ds(r * COLS, COLS), :]
        for j, w in TILES:
            v = spec[r, :, j : j + w] * m[:, :w]
            buf_a[r + 1, 8 : 8 + COLS, j : j + w] = v
            edge[0, 0, r, :, j : j + w] = v[0:1, :]
            edge[0, 1, r, :, j : j + w] = v[COLS - 1 : COLS, :]
        return carry

    lax.fori_loop(0, ROWS, first, 0)

    def halo(buf, step):
        up = jnp.where(s == 0, N_A - 2 - a, a - 1)
        down = jnp.where(s == 0, a - 1, N_A - 2 - a)
        return [
            (up >= 0, down >= 0, rcopy(
                buf.at[ROWS - (ROWS - 1) * s, pl.ds(8, COLS)], buf.at[(ROWS + 1) * s, pl.ds(8, COLS)],
                h_send.at[step, 0], h_recv.at[step, 0], {"aa": lax.rem(a + 1 + (N_A - 2) * s, N_A)})),
            (b < N_B - 1, b > 0, rcopy(
                edge.at[step, 1], edge_in.at[step, 0],
                h_send.at[step, 1], h_recv.at[step, 1], {"ba": lax.rem(b + 1, N_B)})),
            (b > 0, b < N_B - 1, rcopy(
                edge.at[step, 0], edge_in.at[step, 1],
                h_send.at[step, 2], h_recv.at[step, 2], {"ba": lax.rem(b + N_B - 1, N_B)})),
        ]

    def halo_start(copies):
        for can, _, c in copies:
            pl.when(can)(c.start)

    def halo_land(copies, buf, step):
        for i, (_, comes, c) in enumerate(copies):
            pl.when(comes)(c.wait_recv)

            @pl.when(jnp.logical_not(comes))
            def _():
                if i == 0:
                    buf[(ROWS + 1) * s, 8 : 8 + COLS, :] = jnp.zeros((COLS, HALF), F32)
                else:
                    edge_in[step, i - 1] = jnp.zeros((ROWS, 1, HALF), F32)

        for r in range(ROWS):
            buf[r + 1, 7:8, :] = edge_in[step, 0, r]
            buf[r + 1, 8 + COLS : 9 + COLS, :] = edge_in[step, 1, r]

    def halo_sent(copies):
        for can, _, c in copies:
            pl.when(can)(c.wait_send)

    coef_copy.wait()

    def legendre(g, carry):
        rows = []
        for i in range(8):
            order = a * BLOCK + g * 8 + i
            block = jnp.concatenate([coef[g * 8 + i, p].astype(F32) for p in range(2)], axis=0)
            rows.append(jnp.where(lanes(8, NT) >= order, block, 0.0))
        rows = jnp.concatenate(rows, axis=0).astype(BF16)
        leg_copies(g).wait()
        cross = dot(rows, leg[pl.ds(g * 8, 8)].reshape(256, NT), ((1,), (1,)))
        at = pl.ds(pl.multiple_of(g * 8, 8), 8)
        for t in range(2):
            kept = cross[t * 32 : t * 32 + 8, t * 128 : t * 128 + 128]
            for q in range(1, 4):
                m = t * 4 + q
                kept = jnp.where(lanes(8) >= q * 32, cross[m * 8 : m * 8 + 8, t * 128 : t * 128 + 128], kept)
            sall[at, t * 128 : t * 128 + 128] = kept
        return carry

    lax.fori_loop(0, GROUPS // 2, legendre, 0)
    pl.semaphore_wait(barrier, N_A + 2 * N_B - 2 + jnp.where(b == 0, N_A - 1, 0))
    halo_a = halo(buf_a, 0)
    halo_start(halo_a)
    lax.fori_loop(GROUPS // 2, GROUPS, legendre, 0)

    i, o = sublanes(256, 256), lanes(256, 256)
    moved = dot(sall[...].astype(BF16), one_hot(o == (i & 31) // 4 * 32 + (i // 32) * 4 + (i & 3)))
    turned = {}
    for t in range(N_A):
        for q in range(3):
            acc = jnp.zeros((8, 128), F32)
            for g in range(q * 4, min(q * 4 + 4, GROUPS)):
                shift = 32 * ((g - t) % 4)
                key = (g, t // 4, shift)
                if key not in turned:
                    v = moved[g * 8 : g * 8 + 8, t // 4 * 128 : t // 4 * 128 + 128]
                    turned[key] = pltpu.roll(v, shift, axis=1) if shift else v
                at = lanes(8) // 32 == g % 4
                acc = jnp.where(at, turned[key], acc)
            msg[t, :, q * 128 : q * 128 + 128] = acc

    sent = []
    for d in range(1, N_A):
        t = lax.rem(a + d, N_A)
        c = rcopy(msg.at[t], a2a.at[a], a_send.at[d - 1], a_recv.at[a], {"aa": t})
        c.start()
        sent.append(c)
    crossed = []
    for d in range(N_A):
        t = lax.rem(a + d, N_A)
        crossed.append(
            rcopy(msg.at[t], a2x.at[a], x_send.at[d], x_recv.at[a], {"comp": 1 - s, "aa": t})
        )

    @pl.when(b == 0)
    def _():
        for c in crossed:
            c.start()

    a2a[a] = msg[a]


    def tables(out, l, k, active):
        w = k.shape[1]
        count = jnp.full((1, w), cp_ref[a * CYCLES + l], jnp.int32).astype(F32)
        inv = 1.0 / count
        cu, su = turn(sublanes(WAVES // 8, w).astype(F32) * 8.0 * k, count, inv)
        ca[:, :, :w] = cu.reshape(GROUPS, 8, w)
        sa[:, :, :w] = su.reshape(GROUPS, 8, w)
        cv, sv = turn(sublanes(8, w).astype(F32) * k, count, inv)
        cv, sv = cv * active, sv * active
        minus_c, minus_s = -cv, -sv

        def block(i, carry):
            for h in range(4):
                cs, ss = [], []
                for o in range(h * 2, h * 2 + 2):
                    c0, s0 = ca[i, o : o + 1, :w], sa[i, o : o + 1, :w]
                    cs.append(c0 * cv + s0 * minus_s)
                    ss.append(s0 * minus_c + c0 * minus_s)
                at = pl.multiple_of(i * 64 + h * 16, 16)
                out[l, pl.ds(at, 16), :] = jnp.concatenate(cs, axis=0).astype(BF16)
                out[l, pl.ds(WAVES + at, 16), :] = jnp.concatenate(ss, axis=0).astype(BF16)
            return carry

        lax.fori_loop(0, GROUPS, block, 0)
        top = out[l, 0:16, :].astype(F32)
        out[l, 0:16, :] = jnp.where(sublanes(16, w) == 0, top * 0.5, top).astype(BF16)

    near = wc[:, pl.ds(pl.multiple_of(b // 4 * 128, 128), 128)].astype(F32)
    near = pltpu.roll(near, (4 - b % 4) % 4 * COLS, axis=1)
    near = jnp.where(lanes(ROWS) < COLS, near, 0.0)
    side = near
    for q in range(1, 4):
        side = jnp.where(sublanes(ROWS) % 4 == q, pltpu.roll(near, q * COLS, axis=1), side)
    for l in range(CYCLES):
        tables(ptable, l, jnp.sum(side[l * 4 : l * 4 + 4, :], axis=0, keepdims=True), 2.0)

    slots = lanes(1, SLOTS) + b * SLOTS
    for l in range(CYCLES):
        active = jnp.where(slots < cp_ref[a * CYCLES + l], 2.0, 0.0)
        tables(table, l, slots.astype(F32), active)

    i, o = sublanes(384, 512), lanes(384, 512)
    order_in[...] = one_hot((o == (i & 3) * 128 + i // 4) & (i < BLOCK * 4))
    r = sublanes(256, 256)
    order_out[...] = one_hot(lanes(256, 256) == (r & 63) // 4 * 16 + r // 64 * 4 + (r & 3))

    def upwind(buf, r, j, w):
        c = lambda i: cst_ref[s, i : i + 1, j : j + w]
        here = buf[r + 1, 8 : 8 + COLS, j : j + w]
        ux = jnp.where(c(SE) > 0.0, buf[r + 1, 7 : 7 + COLS, j : j + w], buf[r + 1, 9 : 9 + COLS, j : j + w])
        uy = buf[r + 2 * s, 8 : 8 + COLS, j : j + w]
        return here * c(CC) + ux * c(AE) + uy * c(AN)

    halo_land(halo_a, buf_a, 0)

    def second(r, carry):
        m = mask_b[pl.ds(r * COLS, COLS), :]
        for j, w in TILES:
            v = upwind(buf_a, r, j, w) * m[:, :w]
            buf_b[r + 1, 8 : 8 + COLS, j : j + w] = v
            edge[1, 0, r, :, j : j + w] = v[0:1, :]
            edge[1, 1, r, :, j : j + w] = v[COLS - 1 : COLS, :]
        return carry

    lax.fori_loop(0, ROWS, second, 0)
    halo_b = halo(buf_b, 1)
    halo_start(halo_b)

    def compact(landed):
        wide = dot(landed[...].reshape(64, 384).astype(BF16), order_in[...])
        out = []
        for l in range(CYCLES):
            tiles = [jnp.zeros((8, 128), F32) for _ in range(WAVES // 128)]
            for c in range(N_A):
                t, shift = divmod(c * BLOCK, 128)
                piece = wide[c * 8 : c * 8 + 8, l * 128 : l * 128 + 128]
                if shift:
                    piece = pltpu.roll(piece, shift, axis=1)
                    tiles[t] = jnp.where(lanes(8) >= shift, piece, tiles[t])
                    if shift + BLOCK > 128:
                        tiles[t + 1] = jnp.where(lanes(8) < shift, piece, tiles[t + 1])
                else:
                    tiles[t] = jnp.where(lanes(8) < BLOCK, piece, tiles[t])
            out.append(tiles)
        return out

    def lowest(blocks, base):
        for l in range(CYCLES):
            for t in range(WAVES // 128):
                for p in range(2):
                    r = base + p * 4 + l
                    low_f[r : r + 1, t * 128 : t * 128 + 128] = blocks[l][t][p * 4 : p * 4 + 1, :]

    for d in range(1, N_A):
        c = lax.rem(a + N_A - d, N_A)
        rcopy(msg.at[0], a2a.at[c], a_send.at[d - 1], a_recv.at[c], {"aa": c}).wait_recv()
    blocks = compact(a2a)
    low = [
        rcopy(l0, l0, l_send.at[d - 1], l_recv.at[0], {"ba": lax.rem(b + d, N_B)}) for d in range(1, N_B)
    ]

    @pl.when(b == 0)
    def _():
        lowest(blocks, 0)
        for d in range(N_A):
            c = lax.rem(a + N_A - d, N_A)
            rcopy(msg.at[0], a2x.at[c], x_send.at[d], x_recv.at[c], {"comp": 1 - s, "aa": c}).wait_recv()
        lowest(compact(a2x), 8)
        l0[...] = low_f[...].astype(BF16)
        for c in low:
            c.start()

    for t in range(WAVES // 128):
        up = [pltpu.roll(blocks[l][t], 4, axis=0) for l in range(CYCLES)]
        own = [blocks[l][t] for l in range(CYCLES)]
        top = sublanes(8) < 4
        for p in range(2):
            pair = [
                jnp.where(top, own[l], up[l + 1]) if p == 0 else jnp.where(top, up[l], own[l + 1])
                for l in (0, 2)
            ]
            at = p * WAVES + t * 128
            gath[b, :, at : at + 128] = jnp.concatenate(pair, axis=0).astype(BF16)

    gathers = []

    def give(o, device):
        c = rcopy(gath.at[o], gath.at[o], g_send.at[len(gathers)], g_recv.at[o], {"ba": device})
        c.start()
        gathers.append(c)

    def arrived(o):
        rcopy(gath.at[o], gath.at[o], g_send.at[0], g_recv.at[o], {"ba": o}).wait_recv()

    x_peers = [lax.rem(x + d, N_X) * N_Z + z for d in (1, 3, 2)]
    for d in range(1, N_Z):
        give(b, x * N_Z + lax.rem(z + d, N_Z))
    for t in x_peers:
        give(b, t)

    halo_land(halo_b, buf_b, 1)

    def third(r, carry):
        at = pl.ds(r * COLS, COLS)
        m = mask_b[at, :]
        total = jnp.zeros((COLS, 128), F32)
        for j, w in TILES:
            v = upwind(buf_b, r, j, w) * m[:, :w]
            d2[r, :, j : j + w] = v
            term = v * cst_ref[s, WB : WB + 1, j : j + w]
            if w == 128:
                total = total + term
            else:
                part[0, at, :] = total
                part[0, at, :w] = total[:, :w] + term
        return carry

    lax.fori_loop(0, ROWS, third, 0)
    energy_copy = rcopy(part.at[0], part_in, c_send.at[0], c_recv.at[0], partner)
    energy_copy.start()

    for d in range(1, N_Z):
        o = x * N_Z + lax.rem(z + N_Z - d, N_Z)
        arrived(o)
        for t in x_peers:
            give(o, t)

    @pl.when(b > 0)
    def _():
        low[0].wait_recv()

    own, other = [], []
    for l in range(CYCLES):
        pc = dot(l0[...], ptable[l, 0:WAVES, :])
        ps = dot(l0[...], ptable[l, WAVES:, :])
        own.append((pc[l : l + 1, :] + ps[4 + l : 5 + l, :]).astype(BF16).astype(F32))
        other.append((pc[8 + l : 9 + l, :] + ps[12 + l : 13 + l, :]).astype(BF16).astype(F32))
    east = [jnp.where(s == 0, p, q) for p, q in zip(own, other)]
    north = [jnp.where(s == 0, q, p) for p, q in zip(own, other)]
    for l in range(CYCLES):
        east_b[pl.ds(l * POINTS, POINTS), :] = spread(east[l], POINTS)
        north_b[pl.ds(l * POINTS, POINTS), :] = spread(north[l], POINTS)

    def gain_of(e, n, r, j, w):
        c = lambda i: cst_ref[s, i : i + 1, j : j + w]
        align = e[:, :w] * c(QE) + n[:, :w] * c(QN)
        grown = 0.05 * jnp.maximum(align - 1.0, 0.0) * d2[r, :, j : j + w]
        return align, grown

    def fourth(r, carry):
        at = pl.ds(r * COLS, COLS)
        e, n = east_b[at, :], north_b[at, :]
        total = jnp.zeros((COLS, 128), F32)
        for j, w in TILES:
            align, grown = gain_of(e, n, r, j, w)
            term = grown * align * cst_ref[s, WB : WB + 1, j : j + w]
            if w == 128:
                total = total + term
            else:
                part[1, at, :] = total
                part[1, at, :w] = total[:, :w] + term
        return carry

    lax.fori_loop(0, ROWS, fourth, 0)
    for l in range(CYCLES):
        total = jnp.sum(part[1, pl.ds(l * POINTS, POINTS), :], axis=1, keepdims=True)
        kept = jnp.where(sublanes(POINTS) == lanes(POINTS), jnp.broadcast_to(total, (POINTS, 128)), 0.0)
        row = jnp.sum(kept, axis=0, keepdims=True)
        stress[s, b, l : l + 1, :] = row
        stress[s, b, 4 + l : 5 + l, :] = 0.12 * (east[l] * east[l] + north[l] * north[l]) + 0.02
    band = [(s, lax.rem(b + d, N_B)) for d in range(1, N_B)] + [(1 - s, lax.rem(b + d, N_B)) for d in range(N_B)]
    rough_copies = []
    for n, (c, t) in enumerate(band):
        own_block = stress.at[s, b]
        rough_copies.append(
            rcopy(own_block, own_block, r_send.at[n], r_recv.at[s, b], {"comp": c, "ba": t})
        )
        rough_copies[-1].start()

    energy_copy.wait_recv()
    for l in range(CYCLES):
        at = pl.ds(l * POINTS, POINTS)
        level = jnp.sum(part[0, at, :] + part_in[at, :], axis=1, keepdims=True) * 0.125
        mask_b[at, :] = jnp.broadcast_to(level * level, (POINTS, 128))

    def fifth(r, carry):
        at = pl.ds(r * COLS, COLS)
        e, n = east_b[at, :], north_b[at, :]
        square = mask_b[at, :]
        for j, w in TILES:
            _, grown = gain_of(e, n, r, j, w)
            decay = square[:, :w] * cst_ref[s, DF : DF + 1, j : j + w]
            ws_ref[r, :, j : j + w] = (d2[r, :, j : j + w] + grown) / (1.0 + decay)
        return carry

    lax.fori_loop(0, ROWS, fifth, 0)
    ws_copy = pltpu.make_async_copy(ws_ref, ws_out, o_sem.at[0])
    ws_copy.start()

    for xd in range(1, N_X):
        for zd in range(N_Z):
            arrived(lax.rem(x + N_X - xd, N_X) * N_Z + lax.rem(z + zd, N_Z))
    for k in range(0, 2 * WAVES, 256):
        gperm[:, k : k + 256] = dot(order_out[...], gath[:, :, k : k + 256].reshape(256, 256)).astype(BF16)
    for l in range(CYCLES):
        gw_ref[0, l] = dot(gperm[l * 64 : l * 64 + 64, :], table[l]).astype(BF16)
    gw_copy = pltpu.make_async_copy(gw_ref, gw_out, o_sem.at[1])
    gw_copy.start()

    for n, (c, t) in enumerate(band):
        o = lax.rem(2 * b + N_B - t, N_B)
        rcopy(stress.at[c, o], stress.at[c, o], r_send.at[n], r_recv.at[c, o], {"comp": c, "ba": o}).wait_recv()
    total = stress[0, :, 0:4, :] + stress[1, :, 0:4, :]
    rough[:, 0:4, :] = jnp.sqrt(1.0 + 0.03 * total / stress[0, :, 4:8, :])
    rough[:, 4:8, :] = jnp.zeros((N_B, 4, 128), F32)
    rough_copy = pltpu.make_async_copy(rough, rough_out, o_sem.at[2])
    rough_copy.start()
    for c in sent + gathers + rough_copies + [energy_copy]:
        c.wait_send()
    halo_sent(halo_a)
    halo_sent(halo_b)

    @pl.when(b == 0)
    def _():
        for c in low + crossed:
            c.wait_send()

    for c in (ws_copy, gw_copy, rough_copy):
        c.wait()


def last(
    cp_hbm, gw_in, ws_in, rough_in, rs_hbm, gw_ref, ws_ref, ch_ref, cp_ref, gw, ws, rough, rs_ref, sem_in, sem_out
):
    a = lax.axis_index("aa")
    slots = lanes(1, SLOTS) + lax.axis_index("ba") * SLOTS
    step = ROWS // 4
    blocks = [pl.ds(i * step, step) for i in range(4)]
    come = [pltpu.make_async_copy(ws_in.at[k], ws.at[k], sem_in.at[i]) for i, k in enumerate(blocks)]
    come.append(pltpu.make_async_copy(gw_in, gw, sem_in.at[4]))
    go = [pltpu.make_async_copy(ws.at[k], ws_ref.at[k], sem_out.at[i]) for i, k in enumerate(blocks)]
    go.append(pltpu.make_async_copy(gw, gw_ref, sem_out.at[4]))
    other = [
        pltpu.make_async_copy(rough_in, rough, sem_in.at[5]),
        pltpu.make_async_copy(rs_hbm, rs_ref, sem_in.at[6]),
        pltpu.make_async_copy(cp_hbm, cp_ref, sem_in.at[7]),
    ]
    for c in other + come:
        c.start()
    for c, d in zip(come, go):
        c.wait()
        d.start()
    for c in other:
        c.wait()
    for l in range(CYCLES):
        source = rs_ref[l : l + 1, :]
        low_part = ((source >> 9) & 3) * 32 + (source & 31)
        high_part = (source >> 5) & 15
        pick = one_hot(sublanes(128, SLOTS) == low_part)
        values = rough[:, l, :]
        h0 = values.astype(BF16)
        r1 = values - h0.astype(F32)
        h1 = r1.astype(BF16)
        h2 = (r1 - h1.astype(F32)).astype(BF16)
        got = dot(h0, pick) + (dot(h1, pick) + dot(h2, pick))
        keep = sublanes(N_B, SLOTS) == high_part
        row = jnp.sum(jnp.where(keep, got, 0.0), axis=0, keepdims=True)
        ch_ref[l : l + 1, :] = jnp.where(slots < cp_ref[a * CYCLES + l], row, 0.0)
    for c in go:
        c.wait()


def per_device(legendre, coefficients, cycle_points, spectra, sea_mask, wind_column, roughness_source):
    vmem = pl.BlockSpec(memory_space=pltpu.VMEM)
    smem = pl.BlockSpec(memory_space=pltpu.SMEM)
    hbm = pl.BlockSpec(memory_space=pltpu.HBM)
    dma = pltpu.SemaphoreType.DMA
    winds = jax.ShapeDtypeStruct((1, CYCLES, 64, SLOTS), BF16)
    waves = jax.ShapeDtypeStruct((ROWS, COLS, HALF), F32)
    winds_done, waves_done, rough = pl.pallas_call(
        kernel,
        out_shape=(winds, waves, jax.ShapeDtypeStruct((N_B, 8, 128), F32)),
        in_specs=[hbm] * 7,
        out_specs=(hbm, hbm, hbm),
        scratch_shapes=[
            pltpu.VMEM((1, CYCLES, 64, SLOTS), BF16),
            pltpu.VMEM((ROWS, COLS, HALF), F32),
            pltpu.VMEM((N_B, 8, 128), F32),
            pltpu.SMEM((32,), jnp.int32),
            pltpu.VMEM((BLOCK, 32, NT), BF16),
            pltpu.VMEM((BLOCK, 2, 4, NT), BF16),
            pltpu.VMEM((ROWS, COLS, HALF), F32),
            pltpu.VMEM((ROWS, COLS), jnp.int32),
            pltpu.VMEM((ROWS, 512), jnp.int32),
            pltpu.VMEM((2, 16, HALF), F32),
            pltpu.VMEM((BLOCK, 256), F32),
            pltpu.VMEM((N_A, 8, 384), F32),
            pltpu.VMEM((N_A, 8, 384), F32),
            pltpu.VMEM((N_A, 8, 384), F32),
            pltpu.VMEM((N_B, 16, 2 * WAVES), BF16),
            pltpu.VMEM((256, 2 * WAVES), BF16),
            pltpu.VMEM((16, WAVES), F32),
            pltpu.VMEM((16, WAVES), BF16),
            pltpu.VMEM((CYCLES, 2 * WAVES, SLOTS), BF16),
            pltpu.VMEM((CYCLES, 2 * WAVES, POINTS), BF16),
            pltpu.VMEM((GROUPS, 8, SLOTS), F32),
            pltpu.VMEM((GROUPS, 8, SLOTS), F32),
            pltpu.VMEM((ROWS + 2, COLS + 16, HALF), F32),
            pltpu.VMEM((ROWS + 2, COLS + 16, HALF), F32),
            pltpu.VMEM((ROWS, COLS, HALF), F32),
            pltpu.VMEM((2, 2, ROWS, 1, HALF), F32),
            pltpu.VMEM((2, 2, ROWS, 1, HALF), F32),
            pltpu.VMEM((ROWS * COLS, 128), F32),
            pltpu.VMEM((ROWS * COLS, 128), F32),
            pltpu.VMEM((ROWS * COLS, 128), F32),
            pltpu.VMEM((2, ROWS * COLS, 128), F32),
            pltpu.VMEM((ROWS * COLS, 128), F32),
            pltpu.VMEM((2, N_B, 8, 128), F32),
            pltpu.VMEM((384, 512), BF16),
            pltpu.VMEM((256, 256), BF16),
            dma((6,)), dma((GROUPS,)),
            dma((N_A - 1,)), dma((N_A,)),
            dma((N_A,)), dma((N_A,)),
            dma((N_B - 1,)), dma((N_B,)),
            dma((N_B - 1,)), dma((1,)),
            dma((2, 3)), dma((2, 3)),
            dma((1,)), dma((1,)),
            dma((2 * N_B - 1,)), dma((2, N_B)),
            dma((3,)),
        ],
        compiler_params=pltpu.CompilerParams(
            collective_id=0, has_side_effects=True, vmem_limit_bytes=VMEM
        ),
    )(
        cycle_points, legendre, coefficients.reshape(BLOCK, 2, 4, NT), spectra, sea_mask, wind_column,
        jnp.asarray(bin_table()),
    )
    return pl.pallas_call(
        last,
        out_shape=(winds, waves, jax.ShapeDtypeStruct((CYCLES, SLOTS), F32)),
        in_specs=[hbm] * 5,
        out_specs=(hbm, hbm, vmem),
        scratch_shapes=[
            pltpu.SMEM((32,), jnp.int32),
            pltpu.VMEM((1, CYCLES, 64, SLOTS), BF16),
            pltpu.VMEM((ROWS, COLS, HALF), F32),
            pltpu.VMEM((N_B, 8, 128), F32),
            pltpu.VMEM((CYCLES, SLOTS), jnp.int32),
            dma((8,)), dma((5,)),
        ],
        compiler_params=pltpu.CompilerParams(vmem_limit_bytes=VMEM),
    )(cycle_points, winds_done, waves_done, rough, roughness_source)


def solution(mesh):
    in_specs = (
        P("aa", None, None),
        P("comp", "aa", None, "ba", None),
        P(),
        P("aa", "ba", "comp"),
        P("aa", "ba"),
        P("aa", None),
        P("aa", "ba"),
    )
    out_specs = (P("comp", "aa", None, "ba"), P("aa", "ba", "comp"), P("aa", "ba"))
    return jax.shard_map(
        per_device, mesh=mesh, in_specs=in_specs, out_specs=out_specs, check_vma=False
    )
```

```python
import math

import numpy as np

import jax
import jax.numpy as jnp
from jax import lax
from jax.experimental import pallas as pl
from jax.experimental.pallas import tpu as pltpu
from jax.sharding import PartitionSpec as P

LON = 4096
NDIR = 36
NFREQ = 36
F32 = jnp.float32
BF16 = jnp.bfloat16
MESH = pl.DeviceIdType.MESH

N_A = 8
N_B = 16
N_X = 4
N_Z = 4
WAVES = 640
BLOCK = WAVES // N_A
GROUPS = BLOCK // 8
NT = 1280
CYCLES = 4
SLOTS = LON // N_B
ROWS = 16
COLS = 32
VMEM = 64_000_000
HALF = NDIR * NFREQ // 2
POINTS = 128
FAR = [(2, 3), (2, 2), (1, 3), (3, 3), (2, 1), (1, 2), (3, 2), (0, 3), (1, 1), (3, 1), (2, 0), (0, 2), (1, 0), (3, 0), (0, 1)]
TILES = [(j, min(128, HALF - j)) for j in range(0, HALF, 128)]


def bin_table():
    b = np.arange(NDIR * NFREQ)
    theta = 2 * np.pi * (b // NFREQ + 0.5) / NDIR
    ratio = np.exp(-math.log(1.1) * (b % NFREQ))
    freq = 0.04177 / ratio
    east = 0.45 * ratio * np.cos(theta)
    north = 0.45 * ratio * np.sin(theta)
    q = 2 * np.pi * freq / 9.81
    assert (north[:HALF] > 0).all() and (north[HALF:] < 0).all()
    width = 0.1 * freq * (2 * np.pi / NDIR)
    rows = [
        np.abs(east),
        np.abs(north),
        1.0 - np.abs(east) - np.abs(north),
        np.sign(east),
        np.sign(north),
        10.0 * q * np.cos(theta),
        10.0 * q * np.sin(theta),
        width,
        0.5 * freq / 0.2,
    ]
    rows += [np.zeros_like(freq)] * (16 - len(rows))
    table = np.stack(rows).astype(np.float32)
    return np.stack([table[:, :HALF], table[:, HALF:]])


AE, AN, CC, SE, SN, QE, QN, WB, DF = range(9)


def poly(y2, coefs):
    acc = jnp.full_like(y2, coefs[-1])
    for c in coefs[-2::-1]:
        acc = acc * y2 + c
    return acc


SIN_C = [(-1.0) ** i / math.factorial(2 * i + 1) for i in range(7)]
COS_C = [(-1.0) ** i / math.factorial(2 * i) for i in range(7)]


def turn(mk, count, inv):
    rest = mk - jnp.floor(mk * inv + 0.5) * count
    y = (rest * inv) * math.pi
    y2 = y * y
    s = y * poly(y2, SIN_C)
    c = poly(y2, COS_C)
    return 1.0 - 2.0 * s * s, 2.0 * s * c


def rcopy(src, dst, send, recv, device):
    return pltpu.make_async_remote_copy(
        src_ref=src, dst_ref=dst, send_sem=send, recv_sem=recv, device_id=device, device_id_type=MESH
    )


def lanes(rows, width=128):
    return lax.broadcasted_iota(jnp.int32, (rows, width), 1)


def sublanes(rows, width=128):
    return lax.broadcasted_iota(jnp.int32, (rows, width), 0)


def spread(row, n):
    kept = jnp.where(sublanes(n, n) == lanes(n, n), jnp.broadcast_to(row, (n, n)), 0.0)
    return jnp.broadcast_to(jnp.sum(kept, axis=1, keepdims=True), (n, 128))


def one_hot(mask):
    return mask.astype(F32).astype(BF16)


def dot(x, y, dims=((1,), (0,))):
    return lax.dot_general(x, y, (dims, ((), ())), preferred_element_type=F32)


def kernel(
    cp_hbm, leg_hbm, coef_hbm, spec_hbm, mask_hbm, wc_hbm, cst_hbm,
    gw_out, ws_out, rough_out,
    gw_ref, ws_ref, rough, cp_ref, leg, coef, spec, mask_in, wc, cst_ref, sall, msg, a2a, a2x, gath, gperm, low_f, l0,
    table, ptable, ca, sa, buf_a, buf_b, d2, edge, edge_in, row_out, row_in,
    mask_b, east_b, north_b, part, part_in, stress, order_in, order_out,
    i_sem, leg_sem, a_send, a_recv, x_send, x_recv, g_send, g_recv, l_send, l_recv, h_send, h_recv,
    c_send, c_recv, r_send, r_recv, o_sem,
):
    s = lax.axis_index("comp")
    a = lax.axis_index("aa")
    b = lax.axis_index("ba")
    x, z = b // N_Z, b % N_Z
    partner = {"comp": 1 - s}

    flips = lambda v: {0: v, 1: v + 1 - 2 * (v % 2), 2: lax.rem(v + 2, 4), 3: 3 - v}
    flip_x, flip_z, flip_y = flips(x), flips(z), flips(a % 4)
    half = a // 4
    peers_a = [(1 - half) * 4 + flip_y[i] for i in (2, 1, 3, 0)] + [half * 4 + flip_y[i] for i in (2, 1, 3)]
    peers_b = [flip_x[i] * N_Z + flip_z[j] for i, j in FAR]

    small = [
        pltpu.make_async_copy(mask_hbm, mask_in, i_sem.at[1]),
        pltpu.make_async_copy(wc_hbm, wc, i_sem.at[2]),
        pltpu.make_async_copy(cst_hbm, cst_ref, i_sem.at[3]),
        pltpu.make_async_copy(spec_hbm, spec, i_sem.at[4]),
        pltpu.make_async_copy(cp_hbm, cp_ref, i_sem.at[5]),
    ]
    coef_copy = pltpu.make_async_copy(coef_hbm, coef, i_sem.at[0])
    coef_copy.start()
    leg_copies = lambda g: pltpu.make_async_copy(
        leg_hbm.at[pl.ds(g * 8, 8)], leg.at[pl.ds(g * 8, 8)], leg_sem.at[g]
    )
    for g in range(GROUPS):
        leg_copies(g).start()
    for c in small:
        c.start()
    barrier = pltpu.get_barrier_semaphore()
    pl.semaphore_signal(barrier, inc=1, device_id=partner, device_id_type=MESH)
    for t in peers_a:
        pl.semaphore_signal(barrier, inc=1, device_id={"aa": t}, device_id_type=MESH)
    for t in peers_b:
        pl.semaphore_signal(barrier, inc=1, device_id={"ba": t}, device_id_type=MESH)
        pl.semaphore_signal(barrier, inc=1, device_id={"comp": 1 - s, "ba": t}, device_id_type=MESH)

    @pl.when(b == 0)
    def _():
        for t in peers_a:
            pl.semaphore_signal(barrier, inc=1, device_id={"comp": 1 - s, "aa": t}, device_id_type=MESH)

    def halo(buf, step):
        up = jnp.where(s == 0, N_A - 2 - a, a - 1)
        down = jnp.where(s == 0, a - 1, N_A - 2 - a)
        return [
            (up >= 0, down >= 0, rcopy(
                row_out.at[step], row_in.at[step],
                h_send.at[step, 0], h_recv.at[step, 0], {"aa": lax.rem(a + 1 + (N_A - 2) * s, N_A)})),
            (b < N_B - 1, b > 0, rcopy(
                edge.at[step, 1], edge_in.at[step, 0],
                h_send.at[step, 1], h_recv.at[step, 1], {"ba": lax.rem(b + 1, N_B)})),
            (b > 0, b < N_B - 1, rcopy(
                edge.at[step, 0], edge_in.at[step, 1],
                h_send.at[step, 2], h_recv.at[step, 2], {"ba": lax.rem(b + N_B - 1, N_B)})),
        ]

    def halo_start(copies, buf, step):
        row_out[step] = buf[ROWS - (ROWS - 1) * s, 8 : 8 + COLS, :].astype(BF16)
        for can, _, c in copies:
            pl.when(can)(c.start)

    def halo_land(copies, buf, step):
        for i, (_, comes, c) in enumerate(copies):
            pl.when(comes)(c.wait_recv)

            @pl.when(jnp.logical_not(comes))
            def _():
                if i == 0:
                    row_in[step] = jnp.zeros((COLS, HALF), BF16)
                else:
                    edge_in[step, i - 1] = jnp.zeros((ROWS, 1, HALF), F32)

        buf[(ROWS + 1) * s, 8 : 8 + COLS, :] = row_in[step].astype(F32)
        for r in range(ROWS):
            buf[r + 1, 7:8, :] = edge_in[step, 0, r]
            buf[r + 1, 8 + COLS : 9 + COLS, :] = edge_in[step, 1, r]

    def halo_sent(copies):
        for can, _, c in copies:
            pl.when(can)(c.wait_send)

    coef_copy.wait()

    def legendre(g, carry):
        rows = []
        for i in range(8):
            order = a * BLOCK + g * 8 + i
            block = jnp.concatenate([coef[g * 8 + i, p].astype(F32) for p in range(2)], axis=0)
            rows.append(jnp.where(lanes(8, NT) >= order, block, 0.0))
        rows = jnp.concatenate(rows, axis=0).astype(BF16)
        leg_copies(g).wait()
        cross = dot(rows, leg[pl.ds(g * 8, 8)].reshape(256, NT), ((1,), (1,)))
        at = pl.ds(pl.multiple_of(g * 8, 8), 8)
        for t in range(2):
            kept = cross[t * 32 : t * 32 + 8, t * 128 : t * 128 + 128]
            for q in range(1, 4):
                m = t * 4 + q
                kept = jnp.where(lanes(8) >= q * 32, cross[m * 8 : m * 8 + 8, t * 128 : t * 128 + 128], kept)
            sall[at, t * 128 : t * 128 + 128] = kept
        return carry

    lax.fori_loop(0, GROUPS, legendre, 0)

    i, o = sublanes(256, 256), lanes(256, 256)
    moved = dot(sall[...].astype(BF16), one_hot(o == (i & 31) // 4 * 32 + (i // 32) * 4 + (i & 3)))
    turned = {}
    for t in range(N_A):
        for q in range(3):
            acc = jnp.zeros((8, 128), F32)
            for g in range(q * 4, min(q * 4 + 4, GROUPS)):
                shift = 32 * ((g - t) % 4)
                key = (g, t // 4, shift)
                if key not in turned:
                    v = moved[g * 8 : g * 8 + 8, t // 4 * 128 : t // 4 * 128 + 128]
                    turned[key] = pltpu.roll(v, shift, axis=1) if shift else v
                at = lanes(8) // 32 == g % 4
                acc = jnp.where(at, turned[key], acc)
            msg[t, :, q * 128 : q * 128 + 128] = acc

    pl.semaphore_wait(barrier, N_A + 2 * N_B - 2 + jnp.where(b == 0, N_A - 1, 0))
    sent = []
    for d, t in enumerate(peers_a):
        c = rcopy(msg.at[t], a2a.at[a], a_send.at[d], a_recv.at[a], {"aa": t})
        c.start()
        sent.append(c)
    crossed = []
    for d, t in enumerate(peers_a + [a]):
        crossed.append(
            rcopy(msg.at[t], a2x.at[a], x_send.at[d], x_recv.at[a], {"comp": 1 - s, "aa": t})
        )

    @pl.when(b == 0)
    def _():
        for c in crossed:
            c.start()

    a2a[a] = msg[a]


    for c in small:
        c.wait()
    sea = mask_in[...].astype(F32)
    for r in range(ROWS):
        mask_b[r * COLS : (r + 1) * COLS, :] = spread(sea[r : r + 1, :], COLS)

    def first(r, carry):
        m = mask_b[pl.ds(r * COLS, COLS), :]
        for j, w in TILES:
            v = spec[r, :, j : j + w] * m[:, :w]
            buf_a[r + 1, 8 : 8 + COLS, j : j + w] = v
            edge[0, 0, r, :, j : j + w] = v[0:1, :]
            edge[0, 1, r, :, j : j + w] = v[COLS - 1 : COLS, :]
        return carry

    lax.fori_loop(0, ROWS, first, 0)

    halo_a = halo(buf_a, 0)
    halo_start(halo_a, buf_a, 0)

    def tables(out, l, k, active):
        w = k.shape[1]
        count = jnp.full((1, w), cp_ref[a * CYCLES + l], jnp.int32).astype(F32)
        inv = 1.0 / count
        cu, su = turn(sublanes(WAVES // 8, w).astype(F32) * 8.0 * k, count, inv)
        ca[:, :, :w] = cu.reshape(GROUPS, 8, w)
        sa[:, :, :w] = su.reshape(GROUPS, 8, w)
        cv, sv = turn(sublanes(8, w).astype(F32) * k, count, inv)
        cv, sv = cv * active, sv * active
        minus_c, minus_s = -cv, -sv

        def block(i, carry):
            for h in range(4):
                cs, ss = [], []
                for o in range(h * 2, h * 2 + 2):
                    c0, s0 = ca[i, o : o + 1, :w], sa[i, o : o + 1, :w]
                    cs.append(c0 * cv + s0 * minus_s)
                    ss.append(s0 * minus_c + c0 * minus_s)
                at = pl.multiple_of(i * 64 + h * 16, 16)
                out[l, pl.ds(at, 16), :] = jnp.concatenate(cs, axis=0).astype(BF16)
                out[l, pl.ds(WAVES + at, 16), :] = jnp.concatenate(ss, axis=0).astype(BF16)
            return carry

        lax.fori_loop(0, GROUPS, block, 0)
        top = out[l, 0:16, :].astype(F32)
        out[l, 0:16, :] = jnp.where(sublanes(16, w) == 0, top * 0.5, top).astype(BF16)

    near = wc[:, pl.ds(pl.multiple_of(b // 4 * 128, 128), 128)].astype(F32)
    near = pltpu.roll(near, (4 - b % 4) % 4 * COLS, axis=1)
    near = jnp.where(lanes(ROWS) < COLS, near, 0.0)
    side = near
    for q in range(1, 4):
        side = jnp.where(sublanes(ROWS) % 4 == q, pltpu.roll(near, q * COLS, axis=1), side)
    for l in range(CYCLES):
        tables(ptable, l, jnp.sum(side[l * 4 : l * 4 + 4, :], axis=0, keepdims=True), 2.0)

    slots = lanes(1, SLOTS) + b * SLOTS
    for l in range(CYCLES):
        active = jnp.where(slots < cp_ref[a * CYCLES + l], 2.0, 0.0)
        tables(table, l, slots.astype(F32), active)

    i, o = sublanes(384, 512), lanes(384, 512)
    order_in[...] = one_hot((o == (i & 3) * 128 + i // 4) & (i < BLOCK * 4))
    r = sublanes(256, 256)
    order_out[...] = one_hot(lanes(256, 256) == (r & 63) // 4 * 16 + r // 64 * 4 + (r & 3))

    def upwind(buf, r, j, w):
        c = lambda i: cst_ref[s, i : i + 1, j : j + w]
        here = buf[r + 1, 8 : 8 + COLS, j : j + w]
        ux = jnp.where(c(SE) > 0.0, buf[r + 1, 7 : 7 + COLS, j : j + w], buf[r + 1, 9 : 9 + COLS, j : j + w])
        uy = buf[r + 2 * s, 8 : 8 + COLS, j : j + w]
        return here * c(CC) + ux * c(AE) + uy * c(AN)

    halo_land(halo_a, buf_a, 0)

    def second(r, carry):
        m = mask_b[pl.ds(r * COLS, COLS), :]
        for j, w in TILES:
            v = upwind(buf_a, r, j, w) * m[:, :w]
            buf_b[r + 1, 8 : 8 + COLS, j : j + w] = v
            edge[1, 0, r, :, j : j + w] = v[0:1, :]
            edge[1, 1, r, :, j : j + w] = v[COLS - 1 : COLS, :]
        return carry

    lax.fori_loop(0, ROWS, second, 0)
    halo_b = halo(buf_b, 1)
    halo_start(halo_b, buf_b, 1)

    def compact(landed):
        wide = dot(landed[...].reshape(64, 384).astype(BF16), order_in[...])
        out = []
        for l in range(CYCLES):
            tiles = [jnp.zeros((8, 128), F32) for _ in range(WAVES // 128)]
            for c in range(N_A):
                t, shift = divmod(c * BLOCK, 128)
                piece = wide[c * 8 : c * 8 + 8, l * 128 : l * 128 + 128]
                if shift:
                    piece = pltpu.roll(piece, shift, axis=1)
                    tiles[t] = jnp.where(lanes(8) >= shift, piece, tiles[t])
                    if shift + BLOCK > 128:
                        tiles[t + 1] = jnp.where(lanes(8) < shift, piece, tiles[t + 1])
                else:
                    tiles[t] = jnp.where(lanes(8) < BLOCK, piece, tiles[t])
            out.append(tiles)
        return out

    def lowest(blocks, base):
        for l in range(CYCLES):
            for t in range(WAVES // 128):
                for p in range(2):
                    r = base + p * 4 + l
                    low_f[r : r + 1, t * 128 : t * 128 + 128] = blocks[l][t][p * 4 : p * 4 + 1, :]

    for d, c in enumerate(peers_a):
        rcopy(msg.at[0], a2a.at[c], a_send.at[d], a_recv.at[c], {"aa": c}).wait_recv()
    blocks = compact(a2a)
    low = [
        rcopy(l0, l0, l_send.at[d], l_recv.at[0], {"ba": t}) for d, t in enumerate(peers_b)
    ]

    @pl.when(b == 0)
    def _():
        lowest(blocks, 0)
        for d, c in enumerate(peers_a + [a]):
            rcopy(msg.at[0], a2x.at[c], x_send.at[d], x_recv.at[c], {"comp": 1 - s, "aa": c}).wait_recv()
        lowest(compact(a2x), 8)
        l0[...] = low_f[...].astype(BF16)
        for c in low:
            c.start()

    for t in range(WAVES // 128):
        up = [pltpu.roll(blocks[l][t], 4, axis=0) for l in range(CYCLES)]
        own = [blocks[l][t] for l in range(CYCLES)]
        top = sublanes(8) < 4
        for p in range(2):
            pair = [
                jnp.where(top, own[l], up[l + 1]) if p == 0 else jnp.where(top, up[l], own[l + 1])
                for l in (0, 2)
            ]
            at = p * WAVES + t * 128
            gath[b, :, at : at + 128] = jnp.concatenate(pair, axis=0).astype(BF16)

    gathers = []

    def give(o, device):
        c = rcopy(gath.at[o], gath.at[o], g_send.at[len(gathers)], g_recv.at[o], {"ba": device})
        c.start()
        gathers.append(c)

    def arrived(o):
        rcopy(gath.at[o], gath.at[o], g_send.at[0], g_recv.at[o], {"ba": o}).wait_recv()

    x_peers = [flip_x[i] * N_Z + z for i in (2, 1, 3)]
    for i in (3, 2, 1):
        give(b, x * N_Z + flip_z[i])
    for t in x_peers:
        give(b, t)

    halo_land(halo_b, buf_b, 1)

    def third(r, carry):
        at = pl.ds(r * COLS, COLS)
        m = mask_b[at, :]
        total = jnp.zeros((COLS, 128), F32)
        for j, w in TILES:
            v = upwind(buf_b, r, j, w) * m[:, :w]
            d2[r, :, j : j + w] = v
            term = v * cst_ref[s, WB : WB + 1, j : j + w]
            if w == 128:
                total = total + term
            else:
                part[0, at, :] = total
                part[0, at, :w] = total[:, :w] + term
        return carry

    lax.fori_loop(0, ROWS, third, 0)
    energy_copy = rcopy(part.at[0], part_in, c_send.at[0], c_recv.at[0], partner)
    energy_copy.start()

    for i in (1, 2, 3):
        o = x * N_Z + flip_z[i]
        arrived(o)
        for t in x_peers:
            give(o, t)

    @pl.when(b > 0)
    def _():
        low[0].wait_recv()

    own, other = [], []
    for l in range(CYCLES):
        pc = dot(l0[...], ptable[l, 0:WAVES, :])
        ps = dot(l0[...], ptable[l, WAVES:, :])
        own.append((pc[l : l + 1, :] + ps[4 + l : 5 + l, :]).astype(BF16).astype(F32))
        other.append((pc[8 + l : 9 + l, :] + ps[12 + l : 13 + l, :]).astype(BF16).astype(F32))
    east = [jnp.where(s == 0, p, q) for p, q in zip(own, other)]
    north = [jnp.where(s == 0, q, p) for p, q in zip(own, other)]
    for l in range(CYCLES):
        east_b[pl.ds(l * POINTS, POINTS), :] = spread(east[l], POINTS)
        north_b[pl.ds(l * POINTS, POINTS), :] = spread(north[l], POINTS)

    def gain_of(e, n, r, j, w):
        c = lambda i: cst_ref[s, i : i + 1, j : j + w]
        align = e[:, :w] * c(QE) + n[:, :w] * c(QN)
        grown = 0.05 * jnp.maximum(align - 1.0, 0.0) * d2[r, :, j : j + w]
        return align, grown

    def fourth(r, carry):
        at = pl.ds(r * COLS, COLS)
        e, n = east_b[at, :], north_b[at, :]
        total = jnp.zeros((COLS, 128), F32)
        for j, w in TILES:
            align, grown = gain_of(e, n, r, j, w)
            term = grown * align * cst_ref[s, WB : WB + 1, j : j + w]
            if w == 128:
                total = total + term
            else:
                part[1, at, :] = total
                part[1, at, :w] = total[:, :w] + term
        return carry

    lax.fori_loop(0, ROWS, fourth, 0)
    for l in range(CYCLES):
        total = jnp.sum(part[1, pl.ds(l * POINTS, POINTS), :], axis=1, keepdims=True)
        kept = jnp.where(sublanes(POINTS) == lanes(POINTS), jnp.broadcast_to(total, (POINTS, 128)), 0.0)
        row = jnp.sum(kept, axis=0, keepdims=True)
        stress[s, b, l : l + 1, :] = row
        stress[s, b, 4 + l : 5 + l, :] = 0.12 * (east[l] * east[l] + north[l] * north[l]) + 0.02
    band = [(c, t) for t in peers_b for c in (1 - s, s)] + [(1 - s, b)]
    rough_copies = []
    for n, (c, t) in enumerate(band):
        own_block = stress.at[s, b]
        rough_copies.append(
            rcopy(own_block, own_block, r_send.at[n], r_recv.at[s, b], {"comp": c, "ba": t})
        )
        rough_copies[-1].start()

    energy_copy.wait_recv()
    for l in range(CYCLES):
        at = pl.ds(l * POINTS, POINTS)
        level = jnp.sum(part[0, at, :] + part_in[at, :], axis=1, keepdims=True) * 0.125
        mask_b[at, :] = jnp.broadcast_to(level * level, (POINTS, 128))

    def fifth(r, carry):
        at = pl.ds(r * COLS, COLS)
        e, n = east_b[at, :], north_b[at, :]
        square = mask_b[at, :]
        for j, w in TILES:
            _, grown = gain_of(e, n, r, j, w)
            decay = square[:, :w] * cst_ref[s, DF : DF + 1, j : j + w]
            ws_ref[r, :, j : j + w] = (d2[r, :, j : j + w] + grown) / (1.0 + decay)
        return carry

    lax.fori_loop(0, ROWS, fifth, 0)
    ws_copy = pltpu.make_async_copy(ws_ref, ws_out, o_sem.at[0])
    ws_copy.start()

    for xd in range(1, N_X):
        for zd in range(N_Z):
            arrived(lax.rem(x + N_X - xd, N_X) * N_Z + lax.rem(z + zd, N_Z))
    for k in range(0, 2 * WAVES, 256):
        gperm[:, k : k + 256] = dot(order_out[...], gath[:, :, k : k + 256].reshape(256, 256)).astype(BF16)
    for l in range(CYCLES):
        gw_ref[0, l] = dot(gperm[l * 64 : l * 64 + 64, :], table[l]).astype(BF16)
    gw_copy = pltpu.make_async_copy(gw_ref, gw_out, o_sem.at[1])
    gw_copy.start()

    for n, (c, t) in enumerate(band):
        rcopy(stress.at[c, t], stress.at[c, t], r_send.at[n], r_recv.at[c, t], {"comp": c, "ba": t}).wait_recv()
    total = stress[0, :, 0:4, :] + stress[1, :, 0:4, :]
    rough[:, 0:4, :] = jnp.sqrt(1.0 + 0.03 * total / stress[0, :, 4:8, :])
    rough[:, 4:8, :] = jnp.zeros((N_B, 4, 128), F32)
    rough_copy = pltpu.make_async_copy(rough, rough_out, o_sem.at[2])
    rough_copy.start()
    for c in sent + gathers + rough_copies + [energy_copy]:
        c.wait_send()
    halo_sent(halo_a)
    halo_sent(halo_b)

    @pl.when(b == 0)
    def _():
        for c in low + crossed:
            c.wait_send()

    for c in (ws_copy, gw_copy, rough_copy):
        c.wait()


def last(
    cp_hbm, gw_in, ws_in, rough_in, rs_hbm, gw_ref, ws_ref, ch_ref, cp_ref, gw, ws, rough, rs_ref, sem_in, sem_out
):
    a = lax.axis_index("aa")
    slots = lanes(1, SLOTS) + lax.axis_index("ba") * SLOTS
    step = ROWS // 4
    blocks = [pl.ds(i * step, step) for i in range(4)]
    come = [pltpu.make_async_copy(ws_in.at[k], ws.at[k], sem_in.at[i]) for i, k in enumerate(blocks)]
    come.append(pltpu.make_async_copy(gw_in, gw, sem_in.at[4]))
    go = [pltpu.make_async_copy(ws.at[k], ws_ref.at[k], sem_out.at[i]) for i, k in enumerate(blocks)]
    go.append(pltpu.make_async_copy(gw, gw_ref, sem_out.at[4]))
    other = [
        pltpu.make_async_copy(rough_in, rough, sem_in.at[5]),
        pltpu.make_async_copy(rs_hbm, rs_ref, sem_in.at[6]),
        pltpu.make_async_copy(cp_hbm, cp_ref, sem_in.at[7]),
    ]
    for c in other + come:
        c.start()
    for c, d in zip(come, go):
        c.wait()
        d.start()
    for c in other:
        c.wait()
    for l in range(CYCLES):
        source = rs_ref[l : l + 1, :]
        low_part = ((source >> 9) & 3) * 32 + (source & 31)
        high_part = (source >> 5) & 15
        pick = one_hot(sublanes(128, SLOTS) == low_part)
        values = rough[:, l, :]
        h0 = values.astype(BF16)
        r1 = values - h0.astype(F32)
        h1 = r1.astype(BF16)
        h2 = (r1 - h1.astype(F32)).astype(BF16)
        got = dot(h0, pick) + (dot(h1, pick) + dot(h2, pick))
        keep = sublanes(N_B, SLOTS) == high_part
        row = jnp.sum(jnp.where(keep, got, 0.0), axis=0, keepdims=True)
        ch_ref[l : l + 1, :] = jnp.where(slots < cp_ref[a * CYCLES + l], row, 0.0)
    for c in go:
        c.wait()


def per_device(legendre, coefficients, cycle_points, spectra, sea_mask, wind_column, roughness_source):
    vmem = pl.BlockSpec(memory_space=pltpu.VMEM)
    smem = pl.BlockSpec(memory_space=pltpu.SMEM)
    hbm = pl.BlockSpec(memory_space=pltpu.HBM)
    dma = pltpu.SemaphoreType.DMA
    winds = jax.ShapeDtypeStruct((1, CYCLES, 64, SLOTS), BF16)
    waves = jax.ShapeDtypeStruct((ROWS, COLS, HALF), F32)
    winds_done, waves_done, rough = pl.pallas_call(
        kernel,
        out_shape=(winds, waves, jax.ShapeDtypeStruct((N_B, 8, 128), F32)),
        in_specs=[hbm] * 7,
        out_specs=(hbm, hbm, hbm),
        scratch_shapes=[
            pltpu.VMEM((1, CYCLES, 64, SLOTS), BF16),
            pltpu.VMEM((ROWS, COLS, HALF), F32),
            pltpu.VMEM((N_B, 8, 128), F32),
            pltpu.SMEM((32,), jnp.int32),
            pltpu.VMEM((BLOCK, 32, NT), BF16),
            pltpu.VMEM((BLOCK, 2, 4, NT), BF16),
            pltpu.VMEM((ROWS, COLS, HALF), F32),
            pltpu.VMEM((ROWS, COLS), jnp.int32),
            pltpu.VMEM((ROWS, 512), jnp.int32),
            pltpu.VMEM((2, 16, HALF), F32),
            pltpu.VMEM((BLOCK, 256), F32),
            pltpu.VMEM((N_A, 8, 384), F32),
            pltpu.VMEM((N_A, 8, 384), F32),
            pltpu.VMEM((N_A, 8, 384), F32),
            pltpu.VMEM((N_B, 16, 2 * WAVES), BF16),
            pltpu.VMEM((256, 2 * WAVES), BF16),
            pltpu.VMEM((16, WAVES), F32),
            pltpu.VMEM((16, WAVES), BF16),
            pltpu.VMEM((CYCLES, 2 * WAVES, SLOTS), BF16),
            pltpu.VMEM((CYCLES, 2 * WAVES, POINTS), BF16),
            pltpu.VMEM((GROUPS, 8, SLOTS), F32),
            pltpu.VMEM((GROUPS, 8, SLOTS), F32),
            pltpu.VMEM((ROWS + 2, COLS + 16, HALF), F32),
            pltpu.VMEM((ROWS + 2, COLS + 16, HALF), F32),
            pltpu.VMEM((ROWS, COLS, HALF), F32),
            pltpu.VMEM((2, 2, ROWS, 1, HALF), F32),
            pltpu.VMEM((2, 2, ROWS, 1, HALF), F32),
            pltpu.VMEM((2, COLS, HALF), BF16),
            pltpu.VMEM((2, COLS, HALF), BF16),
            pltpu.VMEM((ROWS * COLS, 128), F32),
            pltpu.VMEM((ROWS * COLS, 128), F32),
            pltpu.VMEM((ROWS * COLS, 128), F32),
            pltpu.VMEM((2, ROWS * COLS, 128), F32),
            pltpu.VMEM((ROWS * COLS, 128), F32),
            pltpu.VMEM((2, N_B, 8, 128), F32),
            pltpu.VMEM((384, 512), BF16),
            pltpu.VMEM((256, 256), BF16),
            dma((6,)), dma((GROUPS,)),
            dma((N_A - 1,)), dma((N_A,)),
            dma((N_A,)), dma((N_A,)),
            dma((N_B - 1,)), dma((N_B,)),
            dma((N_B - 1,)), dma((1,)),
            dma((2, 3)), dma((2, 3)),
            dma((1,)), dma((1,)),
            dma((2 * N_B - 1,)), dma((2, N_B)),
            dma((3,)),
        ],
        compiler_params=pltpu.CompilerParams(
            collective_id=0, has_side_effects=True, vmem_limit_bytes=VMEM
        ),
    )(
        cycle_points, legendre, coefficients.reshape(BLOCK, 2, 4, NT), spectra, sea_mask, wind_column,
        jnp.asarray(bin_table()),
    )
    return pl.pallas_call(
        last,
        out_shape=(winds, waves, jax.ShapeDtypeStruct((CYCLES, SLOTS), F32)),
        in_specs=[hbm] * 5,
        out_specs=(hbm, hbm, vmem),
        scratch_shapes=[
            pltpu.SMEM((32,), jnp.int32),
            pltpu.VMEM((1, CYCLES, 64, SLOTS), BF16),
            pltpu.VMEM((ROWS, COLS, HALF), F32),
            pltpu.VMEM((N_B, 8, 128), F32),
            pltpu.VMEM((CYCLES, SLOTS), jnp.int32),
            dma((8,)), dma((5,)),
        ],
        compiler_params=pltpu.CompilerParams(vmem_limit_bytes=VMEM),
    )(cycle_points, winds_done, waves_done, rough, roughness_source)


def solution(mesh):
    in_specs = (
        P("aa", None, None),
        P("comp", "aa", None, "ba", None),
        P(),
        P("aa", "ba", "comp"),
        P("aa", "ba"),
        P("aa", None),
        P("aa", "ba"),
    )
    out_specs = (P("comp", "aa", None, "ba"), P("aa", "ba", "comp"), P("aa", "ba"))
    return jax.shard_map(
        per_device, mesh=mesh, in_specs=in_specs, out_specs=out_specs, check_vma=False
    )
```

```python
import math

import numpy as np

import jax
import jax.numpy as jnp
from jax import lax
from jax.experimental import pallas as pl
from jax.experimental.pallas import tpu as pltpu
from jax.sharding import PartitionSpec as P

LON = 4096
NDIR = 36
NFREQ = 36
F32 = jnp.float32
BF16 = jnp.bfloat16
MESH = pl.DeviceIdType.MESH

N_A = 8
N_B = 16
N_X = 4
N_Z = 4
WAVES = 640
BLOCK = WAVES // N_A
GROUPS = BLOCK // 8
NT = 1280
CYCLES = 4
SLOTS = LON // N_B
ROWS = 16
COLS = 32
VMEM = 64_000_000
HALF = NDIR * NFREQ // 2
POINTS = 128
FAR = [(2, 3), (2, 2), (1, 3), (3, 3), (2, 1), (1, 2), (3, 2), (0, 3), (1, 1), (3, 1), (2, 0), (0, 2), (1, 0), (3, 0), (0, 1)]
TILES = [(j, min(128, HALF - j)) for j in range(0, HALF, 128)]


def bin_table():
    b = np.arange(NDIR * NFREQ)
    theta = 2 * np.pi * (b // NFREQ + 0.5) / NDIR
    ratio = np.exp(-math.log(1.1) * (b % NFREQ))
    freq = 0.04177 / ratio
    east = 0.45 * ratio * np.cos(theta)
    north = 0.45 * ratio * np.sin(theta)
    q = 2 * np.pi * freq / 9.81
    assert (north[:HALF] > 0).all() and (north[HALF:] < 0).all()
    width = 0.1 * freq * (2 * np.pi / NDIR)
    rows = [
        np.abs(east),
        np.abs(north),
        1.0 - np.abs(east) - np.abs(north),
        np.sign(east),
        np.sign(north),
        10.0 * q * np.cos(theta),
        10.0 * q * np.sin(theta),
        width,
        0.5 * freq / 0.2,
    ]
    rows += [np.zeros_like(freq)] * (16 - len(rows))
    table = np.stack(rows).astype(np.float32)
    return np.stack([table[:, :HALF], table[:, HALF:]])


AE, AN, CC, SE, SN, QE, QN, WB, DF = range(9)


def poly(y2, coefs):
    acc = jnp.full_like(y2, coefs[-1])
    for c in coefs[-2::-1]:
        acc = acc * y2 + c
    return acc


SIN_C = [(-1.0) ** i / math.factorial(2 * i + 1) for i in range(7)]
COS_C = [(-1.0) ** i / math.factorial(2 * i) for i in range(7)]


def turn(mk, count, inv):
    rest = mk - jnp.floor(mk * inv + 0.5) * count
    y = (rest * inv) * math.pi
    y2 = y * y
    s = y * poly(y2, SIN_C)
    c = poly(y2, COS_C)
    return 1.0 - 2.0 * s * s, 2.0 * s * c


def rcopy(src, dst, send, recv, device):
    return pltpu.make_async_remote_copy(
        src_ref=src, dst_ref=dst, send_sem=send, recv_sem=recv, device_id=device, device_id_type=MESH
    )


def lanes(rows, width=128):
    return lax.broadcasted_iota(jnp.int32, (rows, width), 1)


def sublanes(rows, width=128):
    return lax.broadcasted_iota(jnp.int32, (rows, width), 0)


def spread(row, n):
    kept = jnp.where(sublanes(n, n) == lanes(n, n), jnp.broadcast_to(row, (n, n)), 0.0)
    return jnp.broadcast_to(jnp.sum(kept, axis=1, keepdims=True), (n, 128))


def one_hot(mask):
    return mask.astype(F32).astype(BF16)


def dot(x, y, dims=((1,), (0,))):
    return lax.dot_general(x, y, (dims, ((), ())), preferred_element_type=F32)


def kernel(
    cp_hbm, leg_hbm, coef_hbm, spec_hbm, mask_hbm, wc_hbm, cst_hbm,
    gw_out, ws_out, rough_out,
    gw_ref, ws_ref, rough, cp_ref, leg, coef, degrees, spec, mask_in, wc, cst_ref, sall, msg, a2a, a2x, gath, gperm, low_f, l0,
    table, ptable, ca, sa, buf_a, buf_b, d2, edge, edge_in, row_out, row_in,
    mask_b, east_b, north_b, part, part_in, stress, order_in, order_out,
    i_sem, leg_sem, a_send, a_recv, x_send, x_recv, g_send, g_recv, l_send, l_recv, h_send, h_recv,
    c_send, c_recv, r_send, r_recv, o_sem,
):
    s = lax.axis_index("comp")
    a = lax.axis_index("aa")
    b = lax.axis_index("ba")
    x, z = b // N_Z, b % N_Z
    partner = {"comp": 1 - s}

    flips = lambda v: {0: v, 1: v + 1 - 2 * (v % 2), 2: lax.rem(v + 2, 4), 3: 3 - v}
    flip_x, flip_z, flip_y = flips(x), flips(z), flips(a % 4)
    half = a // 4
    peers_a = [(1 - half) * 4 + flip_y[i] for i in (2, 1, 3, 0)] + [half * 4 + flip_y[i] for i in (2, 1, 3)]
    peers_b = [flip_x[i] * N_Z + flip_z[j] for i, j in FAR]

    small = [
        pltpu.make_async_copy(mask_hbm, mask_in, i_sem.at[1]),
        pltpu.make_async_copy(wc_hbm, wc, i_sem.at[2]),
        pltpu.make_async_copy(cst_hbm, cst_ref, i_sem.at[3]),
        pltpu.make_async_copy(spec_hbm, spec, i_sem.at[4]),
        pltpu.make_async_copy(cp_hbm, cp_ref, i_sem.at[5]),
    ]
    coef_copy = pltpu.make_async_copy(coef_hbm, coef, i_sem.at[0])
    coef_copy.start()
    leg_copies = lambda g: pltpu.make_async_copy(
        leg_hbm.at[pl.ds(g * 8, 8)], leg.at[pl.ds(g * 8, 8)], leg_sem.at[g]
    )
    for g in range(GROUPS):
        leg_copies(g).start()
    for c in small:
        c.start()
    barrier = pltpu.get_barrier_semaphore()
    pl.semaphore_signal(barrier, inc=1, device_id=partner, device_id_type=MESH)
    for t in peers_a:
        pl.semaphore_signal(barrier, inc=1, device_id={"aa": t}, device_id_type=MESH)
    for t in peers_b:
        pl.semaphore_signal(barrier, inc=1, device_id={"ba": t}, device_id_type=MESH)
        pl.semaphore_signal(barrier, inc=1, device_id={"comp": 1 - s, "ba": t}, device_id_type=MESH)

    @pl.when(b == 0)
    def _():
        for t in peers_a:
            pl.semaphore_signal(barrier, inc=1, device_id={"comp": 1 - s, "aa": t}, device_id_type=MESH)

    def halo(buf, step):
        up = jnp.where(s == 0, N_A - 2 - a, a - 1)
        down = jnp.where(s == 0, a - 1, N_A - 2 - a)
        return [
            (up >= 0, down >= 0, rcopy(
                row_out.at[step], row_in.at[step],
                h_send.at[step, 0], h_recv.at[step, 0], {"aa": lax.rem(a + 1 + (N_A - 2) * s, N_A)})),
            (b < N_B - 1, b > 0, rcopy(
                edge.at[step, 1], edge_in.at[step, 0],
                h_send.at[step, 1], h_recv.at[step, 1], {"ba": lax.rem(b + 1, N_B)})),
            (b > 0, b < N_B - 1, rcopy(
                edge.at[step, 0], edge_in.at[step, 1],
                h_send.at[step, 2], h_recv.at[step, 2], {"ba": lax.rem(b + N_B - 1, N_B)})),
        ]

    def halo_start(copies, buf, step):
        row_out[step] = buf[ROWS - (ROWS - 1) * s, 8 : 8 + COLS, :].astype(BF16)
        for can, _, c in copies:
            pl.when(can)(c.start)

    def halo_land(copies, buf, step):
        for i, (_, comes, c) in enumerate(copies):
            pl.when(comes)(c.wait_recv)

            @pl.when(jnp.logical_not(comes))
            def _():
                if i == 0:
                    row_in[step] = jnp.zeros((COLS, HALF), BF16)
                else:
                    edge_in[step, i - 1] = jnp.zeros((ROWS, 1, HALF), F32)

        buf[(ROWS + 1) * s, 8 : 8 + COLS, :] = row_in[step].astype(F32)
        for r in range(ROWS):
            buf[r + 1, 7:8, :] = edge_in[step, 0, r]
            buf[r + 1, 8 + COLS : 9 + COLS, :] = edge_in[step, 1, r]

    def halo_sent(copies):
        for can, _, c in copies:
            pl.when(can)(c.wait_send)

    coef_copy.wait()

    def masked(g, carry):
        rows = []
        for i in range(8):
            order = a * BLOCK + g * 8 + i
            block = jnp.concatenate([coef[g * 8 + i, p].astype(F32) for p in range(2)], axis=0)
            rows.append(jnp.where(lanes(8, NT) >= order, block, 0.0))
        degrees[g] = jnp.concatenate(rows, axis=0).astype(BF16)
        return carry

    lax.fori_loop(0, GROUPS, masked, 0)

    def legendre(g, carry):
        leg_copies(g).wait()
        cross = dot(degrees[g], leg[pl.ds(g * 8, 8)].reshape(256, NT), ((1,), (1,)))
        at = pl.ds(pl.multiple_of(g * 8, 8), 8)
        for t in range(2):
            kept = cross[t * 32 : t * 32 + 8, t * 128 : t * 128 + 128]
            for q in range(1, 4):
                m = t * 4 + q
                kept = jnp.where(lanes(8) >= q * 32, cross[m * 8 : m * 8 + 8, t * 128 : t * 128 + 128], kept)
            sall[at, t * 128 : t * 128 + 128] = kept
        return carry

    lax.fori_loop(0, GROUPS, legendre, 0)

    i, o = sublanes(256, 256), lanes(256, 256)
    moved = dot(sall[...].astype(BF16), one_hot(o == (i & 31) // 4 * 32 + (i // 32) * 4 + (i & 3)))
    turned = {}
    for t in range(N_A):
        for q in range(3):
            acc = jnp.zeros((8, 128), F32)
            for g in range(q * 4, min(q * 4 + 4, GROUPS)):
                shift = 32 * ((g - t) % 4)
                key = (g, t // 4, shift)
                if key not in turned:
                    v = moved[g * 8 : g * 8 + 8, t // 4 * 128 : t // 4 * 128 + 128]
                    turned[key] = pltpu.roll(v, shift, axis=1) if shift else v
                at = lanes(8) // 32 == g % 4
                acc = jnp.where(at, turned[key], acc)
            msg[t, :, q * 128 : q * 128 + 128] = acc

    pl.semaphore_wait(barrier, N_A + 2 * N_B - 2 + jnp.where(b == 0, N_A - 1, 0))
    sent = []
    for d, t in enumerate(peers_a):
        c = rcopy(msg.at[t], a2a.at[a], a_send.at[d], a_recv.at[a], {"aa": t})
        c.start()
        sent.append(c)
    crossed = []
    for d, t in enumerate(peers_a + [a]):
        crossed.append(
            rcopy(msg.at[t], a2x.at[a], x_send.at[d], x_recv.at[a], {"comp": 1 - s, "aa": t})
        )

    @pl.when(b == 0)
    def _():
        for c in crossed:
            c.start()

    a2a[a] = msg[a]


    for c in small:
        c.wait()
    sea = mask_in[...].astype(F32)
    for r in range(ROWS):
        mask_b[r * COLS : (r + 1) * COLS, :] = spread(sea[r : r + 1, :], COLS)

    def first(r, carry):
        m = mask_b[pl.ds(r * COLS, COLS), :]
        for j, w in TILES:
            v = spec[r, :, j : j + w] * m[:, :w]
            buf_a[r + 1, 8 : 8 + COLS, j : j + w] = v
            edge[0, 0, r, :, j : j + w] = v[0:1, :]
            edge[0, 1, r, :, j : j + w] = v[COLS - 1 : COLS, :]
        return carry

    lax.fori_loop(0, ROWS, first, 0)

    halo_a = halo(buf_a, 0)
    halo_start(halo_a, buf_a, 0)

    def tables(out, l, k, active):
        w = k.shape[1]
        count = jnp.full((1, w), cp_ref[a * CYCLES + l], jnp.int32).astype(F32)
        inv = 1.0 / count
        cu, su = turn(sublanes(WAVES // 8, w).astype(F32) * 8.0 * k, count, inv)
        ca[:, :, :w] = cu.reshape(GROUPS, 8, w)
        sa[:, :, :w] = su.reshape(GROUPS, 8, w)
        cv, sv = turn(sublanes(8, w).astype(F32) * k, count, inv)
        cv, sv = cv * active, sv * active
        minus_c, minus_s = -cv, -sv

        def block(i, carry):
            for h in range(4):
                cs, ss = [], []
                for o in range(h * 2, h * 2 + 2):
                    c0, s0 = ca[i, o : o + 1, :w], sa[i, o : o + 1, :w]
                    cs.append(c0 * cv + s0 * minus_s)
                    ss.append(s0 * minus_c + c0 * minus_s)
                at = pl.multiple_of(i * 64 + h * 16, 16)
                out[l, pl.ds(at, 16), :] = jnp.concatenate(cs, axis=0).astype(BF16)
                out[l, pl.ds(WAVES + at, 16), :] = jnp.concatenate(ss, axis=0).astype(BF16)
            return carry

        lax.fori_loop(0, GROUPS, block, 0)
        top = out[l, 0:16, :].astype(F32)
        out[l, 0:16, :] = jnp.where(sublanes(16, w) == 0, top * 0.5, top).astype(BF16)

    near = wc[:, pl.ds(pl.multiple_of(b // 4 * 128, 128), 128)].astype(F32)
    near = pltpu.roll(near, (4 - b % 4) % 4 * COLS, axis=1)
    near = jnp.where(lanes(ROWS) < COLS, near, 0.0)
    side = near
    for q in range(1, 4):
        side = jnp.where(sublanes(ROWS) % 4 == q, pltpu.roll(near, q * COLS, axis=1), side)
    for l in range(CYCLES):
        tables(ptable, l, jnp.sum(side[l * 4 : l * 4 + 4, :], axis=0, keepdims=True), 2.0)

    slots = lanes(1, SLOTS) + b * SLOTS
    for l in range(CYCLES):
        active = jnp.where(slots < cp_ref[a * CYCLES + l], 2.0, 0.0)
        tables(table, l, slots.astype(F32), active)

    i, o = sublanes(384, 512), lanes(384, 512)
    order_in[...] = one_hot((o == (i & 3) * 128 + i // 4) & (i < BLOCK * 4))
    r = sublanes(256, 256)
    order_out[...] = one_hot(lanes(256, 256) == (r & 63) // 4 * 16 + r // 64 * 4 + (r & 3))

    def upwind(buf, r, j, w):
        c = lambda i: cst_ref[s, i : i + 1, j : j + w]
        here = buf[r + 1, 8 : 8 + COLS, j : j + w]
        ux = jnp.where(c(SE) > 0.0, buf[r + 1, 7 : 7 + COLS, j : j + w], buf[r + 1, 9 : 9 + COLS, j : j + w])
        uy = buf[r + 2 * s, 8 : 8 + COLS, j : j + w]
        return here * c(CC) + ux * c(AE) + uy * c(AN)

    halo_land(halo_a, buf_a, 0)

    def second(r, carry):
        m = mask_b[pl.ds(r * COLS, COLS), :]
        for j, w in TILES:
            v = upwind(buf_a, r, j, w) * m[:, :w]
            buf_b[r + 1, 8 : 8 + COLS, j : j + w] = v
            edge[1, 0, r, :, j : j + w] = v[0:1, :]
            edge[1, 1, r, :, j : j + w] = v[COLS - 1 : COLS, :]
        return carry

    lax.fori_loop(0, ROWS, second, 0)
    halo_b = halo(buf_b, 1)
    halo_start(halo_b, buf_b, 1)

    def compact(landed):
        wide = dot(landed[...].reshape(64, 384).astype(BF16), order_in[...])
        out = []
        for l in range(CYCLES):
            tiles = [jnp.zeros((8, 128), F32) for _ in range(WAVES // 128)]
            for c in range(N_A):
                t, shift = divmod(c * BLOCK, 128)
                piece = wide[c * 8 : c * 8 + 8, l * 128 : l * 128 + 128]
                if shift:
                    piece = pltpu.roll(piece, shift, axis=1)
                    tiles[t] = jnp.where(lanes(8) >= shift, piece, tiles[t])
                    if shift + BLOCK > 128:
                        tiles[t + 1] = jnp.where(lanes(8) < shift, piece, tiles[t + 1])
                else:
                    tiles[t] = jnp.where(lanes(8) < BLOCK, piece, tiles[t])
            out.append(tiles)
        return out

    def lowest(blocks, base):
        for l in range(CYCLES):
            for t in range(WAVES // 128):
                for p in range(2):
                    r = base + p * 4 + l
                    low_f[r : r + 1, t * 128 : t * 128 + 128] = blocks[l][t][p * 4 : p * 4 + 1, :]

    for d, c in enumerate(peers_a):
        rcopy(msg.at[0], a2a.at[c], a_send.at[d], a_recv.at[c], {"aa": c}).wait_recv()
    blocks = compact(a2a)
    low = [
        rcopy(l0, l0, l_send.at[d], l_recv.at[0], {"ba": t}) for d, t in enumerate(peers_b)
    ]

    @pl.when(b == 0)
    def _():
        lowest(blocks, 0)
        for d, c in enumerate(peers_a + [a]):
            rcopy(msg.at[0], a2x.at[c], x_send.at[d], x_recv.at[c], {"comp": 1 - s, "aa": c}).wait_recv()
        lowest(compact(a2x), 8)
        l0[...] = low_f[...].astype(BF16)
        for c in low:
            c.start()

    for t in range(WAVES // 128):
        up = [pltpu.roll(blocks[l][t], 4, axis=0) for l in range(CYCLES)]
        own = [blocks[l][t] for l in range(CYCLES)]
        top = sublanes(8) < 4
        for p in range(2):
            pair = [
                jnp.where(top, own[l], up[l + 1]) if p == 0 else jnp.where(top, up[l], own[l + 1])
                for l in (0, 2)
            ]
            at = p * WAVES + t * 128
            gath[b, :, at : at + 128] = jnp.concatenate(pair, axis=0).astype(BF16)

    gathers = []

    def give(o, device):
        c = rcopy(gath.at[o], gath.at[o], g_send.at[len(gathers)], g_recv.at[o], {"ba": device})
        c.start()
        gathers.append(c)

    def arrived(o):
        rcopy(gath.at[o], gath.at[o], g_send.at[0], g_recv.at[o], {"ba": o}).wait_recv()

    x_peers = [lax.rem(x + d, N_X) * N_Z + z for d in (1, 3, 2)]
    for d in range(1, N_Z):
        give(b, x * N_Z + lax.rem(z + d, N_Z))
    for t in x_peers:
        give(b, t)

    halo_land(halo_b, buf_b, 1)

    def third(r, carry):
        at = pl.ds(r * COLS, COLS)
        m = mask_b[at, :]
        total = jnp.zeros((COLS, 128), F32)
        for j, w in TILES:
            v = upwind(buf_b, r, j, w) * m[:, :w]
            d2[r, :, j : j + w] = v
            term = v * cst_ref[s, WB : WB + 1, j : j + w]
            if w == 128:
                total = total + term
            else:
                part[0, at, :] = total
                part[0, at, :w] = total[:, :w] + term
        return carry

    lax.fori_loop(0, ROWS, third, 0)
    energy_copy = rcopy(part.at[0], part_in, c_send.at[0], c_recv.at[0], partner)
    energy_copy.start()

    for d in range(1, N_Z):
        o = x * N_Z + lax.rem(z + N_Z - d, N_Z)
        arrived(o)
        for t in x_peers:
            give(o, t)

    @pl.when(b > 0)
    def _():
        low[0].wait_recv()

    own, other = [], []
    for l in range(CYCLES):
        pc = dot(l0[...], ptable[l, 0:WAVES, :])
        ps = dot(l0[...], ptable[l, WAVES:, :])
        own.append((pc[l : l + 1, :] + ps[4 + l : 5 + l, :]).astype(BF16).astype(F32))
        other.append((pc[8 + l : 9 + l, :] + ps[12 + l : 13 + l, :]).astype(BF16).astype(F32))
    east = [jnp.where(s == 0, p, q) for p, q in zip(own, other)]
    north = [jnp.where(s == 0, q, p) for p, q in zip(own, other)]
    for l in range(CYCLES):
        east_b[pl.ds(l * POINTS, POINTS), :] = spread(east[l], POINTS)
        north_b[pl.ds(l * POINTS, POINTS), :] = spread(north[l], POINTS)

    def gain_of(e, n, r, j, w):
        c = lambda i: cst_ref[s, i : i + 1, j : j + w]
        align = e[:, :w] * c(QE) + n[:, :w] * c(QN)
        grown = 0.05 * jnp.maximum(align - 1.0, 0.0) * d2[r, :, j : j + w]
        return align, grown

    def fourth(r, carry):
        at = pl.ds(r * COLS, COLS)
        e, n = east_b[at, :], north_b[at, :]
        total = jnp.zeros((COLS, 128), F32)
        for j, w in TILES:
            align, grown = gain_of(e, n, r, j, w)
            term = grown * align * cst_ref[s, WB : WB + 1, j : j + w]
            if w == 128:
                total = total + term
            else:
                part[1, at, :] = total
                part[1, at, :w] = total[:, :w] + term
        return carry

    lax.fori_loop(0, ROWS, fourth, 0)
    for l in range(CYCLES):
        total = jnp.sum(part[1, pl.ds(l * POINTS, POINTS), :], axis=1, keepdims=True)
        kept = jnp.where(sublanes(POINTS) == lanes(POINTS), jnp.broadcast_to(total, (POINTS, 128)), 0.0)
        row = jnp.sum(kept, axis=0, keepdims=True)
        stress[s, b, l : l + 1, :] = row
        stress[s, b, 4 + l : 5 + l, :] = 0.12 * (east[l] * east[l] + north[l] * north[l]) + 0.02
    band = [(c, t) for t in peers_b for c in (1 - s, s)] + [(1 - s, b)]
    rough_copies = []
    for n, (c, t) in enumerate(band):
        own_block = stress.at[s, b]
        rough_copies.append(
            rcopy(own_block, own_block, r_send.at[n], r_recv.at[s, b], {"comp": c, "ba": t})
        )
        rough_copies[-1].start()

    energy_copy.wait_recv()
    for l in range(CYCLES):
        at = pl.ds(l * POINTS, POINTS)
        level = jnp.sum(part[0, at, :] + part_in[at, :], axis=1, keepdims=True) * 0.125
        mask_b[at, :] = jnp.broadcast_to(level * level, (POINTS, 128))

    def fifth(r, carry):
        at = pl.ds(r * COLS, COLS)
        e, n = east_b[at, :], north_b[at, :]
        square = mask_b[at, :]
        for j, w in TILES:
            _, grown = gain_of(e, n, r, j, w)
            decay = square[:, :w] * cst_ref[s, DF : DF + 1, j : j + w]
            ws_ref[r, :, j : j + w] = (d2[r, :, j : j + w] + grown) / (1.0 + decay)
        return carry

    lax.fori_loop(0, ROWS, fifth, 0)
    ws_copy = pltpu.make_async_copy(ws_ref, ws_out, o_sem.at[0])
    ws_copy.start()

    for xd in range(1, N_X):
        for zd in range(N_Z):
            arrived(lax.rem(x + N_X - xd, N_X) * N_Z + lax.rem(z + zd, N_Z))
    for k in range(0, 2 * WAVES, 256):
        gperm[:, k : k + 256] = dot(order_out[...], gath[:, :, k : k + 256].reshape(256, 256)).astype(BF16)
    for l in range(CYCLES):
        gw_ref[0, l] = dot(gperm[l * 64 : l * 64 + 64, :], table[l]).astype(BF16)
    gw_copy = pltpu.make_async_copy(gw_ref, gw_out, o_sem.at[1])
    gw_copy.start()

    for n, (c, t) in enumerate(band):
        rcopy(stress.at[c, t], stress.at[c, t], r_send.at[n], r_recv.at[c, t], {"comp": c, "ba": t}).wait_recv()
    total = stress[0, :, 0:4, :] + stress[1, :, 0:4, :]
    rough[:, 0:4, :] = jnp.sqrt(1.0 + 0.03 * total / stress[0, :, 4:8, :])
    rough[:, 4:8, :] = jnp.zeros((N_B, 4, 128), F32)
    rough_copy = pltpu.make_async_copy(rough, rough_out, o_sem.at[2])
    rough_copy.start()
    for c in sent + gathers + rough_copies + [energy_copy]:
        c.wait_send()
    halo_sent(halo_a)
    halo_sent(halo_b)

    @pl.when(b == 0)
    def _():
        for c in low + crossed:
            c.wait_send()

    for c in (ws_copy, gw_copy, rough_copy):
        c.wait()


def last(
    cp_hbm, gw_in, ws_in, rough_in, rs_hbm, gw_ref, ws_ref, ch_ref, cp_ref, gw, ws, rough, rs_ref, sem_in, sem_out
):
    a = lax.axis_index("aa")
    slots = lanes(1, SLOTS) + lax.axis_index("ba") * SLOTS
    step = ROWS // 4
    blocks = [pl.ds(i * step, step) for i in range(4)]
    come = [pltpu.make_async_copy(ws_in.at[k], ws.at[k], sem_in.at[i]) for i, k in enumerate(blocks)]
    come.append(pltpu.make_async_copy(gw_in, gw, sem_in.at[4]))
    go = [pltpu.make_async_copy(ws.at[k], ws_ref.at[k], sem_out.at[i]) for i, k in enumerate(blocks)]
    go.append(pltpu.make_async_copy(gw, gw_ref, sem_out.at[4]))
    other = [
        pltpu.make_async_copy(rough_in, rough, sem_in.at[5]),
        pltpu.make_async_copy(rs_hbm, rs_ref, sem_in.at[6]),
        pltpu.make_async_copy(cp_hbm, cp_ref, sem_in.at[7]),
    ]
    for c in other + come:
        c.start()
    for c, d in zip(come, go):
        c.wait()
        d.start()
    for c in other:
        c.wait()
    for l in range(CYCLES):
        source = rs_ref[l : l + 1, :]
        low_part = ((source >> 9) & 3) * 32 + (source & 31)
        high_part = (source >> 5) & 15
        pick = one_hot(sublanes(128, SLOTS) == low_part)
        values = rough[:, l, :]
        h0 = values.astype(BF16)
        r1 = values - h0.astype(F32)
        h1 = r1.astype(BF16)
        h2 = (r1 - h1.astype(F32)).astype(BF16)
        got = dot(h0, pick) + (dot(h1, pick) + dot(h2, pick))
        keep = sublanes(N_B, SLOTS) == high_part
        row = jnp.sum(jnp.where(keep, got, 0.0), axis=0, keepdims=True)
        ch_ref[l : l + 1, :] = jnp.where(slots < cp_ref[a * CYCLES + l], row, 0.0)
    for c in go:
        c.wait()


def per_device(legendre, coefficients, cycle_points, spectra, sea_mask, wind_column, roughness_source):
    vmem = pl.BlockSpec(memory_space=pltpu.VMEM)
    smem = pl.BlockSpec(memory_space=pltpu.SMEM)
    hbm = pl.BlockSpec(memory_space=pltpu.HBM)
    dma = pltpu.SemaphoreType.DMA
    winds = jax.ShapeDtypeStruct((1, CYCLES, 64, SLOTS), BF16)
    waves = jax.ShapeDtypeStruct((ROWS, COLS, HALF), F32)
    winds_done, waves_done, rough = pl.pallas_call(
        kernel,
        out_shape=(winds, waves, jax.ShapeDtypeStruct((N_B, 8, 128), F32)),
        in_specs=[hbm] * 7,
        out_specs=(hbm, hbm, hbm),
        scratch_shapes=[
            pltpu.VMEM((1, CYCLES, 64, SLOTS), BF16),
            pltpu.VMEM((ROWS, COLS, HALF), F32),
            pltpu.VMEM((N_B, 8, 128), F32),
            pltpu.SMEM((32,), jnp.int32),
            pltpu.VMEM((BLOCK, 32, NT), BF16),
            pltpu.VMEM((BLOCK, 2, 4, NT), BF16),
            pltpu.VMEM((GROUPS, 64, NT), BF16),
            pltpu.VMEM((ROWS, COLS, HALF), F32),
            pltpu.VMEM((ROWS, COLS), jnp.int32),
            pltpu.VMEM((ROWS, 512), jnp.int32),
            pltpu.VMEM((2, 16, HALF), F32),
            pltpu.VMEM((BLOCK, 256), F32),
            pltpu.VMEM((N_A, 8, 384), F32),
            pltpu.VMEM((N_A, 8, 384), F32),
            pltpu.VMEM((N_A, 8, 384), F32),
            pltpu.VMEM((N_B, 16, 2 * WAVES), BF16),
            pltpu.VMEM((256, 2 * WAVES), BF16),
            pltpu.VMEM((16, WAVES), F32),
            pltpu.VMEM((16, WAVES), BF16),
            pltpu.VMEM((CYCLES, 2 * WAVES, SLOTS), BF16),
            pltpu.VMEM((CYCLES, 2 * WAVES, POINTS), BF16),
            pltpu.VMEM((GROUPS, 8, SLOTS), F32),
            pltpu.VMEM((GROUPS, 8, SLOTS), F32),
            pltpu.VMEM((ROWS + 2, COLS + 16, HALF), F32),
            pltpu.VMEM((ROWS + 2, COLS + 16, HALF), F32),
            pltpu.VMEM((ROWS, COLS, HALF), F32),
            pltpu.VMEM((2, 2, ROWS, 1, HALF), F32),
            pltpu.VMEM((2, 2, ROWS, 1, HALF), F32),
            pltpu.VMEM((2, COLS, HALF), BF16),
            pltpu.VMEM((2, COLS, HALF), BF16),
            pltpu.VMEM((ROWS * COLS, 128), F32),
            pltpu.VMEM((ROWS * COLS, 128), F32),
            pltpu.VMEM((ROWS * COLS, 128), F32),
            pltpu.VMEM((2, ROWS * COLS, 128), F32),
            pltpu.VMEM((ROWS * COLS, 128), F32),
            pltpu.VMEM((2, N_B, 8, 128), F32),
            pltpu.VMEM((384, 512), BF16),
            pltpu.VMEM((256, 256), BF16),
            dma((6,)), dma((GROUPS,)),
            dma((N_A - 1,)), dma((N_A,)),
            dma((N_A,)), dma((N_A,)),
            dma((N_B - 1,)), dma((N_B,)),
            dma((N_B - 1,)), dma((1,)),
            dma((2, 3)), dma((2, 3)),
            dma((1,)), dma((1,)),
            dma((2 * N_B - 1,)), dma((2, N_B)),
            dma((3,)),
        ],
        compiler_params=pltpu.CompilerParams(
            collective_id=0, has_side_effects=True, vmem_limit_bytes=VMEM
        ),
    )(
        cycle_points, legendre, coefficients.reshape(BLOCK, 2, 4, NT), spectra, sea_mask, wind_column,
        jnp.asarray(bin_table()),
    )
    return pl.pallas_call(
        last,
        out_shape=(winds, waves, jax.ShapeDtypeStruct((CYCLES, SLOTS), F32)),
        in_specs=[hbm] * 5,
        out_specs=(hbm, hbm, vmem),
        scratch_shapes=[
            pltpu.SMEM((32,), jnp.int32),
            pltpu.VMEM((1, CYCLES, 64, SLOTS), BF16),
            pltpu.VMEM((ROWS, COLS, HALF), F32),
            pltpu.VMEM((N_B, 8, 128), F32),
            pltpu.VMEM((CYCLES, SLOTS), jnp.int32),
            dma((8,)), dma((5,)),
        ],
        compiler_params=pltpu.CompilerParams(vmem_limit_bytes=VMEM),
    )(cycle_points, winds_done, waves_done, rough, roughness_source)


def solution(mesh):
    in_specs = (
        P("aa", None, None),
        P("comp", "aa", None, "ba", None),
        P(),
        P("aa", "ba", "comp"),
        P("aa", "ba"),
        P("aa", None),
        P("aa", "ba"),
    )
    out_specs = (P("comp", "aa", None, "ba"), P("aa", "ba", "comp"), P("aa", "ba"))
    return jax.shard_map(
        per_device, mesh=mesh, in_specs=in_specs, out_specs=out_specs, check_vma=False
    )
```

```python
import math

import numpy as np

import jax
import jax.numpy as jnp
from jax import lax
from jax.experimental import pallas as pl
from jax.experimental.pallas import tpu as pltpu
from jax.sharding import PartitionSpec as P

LON = 4096
NDIR = 36
NFREQ = 36
F32 = jnp.float32
BF16 = jnp.bfloat16
MESH = pl.DeviceIdType.MESH

N_A = 8
N_B = 16
N_X = 4
N_Z = 4
WAVES = 640
BLOCK = WAVES // N_A
GROUPS = BLOCK // 8
NT = 1280
CYCLES = 4
SLOTS = LON // N_B
ROWS = 16
COLS = 32
VMEM = 64_000_000
HALF = NDIR * NFREQ // 2
POINTS = 128
FAR = [(2, 3), (2, 2), (1, 3), (3, 3), (2, 1), (1, 2), (3, 2), (0, 3), (1, 1), (3, 1), (2, 0), (0, 2), (1, 0), (3, 0), (0, 1)]
TILES = [(j, min(128, HALF - j)) for j in range(0, HALF, 128)]


def bin_table():
    b = np.arange(NDIR * NFREQ)
    theta = 2 * np.pi * (b // NFREQ + 0.5) / NDIR
    ratio = np.exp(-math.log(1.1) * (b % NFREQ))
    freq = 0.04177 / ratio
    east = 0.45 * ratio * np.cos(theta)
    north = 0.45 * ratio * np.sin(theta)
    q = 2 * np.pi * freq / 9.81
    assert (north[:HALF] > 0).all() and (north[HALF:] < 0).all()
    width = 0.1 * freq * (2 * np.pi / NDIR)
    rows = [
        np.abs(east),
        np.abs(north),
        1.0 - np.abs(east) - np.abs(north),
        np.sign(east),
        np.sign(north),
        10.0 * q * np.cos(theta),
        10.0 * q * np.sin(theta),
        width,
        0.5 * freq / 0.2,
    ]
    rows += [np.zeros_like(freq)] * (16 - len(rows))
    table = np.stack(rows).astype(np.float32)
    return np.stack([table[:, :HALF], table[:, HALF:]])


AE, AN, CC, SE, SN, QE, QN, WB, DF = range(9)


def poly(y2, coefs):
    acc = jnp.full_like(y2, coefs[-1])
    for c in coefs[-2::-1]:
        acc = acc * y2 + c
    return acc


SIN_C = [(-1.0) ** i / math.factorial(2 * i + 1) for i in range(7)]
COS_C = [(-1.0) ** i / math.factorial(2 * i) for i in range(7)]


def turn(mk, count, inv):
    rest = mk - jnp.floor(mk * inv + 0.5) * count
    y = (rest * inv) * math.pi
    y2 = y * y
    s = y * poly(y2, SIN_C)
    c = poly(y2, COS_C)
    return 1.0 - 2.0 * s * s, 2.0 * s * c


def rcopy(src, dst, send, recv, device):
    return pltpu.make_async_remote_copy(
        src_ref=src, dst_ref=dst, send_sem=send, recv_sem=recv, device_id=device, device_id_type=MESH
    )


def lanes(rows, width=128):
    return lax.broadcasted_iota(jnp.int32, (rows, width), 1)


def sublanes(rows, width=128):
    return lax.broadcasted_iota(jnp.int32, (rows, width), 0)


def spread(row, n):
    kept = jnp.where(sublanes(n, n) == lanes(n, n), jnp.broadcast_to(row, (n, n)), 0.0)
    return jnp.broadcast_to(jnp.sum(kept, axis=1, keepdims=True), (n, 128))


def one_hot(mask):
    return mask.astype(F32).astype(BF16)


def dot(x, y, dims=((1,), (0,))):
    return lax.dot_general(x, y, (dims, ((), ())), preferred_element_type=F32)


def kernel(
    cp_hbm, leg_hbm, coef_hbm, spec_hbm, mask_hbm, wc_hbm, cst_hbm,
    gw_out, ws_out, rough_out,
    gw_ref, ws_ref, rough, cp_ref, leg, coef, degrees, spec, mask_in, wc, cst_ref, sall, msg, a2a, a2x, gath, gperm, low_f, l0,
    table, ptable, ca, sa, buf_a, buf_b, d2, edge, edge_in, row_out, row_in,
    mask_b, east_b, north_b, part, part_in, stress, order_in, order_out,
    i_sem, leg_sem, a_send, a_recv, x_send, x_recv, g_send, g_recv, l_send, l_recv, h_send, h_recv,
    c_send, c_recv, r_send, r_recv, o_sem,
):
    s = lax.axis_index("comp")
    a = lax.axis_index("aa")
    b = lax.axis_index("ba")
    x, z = b // N_Z, b % N_Z
    partner = {"comp": 1 - s}

    flips = lambda v: {0: v, 1: v + 1 - 2 * (v % 2), 2: lax.rem(v + 2, 4), 3: 3 - v}
    flip_x, flip_z, flip_y = flips(x), flips(z), flips(a % 4)
    half = a // 4
    peers_a = [(1 - half) * 4 + flip_y[i] for i in (2, 1, 3, 0)] + [half * 4 + flip_y[i] for i in (2, 1, 3)]
    peers_b = [flip_x[i] * N_Z + flip_z[j] for i, j in FAR]

    small = [
        pltpu.make_async_copy(mask_hbm, mask_in, i_sem.at[1]),
        pltpu.make_async_copy(wc_hbm, wc, i_sem.at[2]),
        pltpu.make_async_copy(cst_hbm, cst_ref, i_sem.at[3]),
        pltpu.make_async_copy(spec_hbm, spec, i_sem.at[4]),
        pltpu.make_async_copy(cp_hbm, cp_ref, i_sem.at[5]),
    ]
    coef_copy = pltpu.make_async_copy(coef_hbm, coef, i_sem.at[0])
    coef_copy.start()
    leg_copies = lambda g: pltpu.make_async_copy(
        leg_hbm.at[pl.ds(g * 8, 8)], leg.at[pl.ds(g * 8, 8)], leg_sem.at[g]
    )
    for g in range(GROUPS):
        leg_copies(g).start()
    for c in small:
        c.start()
    barrier = pltpu.get_barrier_semaphore()
    pl.semaphore_signal(barrier, inc=1, device_id=partner, device_id_type=MESH)
    for t in peers_a:
        pl.semaphore_signal(barrier, inc=1, device_id={"aa": t}, device_id_type=MESH)
    for t in peers_b:
        pl.semaphore_signal(barrier, inc=1, device_id={"ba": t}, device_id_type=MESH)
        pl.semaphore_signal(barrier, inc=1, device_id={"comp": 1 - s, "ba": t}, device_id_type=MESH)

    @pl.when(b == 0)
    def _():
        for t in peers_a:
            pl.semaphore_signal(barrier, inc=1, device_id={"comp": 1 - s, "aa": t}, device_id_type=MESH)

    def halo(buf, step):
        up = jnp.where(s == 0, N_A - 2 - a, a - 1)
        down = jnp.where(s == 0, a - 1, N_A - 2 - a)
        return [
            (up >= 0, down >= 0, rcopy(
                row_out.at[step], row_in.at[step],
                h_send.at[step, 0], h_recv.at[step, 0], {"aa": lax.rem(a + 1 + (N_A - 2) * s, N_A)})),
            (b < N_B - 1, b > 0, rcopy(
                edge.at[step, 1], edge_in.at[step, 0],
                h_send.at[step, 1], h_recv.at[step, 1], {"ba": lax.rem(b + 1, N_B)})),
            (b > 0, b < N_B - 1, rcopy(
                edge.at[step, 0], edge_in.at[step, 1],
                h_send.at[step, 2], h_recv.at[step, 2], {"ba": lax.rem(b + N_B - 1, N_B)})),
        ]

    def halo_start(copies, buf, step):
        row_out[step] = buf[ROWS - (ROWS - 1) * s, 8 : 8 + COLS, :].astype(BF16)
        for can, _, c in copies:
            pl.when(can)(c.start)

    def halo_land(copies, buf, step):
        for i, (_, comes, c) in enumerate(copies):
            pl.when(comes)(c.wait_recv)

            @pl.when(jnp.logical_not(comes))
            def _():
                if i == 0:
                    row_in[step] = jnp.zeros((COLS, HALF), BF16)
                else:
                    edge_in[step, i - 1] = jnp.zeros((ROWS, 1, HALF), F32)

        buf[(ROWS + 1) * s, 8 : 8 + COLS, :] = row_in[step].astype(F32)
        for r in range(ROWS):
            buf[r + 1, 7:8, :] = edge_in[step, 0, r]
            buf[r + 1, 8 + COLS : 9 + COLS, :] = edge_in[step, 1, r]

    def halo_sent(copies):
        for can, _, c in copies:
            pl.when(can)(c.wait_send)

    coef_copy.wait()

    def masked(g, carry):
        rows = []
        for i in range(8):
            order = a * BLOCK + g * 8 + i
            block = jnp.concatenate([coef[g * 8 + i, p].astype(F32) for p in range(2)], axis=0)
            rows.append(jnp.where(lanes(8, NT) >= order, block, 0.0))
        degrees[g] = jnp.concatenate(rows, axis=0).astype(BF16)
        return carry

    lax.fori_loop(0, GROUPS, masked, 0)

    def legendre(g, carry):
        leg_copies(g).wait()
        cross = dot(degrees[g], leg[pl.ds(g * 8, 8)].reshape(256, NT), ((1,), (1,)))
        at = pl.ds(pl.multiple_of(g * 8, 8), 8)
        for t in range(2):
            kept = cross[t * 32 : t * 32 + 8, t * 128 : t * 128 + 128]
            for q in range(1, 4):
                m = t * 4 + q
                kept = jnp.where(lanes(8) >= q * 32, cross[m * 8 : m * 8 + 8, t * 128 : t * 128 + 128], kept)
            sall[at, t * 128 : t * 128 + 128] = kept
        return carry

    lax.fori_loop(0, GROUPS, legendre, 0)

    i, o = sublanes(256, 256), lanes(256, 256)
    moved = dot(sall[...].astype(BF16), one_hot(o == (i & 31) // 4 * 32 + (i // 32) * 4 + (i & 3)))
    turned = {}
    for t in range(N_A):
        for q in range(3):
            acc = jnp.zeros((8, 128), F32)
            for g in range(q * 4, min(q * 4 + 4, GROUPS)):
                shift = 32 * ((g - t) % 4)
                key = (g, t // 4, shift)
                if key not in turned:
                    v = moved[g * 8 : g * 8 + 8, t // 4 * 128 : t // 4 * 128 + 128]
                    turned[key] = pltpu.roll(v, shift, axis=1) if shift else v
                at = lanes(8) // 32 == g % 4
                acc = jnp.where(at, turned[key], acc)
            msg[t, :, q * 128 : q * 128 + 128] = acc

    pl.semaphore_wait(barrier, N_A + 2 * N_B - 2 + jnp.where(b == 0, N_A - 1, 0))
    sent = []
    for d, t in enumerate(peers_a):
        c = rcopy(msg.at[t], a2a.at[a], a_send.at[d], a_recv.at[a], {"aa": t})
        c.start()
        sent.append(c)
    crossed = []
    for d, t in enumerate(peers_a + [a]):
        crossed.append(
            rcopy(msg.at[t], a2x.at[a], x_send.at[d], x_recv.at[a], {"comp": 1 - s, "aa": t})
        )

    @pl.when(b == 0)
    def _():
        for c in crossed:
            c.start()

    a2a[a] = msg[a]


    for c in small:
        c.wait()
    sea = mask_in[...].astype(F32)
    for r in range(ROWS):
        mask_b[r * COLS : (r + 1) * COLS, :] = spread(sea[r : r + 1, :], COLS)

    def first(r, carry):
        m = mask_b[pl.ds(r * COLS, COLS), :]
        for j, w in TILES:
            v = spec[r, :, j : j + w] * m[:, :w]
            buf_a[r + 1, 8 : 8 + COLS, j : j + w] = v
            edge[0, 0, r, :, j : j + w] = v[0:1, :]
            edge[0, 1, r, :, j : j + w] = v[COLS - 1 : COLS, :]
        return carry

    lax.fori_loop(0, ROWS, first, 0)

    halo_a = halo(buf_a, 0)
    halo_start(halo_a, buf_a, 0)

    def tables(out, l, k, active):
        w = k.shape[1]
        count = jnp.full((1, w), cp_ref[a * CYCLES + l], jnp.int32).astype(F32)
        inv = 1.0 / count
        cu, su = turn(sublanes(WAVES // 8, w).astype(F32) * 8.0 * k, count, inv)
        ca[:, :, :w] = cu.reshape(GROUPS, 8, w)
        sa[:, :, :w] = su.reshape(GROUPS, 8, w)
        cv, sv = turn(sublanes(8, w).astype(F32) * k, count, inv)
        cv, sv = cv * active, sv * active
        minus_c, minus_s = -cv, -sv

        def block(i, carry):
            for h in range(4):
                cs, ss = [], []
                for o in range(h * 2, h * 2 + 2):
                    c0, s0 = ca[i, o : o + 1, :w], sa[i, o : o + 1, :w]
                    cs.append(c0 * cv + s0 * minus_s)
                    ss.append(s0 * minus_c + c0 * minus_s)
                at = pl.multiple_of(i * 64 + h * 16, 16)
                out[l, pl.ds(at, 16), :] = jnp.concatenate(cs, axis=0).astype(BF16)
                out[l, pl.ds(WAVES + at, 16), :] = jnp.concatenate(ss, axis=0).astype(BF16)
            return carry

        lax.fori_loop(0, GROUPS, block, 0)
        top = out[l, 0:16, :].astype(F32)
        out[l, 0:16, :] = jnp.where(sublanes(16, w) == 0, top * 0.5, top).astype(BF16)

    near = wc[:, pl.ds(pl.multiple_of(b // 4 * 128, 128), 128)].astype(F32)
    near = pltpu.roll(near, (4 - b % 4) % 4 * COLS, axis=1)
    near = jnp.where(lanes(ROWS) < COLS, near, 0.0)
    side = near
    for q in range(1, 4):
        side = jnp.where(sublanes(ROWS) % 4 == q, pltpu.roll(near, q * COLS, axis=1), side)
    for l in range(CYCLES):
        tables(ptable, l, jnp.sum(side[l * 4 : l * 4 + 4, :], axis=0, keepdims=True), 2.0)

    slots = lanes(1, SLOTS) + b * SLOTS
    for l in range(CYCLES):
        active = jnp.where(slots < cp_ref[a * CYCLES + l], 2.0, 0.0)
        tables(table, l, slots.astype(F32), active)

    i, o = sublanes(384, 512), lanes(384, 512)
    order_in[...] = one_hot((o == (i & 3) * 128 + i // 4) & (i < BLOCK * 4))
    r = sublanes(256, 256)
    order_out[...] = one_hot(lanes(256, 256) == (r & 63) // 4 * 16 + r // 64 * 4 + (r & 3))

    def upwind(buf, r, j, w):
        c = lambda i: cst_ref[s, i : i + 1, j : j + w]
        here = buf[r + 1, 8 : 8 + COLS, j : j + w]
        ux = jnp.where(c(SE) > 0.0, buf[r + 1, 7 : 7 + COLS, j : j + w], buf[r + 1, 9 : 9 + COLS, j : j + w])
        uy = buf[r + 2 * s, 8 : 8 + COLS, j : j + w]
        return here * c(CC) + ux * c(AE) + uy * c(AN)

    halo_land(halo_a, buf_a, 0)

    def second(r, carry):
        m = mask_b[pl.ds(r * COLS, COLS), :]
        for j, w in TILES:
            v = upwind(buf_a, r, j, w) * m[:, :w]
            buf_b[r + 1, 8 : 8 + COLS, j : j + w] = v
            edge[1, 0, r, :, j : j + w] = v[0:1, :]
            edge[1, 1, r, :, j : j + w] = v[COLS - 1 : COLS, :]
        return carry

    lax.fori_loop(0, ROWS, second, 0)
    halo_b = halo(buf_b, 1)
    halo_start(halo_b, buf_b, 1)

    def compact(landed):
        wide = dot(landed[...].reshape(64, 384).astype(BF16), order_in[...])
        out = []
        for l in range(CYCLES):
            tiles = [jnp.zeros((8, 128), F32) for _ in range(WAVES // 128)]
            for c in range(N_A):
                t, shift = divmod(c * BLOCK, 128)
                piece = wide[c * 8 : c * 8 + 8, l * 128 : l * 128 + 128]
                if shift:
                    piece = pltpu.roll(piece, shift, axis=1)
                    tiles[t] = jnp.where(lanes(8) >= shift, piece, tiles[t])
                    if shift + BLOCK > 128:
                        tiles[t + 1] = jnp.where(lanes(8) < shift, piece, tiles[t + 1])
                else:
                    tiles[t] = jnp.where(lanes(8) < BLOCK, piece, tiles[t])
            out.append(tiles)
        return out

    def lowest(blocks, base):
        for l in range(CYCLES):
            for t in range(WAVES // 128):
                for p in range(2):
                    r = base + p * 4 + l
                    low_f[r : r + 1, t * 128 : t * 128 + 128] = blocks[l][t][p * 4 : p * 4 + 1, :]

    for d, c in enumerate(peers_a):
        rcopy(msg.at[0], a2a.at[c], a_send.at[d], a_recv.at[c], {"aa": c}).wait_recv()
    blocks = compact(a2a)
    low = [
        rcopy(l0, l0, l_send.at[d], l_recv.at[0], {"ba": t}) for d, t in enumerate(peers_b)
    ]

    @pl.when(b == 0)
    def _():
        lowest(blocks, 0)
        for d, c in enumerate(peers_a + [a]):
            rcopy(msg.at[0], a2x.at[c], x_send.at[d], x_recv.at[c], {"comp": 1 - s, "aa": c}).wait_recv()
        lowest(compact(a2x), 8)
        l0[...] = low_f[...].astype(BF16)
        for c in low:
            c.start()

    for t in range(WAVES // 128):
        up = [pltpu.roll(blocks[l][t], 4, axis=0) for l in range(CYCLES)]
        own = [blocks[l][t] for l in range(CYCLES)]
        top = sublanes(8) < 4
        for p in range(2):
            pair = [
                jnp.where(top, own[l], up[l + 1]) if p == 0 else jnp.where(top, up[l], own[l + 1])
                for l in (0, 2)
            ]
            at = p * WAVES + t * 128
            gath[b, :, at : at + 128] = jnp.concatenate(pair, axis=0).astype(BF16)

    gathers = []

    def give(o, device):
        c = rcopy(gath.at[o], gath.at[o], g_send.at[len(gathers)], g_recv.at[o], {"ba": device})
        c.start()
        gathers.append(c)

    def arrived(o):
        rcopy(gath.at[o], gath.at[o], g_send.at[0], g_recv.at[o], {"ba": o}).wait_recv()

    x_peers = [lax.rem(x + d, N_X) * N_Z + z for d in (1, 3, 2)]
    for d in range(1, N_Z):
        give(b, x * N_Z + lax.rem(z + d, N_Z))
    for t in x_peers:
        give(b, t)

    halo_land(halo_b, buf_b, 1)

    def third(r, carry):
        at = pl.ds(r * COLS, COLS)
        m = mask_b[at, :]
        total = jnp.zeros((COLS, 128), F32)
        for j, w in TILES:
            v = upwind(buf_b, r, j, w) * m[:, :w]
            d2[r, :, j : j + w] = v
            term = v * cst_ref[s, WB : WB + 1, j : j + w]
            if w == 128:
                total = total + term
            else:
                part[0, at, :] = total
                part[0, at, :w] = total[:, :w] + term
        return carry

    lax.fori_loop(0, ROWS, third, 0)
    energy_copy = rcopy(part.at[0], part_in, c_send.at[0], c_recv.at[0], partner)
    energy_copy.start()

    z_peers = [x * N_Z + lax.rem(z + d, N_Z) for d in range(1, N_Z)]
    across = lax.rem(x + 2, N_X)
    for n, o in enumerate(z_peers):
        arrived(o)
        for t in x_peers[:2]:
            give(o, t)
        if n == 0:
            arrived(across * N_Z + z)
            for t in z_peers:
                give(across * N_Z + z, t)

    @pl.when(b > 0)
    def _():
        low[0].wait_recv()

    own, other = [], []
    for l in range(CYCLES):
        pc = dot(l0[...], ptable[l, 0:WAVES, :])
        ps = dot(l0[...], ptable[l, WAVES:, :])
        own.append((pc[l : l + 1, :] + ps[4 + l : 5 + l, :]).astype(BF16).astype(F32))
        other.append((pc[8 + l : 9 + l, :] + ps[12 + l : 13 + l, :]).astype(BF16).astype(F32))
    east = [jnp.where(s == 0, p, q) for p, q in zip(own, other)]
    north = [jnp.where(s == 0, q, p) for p, q in zip(own, other)]
    for l in range(CYCLES):
        east_b[pl.ds(l * POINTS, POINTS), :] = spread(east[l], POINTS)
        north_b[pl.ds(l * POINTS, POINTS), :] = spread(north[l], POINTS)

    def gain_of(e, n, r, j, w):
        c = lambda i: cst_ref[s, i : i + 1, j : j + w]
        align = e[:, :w] * c(QE) + n[:, :w] * c(QN)
        grown = 0.05 * jnp.maximum(align - 1.0, 0.0) * d2[r, :, j : j + w]
        return align, grown

    def fourth(r, carry):
        at = pl.ds(r * COLS, COLS)
        e, n = east_b[at, :], north_b[at, :]
        total = jnp.zeros((COLS, 128), F32)
        for j, w in TILES:
            align, grown = gain_of(e, n, r, j, w)
            term = grown * align * cst_ref[s, WB : WB + 1, j : j + w]
            if w == 128:
                total = total + term
            else:
                part[1, at, :] = total
                part[1, at, :w] = total[:, :w] + term
        return carry

    lax.fori_loop(0, ROWS, fourth, 0)
    for l in range(CYCLES):
        total = jnp.sum(part[1, pl.ds(l * POINTS, POINTS), :], axis=1, keepdims=True)
        kept = jnp.where(sublanes(POINTS) == lanes(POINTS), jnp.broadcast_to(total, (POINTS, 128)), 0.0)
        row = jnp.sum(kept, axis=0, keepdims=True)
        stress[s, b, l : l + 1, :] = row
        stress[s, b, 4 + l : 5 + l, :] = 0.12 * (east[l] * east[l] + north[l] * north[l]) + 0.02
    band = [(c, t) for t in peers_b for c in (1 - s, s)] + [(1 - s, b)]
    rough_copies = []
    for n, (c, t) in enumerate(band):
        own_block = stress.at[s, b]
        rough_copies.append(
            rcopy(own_block, own_block, r_send.at[n], r_recv.at[s, b], {"comp": c, "ba": t})
        )
        rough_copies[-1].start()

    energy_copy.wait_recv()
    for l in range(CYCLES):
        at = pl.ds(l * POINTS, POINTS)
        level = jnp.sum(part[0, at, :] + part_in[at, :], axis=1, keepdims=True) * 0.125
        mask_b[at, :] = jnp.broadcast_to(level * level, (POINTS, 128))

    def fifth(r, carry):
        at = pl.ds(r * COLS, COLS)
        e, n = east_b[at, :], north_b[at, :]
        square = mask_b[at, :]
        for j, w in TILES:
            _, grown = gain_of(e, n, r, j, w)
            decay = square[:, :w] * cst_ref[s, DF : DF + 1, j : j + w]
            ws_ref[r, :, j : j + w] = (d2[r, :, j : j + w] + grown) / (1.0 + decay)
        return carry

    lax.fori_loop(0, ROWS, fifth, 0)
    ws_copy = pltpu.make_async_copy(ws_ref, ws_out, o_sem.at[0])
    ws_copy.start()

    for xd in (1, 3, 2):
        for zd in range(N_Z):
            if (xd, zd) != (2, 0):
                arrived(lax.rem(x + xd, N_X) * N_Z + lax.rem(z + zd, N_Z))
    for k in range(0, 2 * WAVES, 256):
        gperm[:, k : k + 256] = dot(order_out[...], gath[:, :, k : k + 256].reshape(256, 256)).astype(BF16)
    for l in range(CYCLES):
        gw_ref[0, l] = dot(gperm[l * 64 : l * 64 + 64, :], table[l]).astype(BF16)
    gw_copy = pltpu.make_async_copy(gw_ref, gw_out, o_sem.at[1])
    gw_copy.start()

    for n, (c, t) in enumerate(band):
        rcopy(stress.at[c, t], stress.at[c, t], r_send.at[n], r_recv.at[c, t], {"comp": c, "ba": t}).wait_recv()
    total = stress[0, :, 0:4, :] + stress[1, :, 0:4, :]
    rough[:, 0:4, :] = jnp.sqrt(1.0 + 0.03 * total / stress[0, :, 4:8, :])
    rough[:, 4:8, :] = jnp.zeros((N_B, 4, 128), F32)
    rough_copy = pltpu.make_async_copy(rough, rough_out, o_sem.at[2])
    rough_copy.start()
    for c in sent + gathers + rough_copies + [energy_copy]:
        c.wait_send()
    halo_sent(halo_a)
    halo_sent(halo_b)

    @pl.when(b == 0)
    def _():
        for c in low + crossed:
            c.wait_send()

    for c in (ws_copy, gw_copy, rough_copy):
        c.wait()


def last(
    cp_hbm, gw_in, ws_in, rough_in, rs_hbm, gw_ref, ws_ref, ch_ref, cp_ref, gw, ws, rough, rs_ref, sem_in, sem_out
):
    a = lax.axis_index("aa")
    slots = lanes(1, SLOTS) + lax.axis_index("ba") * SLOTS
    step = ROWS // 4
    blocks = [pl.ds(i * step, step) for i in range(4)]
    come = [pltpu.make_async_copy(ws_in.at[k], ws.at[k], sem_in.at[i]) for i, k in enumerate(blocks)]
    come.append(pltpu.make_async_copy(gw_in, gw, sem_in.at[4]))
    go = [pltpu.make_async_copy(ws.at[k], ws_ref.at[k], sem_out.at[i]) for i, k in enumerate(blocks)]
    go.append(pltpu.make_async_copy(gw, gw_ref, sem_out.at[4]))
    other = [
        pltpu.make_async_copy(rough_in, rough, sem_in.at[5]),
        pltpu.make_async_copy(rs_hbm, rs_ref, sem_in.at[6]),
        pltpu.make_async_copy(cp_hbm, cp_ref, sem_in.at[7]),
    ]
    for c in other + come:
        c.start()
    for c, d in zip(come, go):
        c.wait()
        d.start()
    for c in other:
        c.wait()
    for l in range(CYCLES):
        source = rs_ref[l : l + 1, :]
        low_part = ((source >> 9) & 3) * 32 + (source & 31)
        high_part = (source >> 5) & 15
        pick = one_hot(sublanes(128, SLOTS) == low_part)
        values = rough[:, l, :]
        h0 = values.astype(BF16)
        r1 = values - h0.astype(F32)
        h1 = r1.astype(BF16)
        h2 = (r1 - h1.astype(F32)).astype(BF16)
        got = dot(h0, pick) + (dot(h1, pick) + dot(h2, pick))
        keep = sublanes(N_B, SLOTS) == high_part
        row = jnp.sum(jnp.where(keep, got, 0.0), axis=0, keepdims=True)
        ch_ref[l : l + 1, :] = jnp.where(slots < cp_ref[a * CYCLES + l], row, 0.0)
    for c in go:
        c.wait()


def per_device(legendre, coefficients, cycle_points, spectra, sea_mask, wind_column, roughness_source):
    vmem = pl.BlockSpec(memory_space=pltpu.VMEM)
    smem = pl.BlockSpec(memory_space=pltpu.SMEM)
    hbm = pl.BlockSpec(memory_space=pltpu.HBM)
    dma = pltpu.SemaphoreType.DMA
    winds = jax.ShapeDtypeStruct((1, CYCLES, 64, SLOTS), BF16)
    waves = jax.ShapeDtypeStruct((ROWS, COLS, HALF), F32)
    winds_done, waves_done, rough = pl.pallas_call(
        kernel,
        out_shape=(winds, waves, jax.ShapeDtypeStruct((N_B, 8, 128), F32)),
        in_specs=[hbm] * 7,
        out_specs=(hbm, hbm, hbm),
        scratch_shapes=[
            pltpu.VMEM((1, CYCLES, 64, SLOTS), BF16),
            pltpu.VMEM((ROWS, COLS, HALF), F32),
            pltpu.VMEM((N_B, 8, 128), F32),
            pltpu.SMEM((32,), jnp.int32),
            pltpu.VMEM((BLOCK, 32, NT), BF16),
            pltpu.VMEM((BLOCK, 2, 4, NT), BF16),
            pltpu.VMEM((GROUPS, 64, NT), BF16),
            pltpu.VMEM((ROWS, COLS, HALF), F32),
            pltpu.VMEM((ROWS, COLS), jnp.int32),
            pltpu.VMEM((ROWS, 512), jnp.int32),
            pltpu.VMEM((2, 16, HALF), F32),
            pltpu.VMEM((BLOCK, 256), F32),
            pltpu.VMEM((N_A, 8, 384), F32),
            pltpu.VMEM((N_A, 8, 384), F32),
            pltpu.VMEM((N_A, 8, 384), F32),
            pltpu.VMEM((N_B, 16, 2 * WAVES), BF16),
            pltpu.VMEM((256, 2 * WAVES), BF16),
            pltpu.VMEM((16, WAVES), F32),
            pltpu.VMEM((16, WAVES), BF16),
            pltpu.VMEM((CYCLES, 2 * WAVES, SLOTS), BF16),
            pltpu.VMEM((CYCLES, 2 * WAVES, POINTS), BF16),
            pltpu.VMEM((GROUPS, 8, SLOTS), F32),
            pltpu.VMEM((GROUPS, 8, SLOTS), F32),
            pltpu.VMEM((ROWS + 2, COLS + 16, HALF), F32),
            pltpu.VMEM((ROWS + 2, COLS + 16, HALF), F32),
            pltpu.VMEM((ROWS, COLS, HALF), F32),
            pltpu.VMEM((2, 2, ROWS, 1, HALF), F32),
            pltpu.VMEM((2, 2, ROWS, 1, HALF), F32),
            pltpu.VMEM((2, COLS, HALF), BF16),
            pltpu.VMEM((2, COLS, HALF), BF16),
            pltpu.VMEM((ROWS * COLS, 128), F32),
            pltpu.VMEM((ROWS * COLS, 128), F32),
            pltpu.VMEM((ROWS * COLS, 128), F32),
            pltpu.VMEM((2, ROWS * COLS, 128), F32),
            pltpu.VMEM((ROWS * COLS, 128), F32),
            pltpu.VMEM((2, N_B, 8, 128), F32),
            pltpu.VMEM((384, 512), BF16),
            pltpu.VMEM((256, 256), BF16),
            dma((6,)), dma((GROUPS,)),
            dma((N_A - 1,)), dma((N_A,)),
            dma((N_A,)), dma((N_A,)),
            dma((N_B - 1,)), dma((N_B,)),
            dma((N_B - 1,)), dma((1,)),
            dma((2, 3)), dma((2, 3)),
            dma((1,)), dma((1,)),
            dma((2 * N_B - 1,)), dma((2, N_B)),
            dma((3,)),
        ],
        compiler_params=pltpu.CompilerParams(
            collective_id=0, has_side_effects=True, vmem_limit_bytes=VMEM
        ),
    )(
        cycle_points, legendre, coefficients.reshape(BLOCK, 2, 4, NT), spectra, sea_mask, wind_column,
        jnp.asarray(bin_table()),
    )
    return pl.pallas_call(
        last,
        out_shape=(winds, waves, jax.ShapeDtypeStruct((CYCLES, SLOTS), F32)),
        in_specs=[hbm] * 5,
        out_specs=(hbm, hbm, vmem),
        scratch_shapes=[
            pltpu.SMEM((32,), jnp.int32),
            pltpu.VMEM((1, CYCLES, 64, SLOTS), BF16),
            pltpu.VMEM((ROWS, COLS, HALF), F32),
            pltpu.VMEM((N_B, 8, 128), F32),
            pltpu.VMEM((CYCLES, SLOTS), jnp.int32),
            dma((8,)), dma((5,)),
        ],
        compiler_params=pltpu.CompilerParams(vmem_limit_bytes=VMEM),
    )(cycle_points, winds_done, waves_done, rough, roughness_source)


def solution(mesh):
    in_specs = (
        P("aa", None, None),
        P("comp", "aa", None, "ba", None),
        P(),
        P("aa", "ba", "comp"),
        P("aa", "ba"),
        P("aa", None),
        P("aa", "ba"),
    )
    out_specs = (P("comp", "aa", None, "ba"), P("aa", "ba", "comp"), P("aa", "ba"))
    return jax.shard_map(
        per_device, mesh=mesh, in_specs=in_specs, out_specs=out_specs, check_vma=False
    )
```

```python
import math

import numpy as np

import jax
import jax.numpy as jnp
from jax import lax
from jax.experimental import pallas as pl
from jax.experimental.pallas import tpu as pltpu
from jax.sharding import PartitionSpec as P

LON = 4096
NDIR = 36
NFREQ = 36
F32 = jnp.float32
BF16 = jnp.bfloat16
MESH = pl.DeviceIdType.MESH

N_A = 8
N_B = 16
N_X = 4
N_Z = 4
WAVES = 640
BLOCK = WAVES // N_A
GROUPS = BLOCK // 8
NT = 1280
CYCLES = 4
SLOTS = LON // N_B
ROWS = 16
COLS = 32
VMEM = 64_000_000
HALF = NDIR * NFREQ // 2
POINTS = 128
FAR = [(2, 3), (2, 2), (1, 3), (3, 3), (2, 1), (1, 2), (3, 2), (0, 3), (1, 1), (3, 1), (2, 0), (0, 2), (1, 0), (3, 0), (0, 1)]
TILES = [(j, min(128, HALF - j)) for j in range(0, HALF, 128)]


def bin_table():
    b = np.arange(NDIR * NFREQ)
    theta = 2 * np.pi * (b // NFREQ + 0.5) / NDIR
    ratio = np.exp(-math.log(1.1) * (b % NFREQ))
    freq = 0.04177 / ratio
    east = 0.45 * ratio * np.cos(theta)
    north = 0.45 * ratio * np.sin(theta)
    q = 2 * np.pi * freq / 9.81
    assert (north[:HALF] > 0).all() and (north[HALF:] < 0).all()
    width = 0.1 * freq * (2 * np.pi / NDIR)
    rows = [
        np.abs(east),
        np.abs(north),
        1.0 - np.abs(east) - np.abs(north),
        np.sign(east),
        np.sign(north),
        10.0 * q * np.cos(theta),
        10.0 * q * np.sin(theta),
        width,
        0.5 * freq / 0.2,
    ]
    rows += [np.zeros_like(freq)] * (16 - len(rows))
    table = np.stack(rows).astype(np.float32)
    return np.stack([table[:, :HALF], table[:, HALF:]])


AE, AN, CC, SE, SN, QE, QN, WB, DF = range(9)


def poly(y2, coefs):
    acc = jnp.full_like(y2, coefs[-1])
    for c in coefs[-2::-1]:
        acc = acc * y2 + c
    return acc


SIN_C = [(-1.0) ** i / math.factorial(2 * i + 1) for i in range(7)]
COS_C = [(-1.0) ** i / math.factorial(2 * i) for i in range(7)]


def turn(mk, count, inv):
    rest = mk - jnp.floor(mk * inv + 0.5) * count
    y = (rest * inv) * math.pi
    y2 = y * y
    s = y * poly(y2, SIN_C)
    c = poly(y2, COS_C)
    return 1.0 - 2.0 * s * s, 2.0 * s * c


def rcopy(src, dst, send, recv, device):
    return pltpu.make_async_remote_copy(
        src_ref=src, dst_ref=dst, send_sem=send, recv_sem=recv, device_id=device, device_id_type=MESH
    )


def lanes(rows, width=128):
    return lax.broadcasted_iota(jnp.int32, (rows, width), 1)


def sublanes(rows, width=128):
    return lax.broadcasted_iota(jnp.int32, (rows, width), 0)


def spread(row, n):
    kept = jnp.where(sublanes(n, n) == lanes(n, n), jnp.broadcast_to(row, (n, n)), 0.0)
    return jnp.broadcast_to(jnp.sum(kept, axis=1, keepdims=True), (n, 128))


def one_hot(mask):
    return mask.astype(F32).astype(BF16)


def dot(x, y, dims=((1,), (0,))):
    return lax.dot_general(x, y, (dims, ((), ())), preferred_element_type=F32)


def kernel(
    cp_hbm, leg_hbm, coef_hbm, spec_hbm, mask_hbm, wc_hbm, cst_hbm,
    gw_out, ws_out, rough_out,
    gw_ref, ws_ref, rough, cp_ref, leg, coef, degrees, spec, mask_in, wc, cst_ref, sall, msg, a2a, a2x, gath, gperm, low_f, l0,
    table, ptable, ca, sa, buf_a, buf_b, d2, edge, edge_in, row_out, row_in,
    mask_b, east_b, north_b, part, part_in, st, st_in, order_in, order_out,
    i_sem, leg_sem, a_send, a_recv, x_send, x_recv, g_send, g_recv, l_send, l_recv, h_send, h_recv,
    c_send, c_recv, r_send, r_recv, o_sem,
):
    s = lax.axis_index("comp")
    a = lax.axis_index("aa")
    b = lax.axis_index("ba")
    x, z = b // N_Z, b % N_Z
    partner = {"comp": 1 - s}

    flips = lambda v: {0: v, 1: v + 1 - 2 * (v % 2), 2: lax.rem(v + 2, 4), 3: 3 - v}
    flip_x, flip_z, flip_y = flips(x), flips(z), flips(a % 4)
    half = a // 4
    peers_a = [(1 - half) * 4 + flip_y[i] for i in (2, 1, 3, 0)] + [half * 4 + flip_y[i] for i in (2, 1, 3)]
    peers_b = [flip_x[i] * N_Z + flip_z[j] for i, j in FAR]

    small = [
        pltpu.make_async_copy(mask_hbm, mask_in, i_sem.at[1]),
        pltpu.make_async_copy(wc_hbm, wc, i_sem.at[2]),
        pltpu.make_async_copy(cst_hbm, cst_ref, i_sem.at[3]),
        pltpu.make_async_copy(spec_hbm, spec, i_sem.at[4]),
        pltpu.make_async_copy(cp_hbm, cp_ref, i_sem.at[5]),
    ]
    coef_copy = pltpu.make_async_copy(coef_hbm, coef, i_sem.at[0])
    coef_copy.start()
    leg_copies = lambda g: pltpu.make_async_copy(
        leg_hbm.at[pl.ds(g * 8, 8)], leg.at[pl.ds(g * 8, 8)], leg_sem.at[g]
    )
    for g in range(GROUPS):
        leg_copies(g).start()
    for c in small:
        c.start()
    barrier = pltpu.get_barrier_semaphore()
    pl.semaphore_signal(barrier, inc=1, device_id=partner, device_id_type=MESH)
    for t in peers_a:
        pl.semaphore_signal(barrier, inc=1, device_id={"aa": t}, device_id_type=MESH)
    for t in peers_b:
        pl.semaphore_signal(barrier, inc=1, device_id={"ba": t}, device_id_type=MESH)

    @pl.when(b == 0)
    def _():
        for t in peers_a:
            pl.semaphore_signal(barrier, inc=1, device_id={"comp": 1 - s, "aa": t}, device_id_type=MESH)

    def halo(buf, step):
        up = jnp.where(s == 0, N_A - 2 - a, a - 1)
        down = jnp.where(s == 0, a - 1, N_A - 2 - a)
        return [
            (up >= 0, down >= 0, rcopy(
                row_out.at[step], row_in.at[step],
                h_send.at[step, 0], h_recv.at[step, 0], {"aa": lax.rem(a + 1 + (N_A - 2) * s, N_A)})),
            (b < N_B - 1, b > 0, rcopy(
                edge.at[step, 1], edge_in.at[step, 0],
                h_send.at[step, 1], h_recv.at[step, 1], {"ba": lax.rem(b + 1, N_B)})),
            (b > 0, b < N_B - 1, rcopy(
                edge.at[step, 0], edge_in.at[step, 1],
                h_send.at[step, 2], h_recv.at[step, 2], {"ba": lax.rem(b + N_B - 1, N_B)})),
        ]

    def halo_start(copies, buf, step):
        row_out[step] = buf[ROWS - (ROWS - 1) * s, 8 : 8 + COLS, :].astype(BF16)
        for can, _, c in copies:
            pl.when(can)(c.start)

    def halo_land(copies, buf, step):
        for i, (_, comes, c) in enumerate(copies):
            pl.when(comes)(c.wait_recv)

            @pl.when(jnp.logical_not(comes))
            def _():
                if i == 0:
                    row_in[step] = jnp.zeros((COLS, HALF), BF16)
                else:
                    edge_in[step, i - 1] = jnp.zeros((ROWS, 1, HALF), F32)

        buf[(ROWS + 1) * s, 8 : 8 + COLS, :] = row_in[step].astype(F32)
        for r in range(ROWS):
            buf[r + 1, 7:8, :] = edge_in[step, 0, r]
            buf[r + 1, 8 + COLS : 9 + COLS, :] = edge_in[step, 1, r]

    def halo_sent(copies):
        for can, _, c in copies:
            pl.when(can)(c.wait_send)

    coef_copy.wait()

    def masked(g, carry):
        rows = []
        for i in range(8):
            order = a * BLOCK + g * 8 + i
            block = jnp.concatenate([coef[g * 8 + i, p].astype(F32) for p in range(2)], axis=0)
            rows.append(jnp.where(lanes(8, NT) >= order, block, 0.0))
        degrees[g] = jnp.concatenate(rows, axis=0).astype(BF16)
        return carry

    lax.fori_loop(0, GROUPS, masked, 0)

    def legendre(g, carry):
        leg_copies(g).wait()
        cross = dot(degrees[g], leg[pl.ds(g * 8, 8)].reshape(256, NT), ((1,), (1,)))
        at = pl.ds(pl.multiple_of(g * 8, 8), 8)
        for t in range(2):
            kept = cross[t * 32 : t * 32 + 8, t * 128 : t * 128 + 128]
            for q in range(1, 4):
                m = t * 4 + q
                kept = jnp.where(lanes(8) >= q * 32, cross[m * 8 : m * 8 + 8, t * 128 : t * 128 + 128], kept)
            sall[at, t * 128 : t * 128 + 128] = kept
        return carry

    lax.fori_loop(0, GROUPS, legendre, 0)

    i, o = sublanes(256, 256), lanes(256, 256)
    moved = dot(sall[...].astype(BF16), one_hot(o == (i & 31) // 4 * 32 + (i // 32) * 4 + (i & 3)))
    turned = {}
    for t in range(N_A):
        for q in range(3):
            acc = jnp.zeros((8, 128), F32)
            for g in range(q * 4, min(q * 4 + 4, GROUPS)):
                shift = 32 * ((g - t) % 4)
                key = (g, t // 4, shift)
                if key not in turned:
                    v = moved[g * 8 : g * 8 + 8, t // 4 * 128 : t // 4 * 128 + 128]
                    turned[key] = pltpu.roll(v, shift, axis=1) if shift else v
                at = lanes(8) // 32 == g % 4
                acc = jnp.where(at, turned[key], acc)
            msg[t, :, q * 128 : q * 128 + 128] = acc

    pl.semaphore_wait(barrier, N_A + N_B - 1 + jnp.where(b == 0, N_A - 1, 0))
    sent = []
    for d, t in enumerate(peers_a):
        c = rcopy(msg.at[t], a2a.at[a], a_send.at[d], a_recv.at[a], {"aa": t})
        c.start()
        sent.append(c)
    crossed = []
    for d, t in enumerate(peers_a + [a]):
        crossed.append(
            rcopy(msg.at[t], a2x.at[a], x_send.at[d], x_recv.at[a], {"comp": 1 - s, "aa": t})
        )

    @pl.when(b == 0)
    def _():
        for c in crossed:
            c.start()

    a2a[a] = msg[a]


    for c in small:
        c.wait()
    sea = mask_in[...].astype(F32)
    for r in range(ROWS):
        mask_b[r * COLS : (r + 1) * COLS, :] = spread(sea[r : r + 1, :], COLS)

    def first(r, carry):
        m = mask_b[pl.ds(r * COLS, COLS), :]
        for j, w in TILES:
            v = spec[r, :, j : j + w] * m[:, :w]
            buf_a[r + 1, 8 : 8 + COLS, j : j + w] = v
            edge[0, 0, r, :, j : j + w] = v[0:1, :]
            edge[0, 1, r, :, j : j + w] = v[COLS - 1 : COLS, :]
        return carry

    lax.fori_loop(0, ROWS, first, 0)

    halo_a = halo(buf_a, 0)
    halo_start(halo_a, buf_a, 0)

    def tables(out, l, k, active):
        w = k.shape[1]
        count = jnp.full((1, w), cp_ref[a * CYCLES + l], jnp.int32).astype(F32)
        inv = 1.0 / count
        cu, su = turn(sublanes(WAVES // 8, w).astype(F32) * 8.0 * k, count, inv)
        ca[:, :, :w] = cu.reshape(GROUPS, 8, w)
        sa[:, :, :w] = su.reshape(GROUPS, 8, w)
        cv, sv = turn(sublanes(8, w).astype(F32) * k, count, inv)
        cv, sv = cv * active, sv * active
        minus_c, minus_s = -cv, -sv

        def block(i, carry):
            for h in range(4):
                cs, ss = [], []
                for o in range(h * 2, h * 2 + 2):
                    c0, s0 = ca[i, o : o + 1, :w], sa[i, o : o + 1, :w]
                    cs.append(c0 * cv + s0 * minus_s)
                    ss.append(s0 * minus_c + c0 * minus_s)
                at = pl.multiple_of(i * 64 + h * 16, 16)
                out[l, pl.ds(at, 16), :] = jnp.concatenate(cs, axis=0).astype(BF16)
                out[l, pl.ds(WAVES + at, 16), :] = jnp.concatenate(ss, axis=0).astype(BF16)
            return carry

        lax.fori_loop(0, GROUPS, block, 0)
        top = out[l, 0:16, :].astype(F32)
        out[l, 0:16, :] = jnp.where(sublanes(16, w) == 0, top * 0.5, top).astype(BF16)

    near = wc[:, pl.ds(pl.multiple_of(b // 4 * 128, 128), 128)].astype(F32)
    near = pltpu.roll(near, (4 - b % 4) % 4 * COLS, axis=1)
    near = jnp.where(lanes(ROWS) < COLS, near, 0.0)
    side = near
    for q in range(1, 4):
        side = jnp.where(sublanes(ROWS) % 4 == q, pltpu.roll(near, q * COLS, axis=1), side)
    for l in range(CYCLES):
        tables(ptable, l, jnp.sum(side[l * 4 : l * 4 + 4, :], axis=0, keepdims=True), 2.0)

    slots = lanes(1, SLOTS) + b * SLOTS
    for l in range(CYCLES):
        active = jnp.where(slots < cp_ref[a * CYCLES + l], 2.0, 0.0)
        tables(table, l, slots.astype(F32), active)

    i, o = sublanes(384, 512), lanes(384, 512)
    order_in[...] = one_hot((o == (i & 3) * 128 + i // 4) & (i < BLOCK * 4))
    r = sublanes(64, 64)
    order_out[...] = one_hot(lanes(64, 64) == (r & 15) // 4 * 16 + r // 16 * 4 + (r & 3))

    def upwind(buf, r, j, w):
        c = lambda i: cst_ref[s, i : i + 1, j : j + w]
        here = buf[r + 1, 8 : 8 + COLS, j : j + w]
        ux = jnp.where(c(SE) > 0.0, buf[r + 1, 7 : 7 + COLS, j : j + w], buf[r + 1, 9 : 9 + COLS, j : j + w])
        uy = buf[r + 2 * s, 8 : 8 + COLS, j : j + w]
        return here * c(CC) + ux * c(AE) + uy * c(AN)

    halo_land(halo_a, buf_a, 0)

    def second(r, carry):
        m = mask_b[pl.ds(r * COLS, COLS), :]
        for j, w in TILES:
            v = upwind(buf_a, r, j, w) * m[:, :w]
            buf_b[r + 1, 8 : 8 + COLS, j : j + w] = v
            edge[1, 0, r, :, j : j + w] = v[0:1, :]
            edge[1, 1, r, :, j : j + w] = v[COLS - 1 : COLS, :]
        return carry

    lax.fori_loop(0, ROWS, second, 0)
    halo_b = halo(buf_b, 1)
    halo_start(halo_b, buf_b, 1)

    def compact(landed):
        wide = dot(landed[...].reshape(64, 384).astype(BF16), order_in[...])
        out = []
        for l in range(CYCLES):
            tiles = [jnp.zeros((8, 128), F32) for _ in range(WAVES // 128)]
            for c in range(N_A):
                t, shift = divmod(c * BLOCK, 128)
                piece = wide[c * 8 : c * 8 + 8, l * 128 : l * 128 + 128]
                if shift:
                    piece = pltpu.roll(piece, shift, axis=1)
                    tiles[t] = jnp.where(lanes(8) >= shift, piece, tiles[t])
                    if shift + BLOCK > 128:
                        tiles[t + 1] = jnp.where(lanes(8) < shift, piece, tiles[t + 1])
                else:
                    tiles[t] = jnp.where(lanes(8) < BLOCK, piece, tiles[t])
            out.append(tiles)
        return out

    def lowest(blocks, base):
        for l in range(CYCLES):
            for t in range(WAVES // 128):
                for p in range(2):
                    r = base + p * 4 + l
                    low_f[r : r + 1, t * 128 : t * 128 + 128] = blocks[l][t][p * 4 : p * 4 + 1, :]

    for d, c in enumerate(peers_a):
        rcopy(msg.at[0], a2a.at[c], a_send.at[d], a_recv.at[c], {"aa": c}).wait_recv()
    blocks = compact(a2a)
    low = [
        rcopy(l0, l0, l_send.at[d], l_recv.at[0], {"ba": t}) for d, t in enumerate(peers_b)
    ]

    @pl.when(b == 0)
    def _():
        lowest(blocks, 0)
        for d, c in enumerate(peers_a + [a]):
            rcopy(msg.at[0], a2x.at[c], x_send.at[d], x_recv.at[c], {"comp": 1 - s, "aa": c}).wait_recv()
        lowest(compact(a2x), 8)
        l0[...] = low_f[...].astype(BF16)
        for c in low:
            c.start()

    for t in range(WAVES // 128):
        up = [pltpu.roll(blocks[l][t], 4, axis=0) for l in range(CYCLES)]
        own = [blocks[l][t] for l in range(CYCLES)]
        top = sublanes(8) < 4
        for p in range(2):
            pair = [
                jnp.where(top, own[l], up[l + 1]) if p == 0 else jnp.where(top, up[l], own[l + 1])
                for l in (0, 2)
            ]
            at = p * WAVES + t * 128
            gath[b, :, at : at + 128] = jnp.concatenate(pair, axis=0).astype(BF16)

    gathers = []

    def give(o, device):
        c = rcopy(gath.at[o], gath.at[o], g_send.at[len(gathers)], g_recv.at[o], {"ba": device})
        c.start()
        gathers.append(c)

    def arrived(o):
        rcopy(gath.at[o], gath.at[o], g_send.at[0], g_recv.at[o], {"ba": o}).wait_recv()

    x_peers = [lax.rem(x + d, N_X) * N_Z + z for d in (1, 3, 2)]
    for d in range(1, N_Z):
        give(b, x * N_Z + lax.rem(z + d, N_Z))
    for t in x_peers:
        give(b, t)

    halo_land(halo_b, buf_b, 1)

    def third(r, carry):
        at = pl.ds(r * COLS, COLS)
        m = mask_b[at, :]
        total = jnp.zeros((COLS, 128), F32)
        for j, w in TILES:
            v = upwind(buf_b, r, j, w) * m[:, :w]
            d2[r, :, j : j + w] = v
            term = v * cst_ref[s, WB : WB + 1, j : j + w]
            if w == 128:
                total = total + term
            else:
                part[0, at, :] = total
                part[0, at, :w] = total[:, :w] + term
        return carry

    lax.fori_loop(0, ROWS, third, 0)
    energy_copy = rcopy(part.at[0], part_in, c_send.at[0], c_recv.at[0], partner)
    energy_copy.start()

    for d in range(1, N_Z):
        o = x * N_Z + lax.rem(z + N_Z - d, N_Z)
        arrived(o)
        for t in x_peers:
            give(o, t)

    @pl.when(b > 0)
    def _():
        low[0].wait_recv()

    own, other = [], []
    for l in range(CYCLES):
        pc = dot(l0[...], ptable[l, 0:WAVES, :])
        ps = dot(l0[...], ptable[l, WAVES:, :])
        own.append((pc[l : l + 1, :] + ps[4 + l : 5 + l, :]).astype(BF16).astype(F32))
        other.append((pc[8 + l : 9 + l, :] + ps[12 + l : 13 + l, :]).astype(BF16).astype(F32))
    east = [jnp.where(s == 0, p, q) for p, q in zip(own, other)]
    north = [jnp.where(s == 0, q, p) for p, q in zip(own, other)]
    for l in range(CYCLES):
        east_b[pl.ds(l * POINTS, POINTS), :] = spread(east[l], POINTS)
        north_b[pl.ds(l * POINTS, POINTS), :] = spread(north[l], POINTS)

    def gain_of(e, n, r, j, w):
        c = lambda i: cst_ref[s, i : i + 1, j : j + w]
        align = e[:, :w] * c(QE) + n[:, :w] * c(QN)
        grown = 0.05 * jnp.maximum(align - 1.0, 0.0) * d2[r, :, j : j + w]
        return align, grown

    def fourth(r, carry):
        at = pl.ds(r * COLS, COLS)
        e, n = east_b[at, :], north_b[at, :]
        total = jnp.zeros((COLS, 128), F32)
        for j, w in TILES:
            align, grown = gain_of(e, n, r, j, w)
            term = grown * align * cst_ref[s, WB : WB + 1, j : j + w]
            if w == 128:
                total = total + term
            else:
                part[1, at, :] = total
                part[1, at, :w] = total[:, :w] + term
        return carry

    lax.fori_loop(0, ROWS, fourth, 0)
    for l in range(CYCLES):
        total = jnp.sum(part[1, pl.ds(l * POINTS, POINTS), :], axis=1, keepdims=True)
        kept = jnp.where(sublanes(POINTS) == lanes(POINTS), jnp.broadcast_to(total, (POINTS, 128)), 0.0)
        row = jnp.sum(kept, axis=0, keepdims=True)
        st[l : l + 1, :] = row
        st[4 + l : 5 + l, :] = row
    stress_copy = rcopy(st, st_in, c_send.at[1], c_recv.at[1], partner)
    stress_copy.start()

    energy_copy.wait_recv()
    for l in range(CYCLES):
        at = pl.ds(l * POINTS, POINTS)
        level = jnp.sum(part[0, at, :] + part_in[at, :], axis=1, keepdims=True) * 0.125
        mask_b[at, :] = jnp.broadcast_to(level * level, (POINTS, 128))

    def fifth(r, carry):
        at = pl.ds(r * COLS, COLS)
        e, n = east_b[at, :], north_b[at, :]
        square = mask_b[at, :]
        for j, w in TILES:
            _, grown = gain_of(e, n, r, j, w)
            decay = square[:, :w] * cst_ref[s, DF : DF + 1, j : j + w]
            ws_ref[r, :, j : j + w] = (d2[r, :, j : j + w] + grown) / (1.0 + decay)
        return carry

    lax.fori_loop(0, ROWS, fifth, 0)
    ws_copy = pltpu.make_async_copy(ws_ref, ws_out, o_sem.at[0])
    ws_copy.start()

    stress_copy.wait_recv()
    e, n = jnp.concatenate(east * 2, axis=0), jnp.concatenate(north * 2, axis=0)
    rough[b] = jnp.sqrt(1.0 + 0.03 * (st[...] + st_in[...]) / (0.12 * (e * e + n * n) + 0.02))
    rough_copies = []
    for d, t in enumerate(peers_b):
        rough_copies.append(rcopy(rough.at[b], rough.at[b], r_send.at[d], r_recv.at[b], {"ba": t}))
        rough_copies[-1].start()

    for xd in (0, 1, 3, 2):
        col = lax.rem(x + xd, N_X)
        if xd:
            for zd in range(N_Z):
                arrived(col * N_Z + lax.rem(z + zd, N_Z))
        block = gath[pl.ds(col * N_Z, N_Z)].reshape(64, 2 * WAVES)
        gperm[...] = dot(order_out[...], block).astype(BF16)
        for l in range(CYCLES):
            gw_ref[0, l, pl.ds(pl.multiple_of(col * 16, 16), 16), :] = dot(
                gperm[l * 16 : l * 16 + 16, :], table[l]
            ).astype(BF16)
    gw_copy = pltpu.make_async_copy(gw_ref, gw_out, o_sem.at[1])
    gw_copy.start()

    for d, t in enumerate(peers_b):
        rcopy(rough.at[t], rough.at[t], r_send.at[d], r_recv.at[t], {"ba": t}).wait_recv()
    rough_copy = pltpu.make_async_copy(rough, rough_out, o_sem.at[2])
    rough_copy.start()
    for c in sent + gathers + rough_copies + [energy_copy, stress_copy]:
        c.wait_send()
    halo_sent(halo_a)
    halo_sent(halo_b)

    @pl.when(b == 0)
    def _():
        for c in low + crossed:
            c.wait_send()

    for c in (ws_copy, gw_copy, rough_copy):
        c.wait()


def last(
    cp_hbm, gw_in, ws_in, rough_in, rs_hbm, gw_ref, ws_ref, ch_ref, cp_ref, gw, ws, rough, rs_ref, sem_in, sem_out
):
    a = lax.axis_index("aa")
    slots = lanes(1, SLOTS) + lax.axis_index("ba") * SLOTS
    step = ROWS // 4
    blocks = [pl.ds(i * step, step) for i in range(4)]
    come = [pltpu.make_async_copy(ws_in.at[k], ws.at[k], sem_in.at[i]) for i, k in enumerate(blocks)]
    come.append(pltpu.make_async_copy(gw_in, gw, sem_in.at[4]))
    go = [pltpu.make_async_copy(ws.at[k], ws_ref.at[k], sem_out.at[i]) for i, k in enumerate(blocks)]
    go.append(pltpu.make_async_copy(gw, gw_ref, sem_out.at[4]))
    other = [
        pltpu.make_async_copy(rough_in, rough, sem_in.at[5]),
        pltpu.make_async_copy(rs_hbm, rs_ref, sem_in.at[6]),
        pltpu.make_async_copy(cp_hbm, cp_ref, sem_in.at[7]),
    ]
    for c in other + come:
        c.start()
    for c, d in zip(come, go):
        c.wait()
        d.start()
    for c in other:
        c.wait()
    for l in range(CYCLES):
        source = rs_ref[l : l + 1, :]
        low_part = ((source >> 9) & 3) * 32 + (source & 31)
        high_part = (source >> 5) & 15
        pick = one_hot(sublanes(128, SLOTS) == low_part)
        values = rough[:, l, :]
        h0 = values.astype(BF16)
        r1 = values - h0.astype(F32)
        h1 = r1.astype(BF16)
        h2 = (r1 - h1.astype(F32)).astype(BF16)
        got = dot(h0, pick) + (dot(h1, pick) + dot(h2, pick))
        keep = sublanes(N_B, SLOTS) == high_part
        row = jnp.sum(jnp.where(keep, got, 0.0), axis=0, keepdims=True)
        ch_ref[l : l + 1, :] = jnp.where(slots < cp_ref[a * CYCLES + l], row, 0.0)
    for c in go:
        c.wait()


def per_device(legendre, coefficients, cycle_points, spectra, sea_mask, wind_column, roughness_source):
    vmem = pl.BlockSpec(memory_space=pltpu.VMEM)
    smem = pl.BlockSpec(memory_space=pltpu.SMEM)
    hbm = pl.BlockSpec(memory_space=pltpu.HBM)
    dma = pltpu.SemaphoreType.DMA
    winds = jax.ShapeDtypeStruct((1, CYCLES, 64, SLOTS), BF16)
    waves = jax.ShapeDtypeStruct((ROWS, COLS, HALF), F32)
    winds_done, waves_done, rough = pl.pallas_call(
        kernel,
        out_shape=(winds, waves, jax.ShapeDtypeStruct((N_B, 8, 128), F32)),
        in_specs=[hbm] * 7,
        out_specs=(hbm, hbm, hbm),
        scratch_shapes=[
            pltpu.VMEM((1, CYCLES, 64, SLOTS), BF16),
            pltpu.VMEM((ROWS, COLS, HALF), F32),
            pltpu.VMEM((N_B, 8, 128), F32),
            pltpu.SMEM((32,), jnp.int32),
            pltpu.VMEM((BLOCK, 32, NT), BF16),
            pltpu.VMEM((BLOCK, 2, 4, NT), BF16),
            pltpu.VMEM((GROUPS, 64, NT), BF16),
            pltpu.VMEM((ROWS, COLS, HALF), F32),
            pltpu.VMEM((ROWS, COLS), jnp.int32),
            pltpu.VMEM((ROWS, 512), jnp.int32),
            pltpu.VMEM((2, 16, HALF), F32),
            pltpu.VMEM((BLOCK, 256), F32),
            pltpu.VMEM((N_A, 8, 384), F32),
            pltpu.VMEM((N_A, 8, 384), F32),
            pltpu.VMEM((N_A, 8, 384), F32),
            pltpu.VMEM((N_B, 16, 2 * WAVES), BF16),
            pltpu.VMEM((64, 2 * WAVES), BF16),
            pltpu.VMEM((16, WAVES), F32),
            pltpu.VMEM((16, WAVES), BF16),
            pltpu.VMEM((CYCLES, 2 * WAVES, SLOTS), BF16),
            pltpu.VMEM((CYCLES, 2 * WAVES, POINTS), BF16),
            pltpu.VMEM((GROUPS, 8, SLOTS), F32),
            pltpu.VMEM((GROUPS, 8, SLOTS), F32),
            pltpu.VMEM((ROWS + 2, COLS + 16, HALF), F32),
            pltpu.VMEM((ROWS + 2, COLS + 16, HALF), F32),
            pltpu.VMEM((ROWS, COLS, HALF), F32),
            pltpu.VMEM((2, 2, ROWS, 1, HALF), F32),
            pltpu.VMEM((2, 2, ROWS, 1, HALF), F32),
            pltpu.VMEM((2, COLS, HALF), BF16),
            pltpu.VMEM((2, COLS, HALF), BF16),
            pltpu.VMEM((ROWS * COLS, 128), F32),
            pltpu.VMEM((ROWS * COLS, 128), F32),
            pltpu.VMEM((ROWS * COLS, 128), F32),
            pltpu.VMEM((2, ROWS * COLS, 128), F32),
            pltpu.VMEM((ROWS * COLS, 128), F32),
            pltpu.VMEM((8, 128), F32),
            pltpu.VMEM((8, 128), F32),
            pltpu.VMEM((384, 512), BF16),
            pltpu.VMEM((64, 64), BF16),
            dma((6,)), dma((GROUPS,)),
            dma((N_A - 1,)), dma((N_A,)),
            dma((N_A,)), dma((N_A,)),
            dma((N_B - 1,)), dma((N_B,)),
            dma((N_B - 1,)), dma((1,)),
            dma((2, 3)), dma((2, 3)),
            dma((2,)), dma((2,)),
            dma((N_B - 1,)), dma((N_B,)),
            dma((3,)),
        ],
        compiler_params=pltpu.CompilerParams(
            collective_id=0, has_side_effects=True, vmem_limit_bytes=VMEM
        ),
    )(
        cycle_points, legendre, coefficients.reshape(BLOCK, 2, 4, NT), spectra, sea_mask, wind_column,
        jnp.asarray(bin_table()),
    )
    return pl.pallas_call(
        last,
        out_shape=(winds, waves, jax.ShapeDtypeStruct((CYCLES, SLOTS), F32)),
        in_specs=[hbm] * 5,
        out_specs=(hbm, hbm, vmem),
        scratch_shapes=[
            pltpu.SMEM((32,), jnp.int32),
            pltpu.VMEM((1, CYCLES, 64, SLOTS), BF16),
            pltpu.VMEM((ROWS, COLS, HALF), F32),
            pltpu.VMEM((N_B, 8, 128), F32),
            pltpu.VMEM((CYCLES, SLOTS), jnp.int32),
            dma((8,)), dma((5,)),
        ],
        compiler_params=pltpu.CompilerParams(vmem_limit_bytes=VMEM),
    )(cycle_points, winds_done, waves_done, rough, roughness_source)


def solution(mesh):
    in_specs = (
        P("aa", None, None),
        P("comp", "aa", None, "ba", None),
        P(),
        P("aa", "ba", "comp"),
        P("aa", "ba"),
        P("aa", None),
        P("aa", "ba"),
    )
    out_specs = (P("comp", "aa", None, "ba"), P("aa", "ba", "comp"), P("aa", "ba"))
    return jax.shard_map(
        per_device, mesh=mesh, in_specs=in_specs, out_specs=out_specs, check_vma=False
    )
```

```python
import math

import numpy as np

import jax
import jax.numpy as jnp
from jax import lax
from jax.experimental import pallas as pl
from jax.experimental.pallas import tpu as pltpu
from jax.sharding import PartitionSpec as P

LON = 4096
NDIR = 36
NFREQ = 36
F32 = jnp.float32
BF16 = jnp.bfloat16
MESH = pl.DeviceIdType.MESH

N_A = 8
N_B = 16
N_X = 4
N_Z = 4
WAVES = 640
BLOCK = WAVES // N_A
GROUPS = BLOCK // 8
NT = 1280
CYCLES = 4
SLOTS = LON // N_B
ROWS = 16
COLS = 32
VMEM = 64_000_000
HALF = NDIR * NFREQ // 2
POINTS = 128
FAR = [(2, 3), (2, 2), (1, 3), (3, 3), (2, 1), (1, 2), (3, 2), (0, 3), (1, 1), (3, 1), (2, 0), (0, 2), (1, 0), (3, 0), (0, 1)]
TILES = [(j, min(128, HALF - j)) for j in range(0, HALF, 128)]


def bin_table():
    b = np.arange(NDIR * NFREQ)
    theta = 2 * np.pi * (b // NFREQ + 0.5) / NDIR
    ratio = np.exp(-math.log(1.1) * (b % NFREQ))
    freq = 0.04177 / ratio
    east = 0.45 * ratio * np.cos(theta)
    north = 0.45 * ratio * np.sin(theta)
    q = 2 * np.pi * freq / 9.81
    assert (north[:HALF] > 0).all() and (north[HALF:] < 0).all()
    width = 0.1 * freq * (2 * np.pi / NDIR)
    rows = [
        np.abs(east),
        np.abs(north),
        1.0 - np.abs(east) - np.abs(north),
        np.sign(east),
        np.sign(north),
        10.0 * q * np.cos(theta),
        10.0 * q * np.sin(theta),
        width,
        0.5 * freq / 0.2,
    ]
    rows += [np.zeros_like(freq)] * (16 - len(rows))
    table = np.stack(rows).astype(np.float32)
    return np.stack([table[:, :HALF], table[:, HALF:]])


AE, AN, CC, SE, SN, QE, QN, WB, DF = range(9)


def poly(y2, coefs):
    acc = jnp.full_like(y2, coefs[-1])
    for c in coefs[-2::-1]:
        acc = acc * y2 + c
    return acc


SIN_C = [(-1.0) ** i / math.factorial(2 * i + 1) for i in range(7)]
COS_C = [(-1.0) ** i / math.factorial(2 * i) for i in range(7)]


def turn(mk, count, inv):
    rest = mk - jnp.floor(mk * inv + 0.5) * count
    y = (rest * inv) * math.pi
    y2 = y * y
    s = y * poly(y2, SIN_C)
    c = poly(y2, COS_C)
    return 1.0 - 2.0 * s * s, 2.0 * s * c


def rcopy(src, dst, send, recv, device):
    return pltpu.make_async_remote_copy(
        src_ref=src, dst_ref=dst, send_sem=send, recv_sem=recv, device_id=device, device_id_type=MESH
    )


def lanes(rows, width=128):
    return lax.broadcasted_iota(jnp.int32, (rows, width), 1)


def sublanes(rows, width=128):
    return lax.broadcasted_iota(jnp.int32, (rows, width), 0)


def spread(row, n):
    kept = jnp.where(sublanes(n, n) == lanes(n, n), jnp.broadcast_to(row, (n, n)), 0.0)
    return jnp.broadcast_to(jnp.sum(kept, axis=1, keepdims=True), (n, 128))


def one_hot(mask):
    return mask.astype(F32).astype(BF16)


def dot(x, y, dims=((1,), (0,))):
    return lax.dot_general(x, y, (dims, ((), ())), preferred_element_type=F32)


def kernel(
    cp_hbm, leg_hbm, coef_hbm, spec_hbm, mask_hbm, wc_hbm, cst_hbm,
    gw_out, ws_out, rough_out,
    gw_ref, ws_ref, rough, cp_ref, leg, coef, degrees, spec, mask_in, wc, cst_ref, sall, msg, a2a, a2x, gath, gperm, low_f, l0,
    table, ptable, ca, sa, buf_a, buf_b, d2, edge, edge_in, row_out, row_in,
    mask_b, east_b, north_b, part, part_in, st, st_in, order_in, order_out,
    i_sem, leg_sem, a_send, a_recv, x_send, x_recv, g_send, g_recv, l_send, l_recv, h_send, h_recv,
    c_send, c_recv, r_send, r_recv, o_sem,
):
    s = lax.axis_index("comp")
    a = lax.axis_index("aa")
    b = lax.axis_index("ba")
    x, z = b // N_Z, b % N_Z
    partner = {"comp": 1 - s}

    flips = lambda v: {0: v, 1: v + 1 - 2 * (v % 2), 2: lax.rem(v + 2, 4), 3: 3 - v}
    flip_x, flip_z, flip_y = flips(x), flips(z), flips(a % 4)
    half = a // 4
    peers_a = [(1 - half) * 4 + flip_y[i] for i in (2, 1, 3, 0)] + [half * 4 + flip_y[i] for i in (2, 1, 3)]
    peers_b = [flip_x[i] * N_Z + flip_z[j] for i, j in FAR]

    small = [
        pltpu.make_async_copy(mask_hbm, mask_in, i_sem.at[1]),
        pltpu.make_async_copy(wc_hbm, wc, i_sem.at[2]),
        pltpu.make_async_copy(cst_hbm, cst_ref, i_sem.at[3]),
        pltpu.make_async_copy(spec_hbm, spec, i_sem.at[4]),
        pltpu.make_async_copy(cp_hbm, cp_ref, i_sem.at[5]),
    ]
    coef_copy = pltpu.make_async_copy(coef_hbm, coef, i_sem.at[0])
    coef_copy.start()
    leg_copies = lambda g: pltpu.make_async_copy(
        leg_hbm.at[pl.ds(g * 8, 8)], leg.at[pl.ds(g * 8, 8)], leg_sem.at[g]
    )
    for g in range(GROUPS):
        leg_copies(g).start()
    for c in small:
        c.start()
    barrier = pltpu.get_barrier_semaphore()
    pl.semaphore_signal(barrier, inc=1, device_id=partner, device_id_type=MESH)
    for t in peers_a:
        pl.semaphore_signal(barrier, inc=1, device_id={"aa": t}, device_id_type=MESH)
    for t in peers_b:
        pl.semaphore_signal(barrier, inc=1, device_id={"ba": t}, device_id_type=MESH)

    @pl.when(b == 0)
    def _():
        for t in peers_a:
            pl.semaphore_signal(barrier, inc=1, device_id={"comp": 1 - s, "aa": t}, device_id_type=MESH)

    def halo(buf, step):
        up = jnp.where(s == 0, N_A - 2 - a, a - 1)
        down = jnp.where(s == 0, a - 1, N_A - 2 - a)
        return [
            (up >= 0, down >= 0, rcopy(
                row_out.at[step], row_in.at[step],
                h_send.at[step, 0], h_recv.at[step, 0], {"aa": lax.rem(a + 1 + (N_A - 2) * s, N_A)})),
            (b < N_B - 1, b > 0, rcopy(
                edge.at[step, 1], edge_in.at[step, 0],
                h_send.at[step, 1], h_recv.at[step, 1], {"ba": lax.rem(b + 1, N_B)})),
            (b > 0, b < N_B - 1, rcopy(
                edge.at[step, 0], edge_in.at[step, 1],
                h_send.at[step, 2], h_recv.at[step, 2], {"ba": lax.rem(b + N_B - 1, N_B)})),
        ]

    def halo_start(copies, buf, step):
        row_out[step] = buf[ROWS - (ROWS - 1) * s, 8 : 8 + COLS, :].astype(BF16)
        for can, _, c in copies:
            pl.when(can)(c.start)

    def halo_land(copies, buf, step):
        for i, (_, comes, c) in enumerate(copies):
            pl.when(comes)(c.wait_recv)

            @pl.when(jnp.logical_not(comes))
            def _():
                if i == 0:
                    row_in[step] = jnp.zeros((COLS, HALF), BF16)
                else:
                    edge_in[step, i - 1] = jnp.zeros((ROWS, 1, HALF), F32)

        buf[(ROWS + 1) * s, 8 : 8 + COLS, :] = row_in[step].astype(F32)
        for r in range(ROWS):
            buf[r + 1, 7:8, :] = edge_in[step, 0, r]
            buf[r + 1, 8 + COLS : 9 + COLS, :] = edge_in[step, 1, r]

    def halo_sent(copies):
        for can, _, c in copies:
            pl.when(can)(c.wait_send)

    coef_copy.wait()

    def masked(g, carry):
        rows = []
        for i in range(8):
            order = a * BLOCK + g * 8 + i
            block = jnp.concatenate([coef[g * 8 + i, p].astype(F32) for p in range(2)], axis=0)
            rows.append(jnp.where(lanes(8, NT) >= order, block, 0.0))
        degrees[g] = jnp.concatenate(rows, axis=0).astype(BF16)
        return carry

    lax.fori_loop(0, GROUPS, masked, 0)

    def legendre(g, carry):
        leg_copies(g).wait()
        cross = dot(degrees[g], leg[pl.ds(g * 8, 8)].reshape(256, NT), ((1,), (1,)))
        at = pl.ds(pl.multiple_of(g * 8, 8), 8)
        for t in range(2):
            kept = cross[t * 32 : t * 32 + 8, t * 128 : t * 128 + 128]
            for q in range(1, 4):
                m = t * 4 + q
                kept = jnp.where(lanes(8) >= q * 32, cross[m * 8 : m * 8 + 8, t * 128 : t * 128 + 128], kept)
            sall[at, t * 128 : t * 128 + 128] = kept
        return carry

    lax.fori_loop(0, GROUPS, legendre, 0)

    i, o = sublanes(256, 256), lanes(256, 256)
    moved = dot(sall[...].astype(BF16), one_hot(o == (i & 31) // 4 * 32 + (i // 32) * 4 + (i & 3)))
    turned = {}
    for t in range(N_A):
        for q in range(3):
            acc = jnp.zeros((8, 128), F32)
            for g in range(q * 4, min(q * 4 + 4, GROUPS)):
                shift = 32 * ((g - t) % 4)
                key = (g, t // 4, shift)
                if key not in turned:
                    v = moved[g * 8 : g * 8 + 8, t // 4 * 128 : t // 4 * 128 + 128]
                    turned[key] = pltpu.roll(v, shift, axis=1) if shift else v
                at = lanes(8) // 32 == g % 4
                acc = jnp.where(at, turned[key], acc)
            msg[t, :, q * 128 : q * 128 + 128] = acc

    pl.semaphore_wait(barrier, N_A + N_B - 1 + jnp.where(b == 0, N_A - 1, 0))
    sent = []
    for d, t in enumerate(peers_a):
        c = rcopy(msg.at[t], a2a.at[a], a_send.at[d], a_recv.at[a], {"aa": t})
        c.start()
        sent.append(c)
    crossed = []
    for d, t in enumerate(peers_a + [a]):
        crossed.append(
            rcopy(msg.at[t], a2x.at[a], x_send.at[d], x_recv.at[a], {"comp": 1 - s, "aa": t})
        )

    @pl.when(b == 0)
    def _():
        for c in crossed:
            c.start()

    a2a[a] = msg[a]


    for c in small:
        c.wait()
    sea = mask_in[...].astype(F32)
    for r in range(ROWS):
        mask_b[r * COLS : (r + 1) * COLS, :] = spread(sea[r : r + 1, :], COLS)

    def first(r, carry):
        m = mask_b[pl.ds(r * COLS, COLS), :]
        for j, w in TILES:
            v = spec[r, :, j : j + w] * m[:, :w]
            buf_a[r + 1, 8 : 8 + COLS, j : j + w] = v
            edge[0, 0, r, :, j : j + w] = v[0:1, :]
            edge[0, 1, r, :, j : j + w] = v[COLS - 1 : COLS, :]
        return carry

    lax.fori_loop(0, ROWS, first, 0)

    halo_a = halo(buf_a, 0)
    halo_start(halo_a, buf_a, 0)

    def tables(out, l, k, active):
        w = k.shape[1]
        count = jnp.full((1, w), cp_ref[a * CYCLES + l], jnp.int32).astype(F32)
        inv = 1.0 / count
        cu, su = turn(sublanes(WAVES // 8, w).astype(F32) * 8.0 * k, count, inv)
        ca[:, :, :w] = cu.reshape(GROUPS, 8, w)
        sa[:, :, :w] = su.reshape(GROUPS, 8, w)
        cv, sv = turn(sublanes(8, w).astype(F32) * k, count, inv)
        cv, sv = cv * active, sv * active
        minus_c, minus_s = -cv, -sv

        def block(i, carry):
            for h in range(4):
                cs, ss = [], []
                for o in range(h * 2, h * 2 + 2):
                    c0, s0 = ca[i, o : o + 1, :w], sa[i, o : o + 1, :w]
                    cs.append(c0 * cv + s0 * minus_s)
                    ss.append(s0 * minus_c + c0 * minus_s)
                at = pl.multiple_of(i * 64 + h * 16, 16)
                out[l, pl.ds(at, 16), :] = jnp.concatenate(cs, axis=0).astype(BF16)
                out[l, pl.ds(WAVES + at, 16), :] = jnp.concatenate(ss, axis=0).astype(BF16)
            return carry

        lax.fori_loop(0, GROUPS, block, 0)
        top = out[l, 0:16, :].astype(F32)
        out[l, 0:16, :] = jnp.where(sublanes(16, w) == 0, top * 0.5, top).astype(BF16)

    near = wc[:, pl.ds(pl.multiple_of(b // 4 * 128, 128), 128)].astype(F32)
    near = pltpu.roll(near, (4 - b % 4) % 4 * COLS, axis=1)
    near = jnp.where(lanes(ROWS) < COLS, near, 0.0)
    side = near
    for q in range(1, 4):
        side = jnp.where(sublanes(ROWS) % 4 == q, pltpu.roll(near, q * COLS, axis=1), side)
    for l in range(CYCLES):
        tables(ptable, l, jnp.sum(side[l * 4 : l * 4 + 4, :], axis=0, keepdims=True), 2.0)

    slots = lanes(1, SLOTS) + b * SLOTS
    for l in range(CYCLES):
        active = jnp.where(slots < cp_ref[a * CYCLES + l], 2.0, 0.0)
        tables(table, l, slots.astype(F32), active)

    i, o = sublanes(384, 512), lanes(384, 512)
    order_in[...] = one_hot((o == (i & 3) * 128 + i // 4) & (i < BLOCK * 4))
    r = sublanes(64, 64)
    order_out[...] = one_hot(lanes(64, 64) == (r & 15) // 4 * 16 + r // 16 * 4 + (r & 3))

    def upwind(buf, r, j, w):
        c = lambda i: cst_ref[s, i : i + 1, j : j + w]
        here = buf[r + 1, 8 : 8 + COLS, j : j + w]
        ux = jnp.where(c(SE) > 0.0, buf[r + 1, 7 : 7 + COLS, j : j + w], buf[r + 1, 9 : 9 + COLS, j : j + w])
        uy = buf[r + 2 * s, 8 : 8 + COLS, j : j + w]
        return here * c(CC) + ux * c(AE) + uy * c(AN)

    halo_land(halo_a, buf_a, 0)

    def second(r, carry):
        m = mask_b[pl.ds(r * COLS, COLS), :]
        for j, w in TILES:
            v = upwind(buf_a, r, j, w) * m[:, :w]
            buf_b[r + 1, 8 : 8 + COLS, j : j + w] = v
            edge[1, 0, r, :, j : j + w] = v[0:1, :]
            edge[1, 1, r, :, j : j + w] = v[COLS - 1 : COLS, :]
        return carry

    lax.fori_loop(0, ROWS // 2, lambda r, c: second(2 * r + 1, second(2 * r, c)), 0)
    halo_b = halo(buf_b, 1)
    halo_start(halo_b, buf_b, 1)

    def compact(landed):
        wide = dot(landed[...].reshape(64, 384).astype(BF16), order_in[...])
        out = []
        for l in range(CYCLES):
            tiles = [jnp.zeros((8, 128), F32) for _ in range(WAVES // 128)]
            for c in range(N_A):
                t, shift = divmod(c * BLOCK, 128)
                piece = wide[c * 8 : c * 8 + 8, l * 128 : l * 128 + 128]
                if shift:
                    piece = pltpu.roll(piece, shift, axis=1)
                    tiles[t] = jnp.where(lanes(8) >= shift, piece, tiles[t])
                    if shift + BLOCK > 128:
                        tiles[t + 1] = jnp.where(lanes(8) < shift, piece, tiles[t + 1])
                else:
                    tiles[t] = jnp.where(lanes(8) < BLOCK, piece, tiles[t])
            out.append(tiles)
        return out

    def lowest(blocks, base):
        for l in range(CYCLES):
            for t in range(WAVES // 128):
                for p in range(2):
                    r = base + p * 4 + l
                    low_f[r : r + 1, t * 128 : t * 128 + 128] = blocks[l][t][p * 4 : p * 4 + 1, :]

    for d, c in enumerate(peers_a):
        rcopy(msg.at[0], a2a.at[c], a_send.at[d], a_recv.at[c], {"aa": c}).wait_recv()
    blocks = compact(a2a)
    low = [
        rcopy(l0, l0, l_send.at[d], l_recv.at[0], {"ba": t}) for d, t in enumerate(peers_b)
    ]

    @pl.when(b == 0)
    def _():
        lowest(blocks, 0)
        for d, c in enumerate(peers_a + [a]):
            rcopy(msg.at[0], a2x.at[c], x_send.at[d], x_recv.at[c], {"comp": 1 - s, "aa": c}).wait_recv()
        lowest(compact(a2x), 8)
        l0[...] = low_f[...].astype(BF16)
        for c in low:
            c.start()

    for t in range(WAVES // 128):
        up = [pltpu.roll(blocks[l][t], 4, axis=0) for l in range(CYCLES)]
        own = [blocks[l][t] for l in range(CYCLES)]
        top = sublanes(8) < 4
        for p in range(2):
            pair = [
                jnp.where(top, own[l], up[l + 1]) if p == 0 else jnp.where(top, up[l], own[l + 1])
                for l in (0, 2)
            ]
            at = p * WAVES + t * 128
            gath[b, :, at : at + 128] = jnp.concatenate(pair, axis=0).astype(BF16)

    gathers = []

    def give(o, device):
        c = rcopy(gath.at[o], gath.at[o], g_send.at[len(gathers)], g_recv.at[o], {"ba": device})
        c.start()
        gathers.append(c)

    def arrived(o):
        rcopy(gath.at[o], gath.at[o], g_send.at[0], g_recv.at[o], {"ba": o}).wait_recv()

    x_peers = [lax.rem(x + d, N_X) * N_Z + z for d in (1, 3, 2)]
    for d in range(1, N_Z):
        give(b, x * N_Z + lax.rem(z + d, N_Z))

    halo_land(halo_b, buf_b, 1)

    def third(r, carry):
        at = pl.ds(r * COLS, COLS)
        m = mask_b[at, :]
        total = jnp.zeros((COLS, 128), F32)
        for j, w in TILES:
            v = upwind(buf_b, r, j, w) * m[:, :w]
            d2[r, :, j : j + w] = v
            term = v * cst_ref[s, WB : WB + 1, j : j + w]
            if w == 128:
                total = total + term
            else:
                part[0, at, :] = total
                part[0, at, :w] = total[:, :w] + term
        return carry

    lax.fori_loop(0, ROWS // 2, lambda r, c: third(2 * r + 1, third(2 * r, c)), 0)
    energy_copy = rcopy(part.at[0], part_in, c_send.at[0], c_recv.at[0], partner)
    energy_copy.start()

    for t in x_peers:
        give(b, t)
    for d in range(1, N_Z):
        o = x * N_Z + lax.rem(z + N_Z - d, N_Z)
        arrived(o)
        for t in x_peers:
            give(o, t)

    @pl.when(b > 0)
    def _():
        low[0].wait_recv()

    own, other = [], []
    for l in range(CYCLES):
        pc = dot(l0[...], ptable[l, 0:WAVES, :])
        ps = dot(l0[...], ptable[l, WAVES:, :])
        own.append((pc[l : l + 1, :] + ps[4 + l : 5 + l, :]).astype(BF16).astype(F32))
        other.append((pc[8 + l : 9 + l, :] + ps[12 + l : 13 + l, :]).astype(BF16).astype(F32))
    east = [jnp.where(s == 0, p, q) for p, q in zip(own, other)]
    north = [jnp.where(s == 0, q, p) for p, q in zip(own, other)]
    for l in range(CYCLES):
        east_b[pl.ds(l * POINTS, POINTS), :] = spread(east[l], POINTS)
        north_b[pl.ds(l * POINTS, POINTS), :] = spread(north[l], POINTS)

    def gain_of(e, n, r, j, w):
        c = lambda i: cst_ref[s, i : i + 1, j : j + w]
        align = e[:, :w] * c(QE) + n[:, :w] * c(QN)
        grown = 0.05 * jnp.maximum(align - 1.0, 0.0) * d2[r, :, j : j + w]
        return align, grown

    def fourth(r, carry):
        at = pl.ds(r * COLS, COLS)
        e, n = east_b[at, :], north_b[at, :]
        total = jnp.zeros((COLS, 128), F32)
        for j, w in TILES:
            align, grown = gain_of(e, n, r, j, w)
            term = grown * align * cst_ref[s, WB : WB + 1, j : j + w]
            if w == 128:
                total = total + term
            else:
                part[1, at, :] = total
                part[1, at, :w] = total[:, :w] + term
        return carry

    lax.fori_loop(0, ROWS // 2, lambda r, c: fourth(2 * r + 1, fourth(2 * r, c)), 0)
    for l in range(CYCLES):
        total = jnp.sum(part[1, pl.ds(l * POINTS, POINTS), :], axis=1, keepdims=True)
        kept = jnp.where(sublanes(POINTS) == lanes(POINTS), jnp.broadcast_to(total, (POINTS, 128)), 0.0)
        row = jnp.sum(kept, axis=0, keepdims=True)
        st[l : l + 1, :] = row
        st[4 + l : 5 + l, :] = row
    stress_copy = rcopy(st, st_in, c_send.at[1], c_recv.at[1], partner)
    stress_copy.start()

    energy_copy.wait_recv()
    for l in range(CYCLES):
        at = pl.ds(l * POINTS, POINTS)
        level = jnp.sum(part[0, at, :] + part_in[at, :], axis=1, keepdims=True) * 0.125
        mask_b[at, :] = jnp.broadcast_to(level * level, (POINTS, 128))

    def fifth(r, carry):
        at = pl.ds(r * COLS, COLS)
        e, n = east_b[at, :], north_b[at, :]
        square = mask_b[at, :]
        for j, w in TILES:
            _, grown = gain_of(e, n, r, j, w)
            decay = square[:, :w] * cst_ref[s, DF : DF + 1, j : j + w]
            ws_ref[r, :, j : j + w] = (d2[r, :, j : j + w] + grown) / (1.0 + decay)
        return carry

    lax.fori_loop(0, ROWS // 2, lambda r, c: fifth(2 * r + 1, fifth(2 * r, c)), 0)
    ws_copy = pltpu.make_async_copy(ws_ref, ws_out, o_sem.at[0])
    ws_copy.start()

    stress_copy.wait_recv()
    e, n = jnp.concatenate(east * 2, axis=0), jnp.concatenate(north * 2, axis=0)
    rough[b] = jnp.sqrt(1.0 + 0.03 * (st[...] + st_in[...]) / (0.12 * (e * e + n * n) + 0.02))
    rough_copies = []
    for d, t in enumerate(peers_b):
        rough_copies.append(rcopy(rough.at[b], rough.at[b], r_send.at[d], r_recv.at[b], {"ba": t}))
        rough_copies[-1].start()

    for xd in (0, 1, 3, 2):
        col = lax.rem(x + xd, N_X)
        if xd:
            for zd in range(N_Z):
                arrived(col * N_Z + lax.rem(z + zd, N_Z))
        block = gath[pl.ds(col * N_Z, N_Z)].reshape(64, 2 * WAVES)
        gperm[...] = dot(order_out[...], block).astype(BF16)
        for l in range(CYCLES):
            gw_ref[0, l, pl.ds(pl.multiple_of(col * 16, 16), 16), :] = dot(
                gperm[l * 16 : l * 16 + 16, :], table[l]
            ).astype(BF16)
    gw_copy = pltpu.make_async_copy(gw_ref, gw_out, o_sem.at[1])
    gw_copy.start()

    for d, t in enumerate(peers_b):
        rcopy(rough.at[t], rough.at[t], r_send.at[d], r_recv.at[t], {"ba": t}).wait_recv()
    rough_copy = pltpu.make_async_copy(rough, rough_out, o_sem.at[2])
    rough_copy.start()
    for c in sent + gathers + rough_copies + [energy_copy, stress_copy]:
        c.wait_send()
    halo_sent(halo_a)
    halo_sent(halo_b)

    @pl.when(b == 0)
    def _():
        for c in low + crossed:
            c.wait_send()

    for c in (ws_copy, gw_copy, rough_copy):
        c.wait()


def last(
    cp_hbm, gw_in, ws_in, rough_in, rs_hbm, gw_ref, ws_ref, ch_ref, cp_ref, gw, ws, rough, rs_ref, sem_in, sem_out
):
    a = lax.axis_index("aa")
    slots = lanes(1, SLOTS) + lax.axis_index("ba") * SLOTS
    step = ROWS // 4
    blocks = [pl.ds(i * step, step) for i in range(4)]
    come = [pltpu.make_async_copy(ws_in.at[k], ws.at[k], sem_in.at[i]) for i, k in enumerate(blocks)]
    come.append(pltpu.make_async_copy(gw_in, gw, sem_in.at[4]))
    go = [pltpu.make_async_copy(ws.at[k], ws_ref.at[k], sem_out.at[i]) for i, k in enumerate(blocks)]
    go.append(pltpu.make_async_copy(gw, gw_ref, sem_out.at[4]))
    other = [
        pltpu.make_async_copy(rough_in, rough, sem_in.at[5]),
        pltpu.make_async_copy(rs_hbm, rs_ref, sem_in.at[6]),
        pltpu.make_async_copy(cp_hbm, cp_ref, sem_in.at[7]),
    ]
    for c in other + come:
        c.start()
    for c, d in zip(come, go):
        c.wait()
        d.start()
    for c in other:
        c.wait()
    for l in range(CYCLES):
        source = rs_ref[l : l + 1, :]
        low_part = ((source >> 9) & 3) * 32 + (source & 31)
        high_part = (source >> 5) & 15
        pick = one_hot(sublanes(128, SLOTS) == low_part)
        values = rough[:, l, :]
        h0 = values.astype(BF16)
        r1 = values - h0.astype(F32)
        h1 = r1.astype(BF16)
        h2 = (r1 - h1.astype(F32)).astype(BF16)
        got = dot(h0, pick) + (dot(h1, pick) + dot(h2, pick))
        keep = sublanes(N_B, SLOTS) == high_part
        row = jnp.sum(jnp.where(keep, got, 0.0), axis=0, keepdims=True)
        ch_ref[l : l + 1, :] = jnp.where(slots < cp_ref[a * CYCLES + l], row, 0.0)
    for c in go:
        c.wait()


def per_device(legendre, coefficients, cycle_points, spectra, sea_mask, wind_column, roughness_source):
    vmem = pl.BlockSpec(memory_space=pltpu.VMEM)
    smem = pl.BlockSpec(memory_space=pltpu.SMEM)
    hbm = pl.BlockSpec(memory_space=pltpu.HBM)
    dma = pltpu.SemaphoreType.DMA
    winds = jax.ShapeDtypeStruct((1, CYCLES, 64, SLOTS), BF16)
    waves = jax.ShapeDtypeStruct((ROWS, COLS, HALF), F32)
    winds_done, waves_done, rough = pl.pallas_call(
        kernel,
        out_shape=(winds, waves, jax.ShapeDtypeStruct((N_B, 8, 128), F32)),
        in_specs=[hbm] * 7,
        out_specs=(hbm, hbm, hbm),
        scratch_shapes=[
            pltpu.VMEM((1, CYCLES, 64, SLOTS), BF16),
            pltpu.VMEM((ROWS, COLS, HALF), F32),
            pltpu.VMEM((N_B, 8, 128), F32),
            pltpu.SMEM((32,), jnp.int32),
            pltpu.VMEM((BLOCK, 32, NT), BF16),
            pltpu.VMEM((BLOCK, 2, 4, NT), BF16),
            pltpu.VMEM((GROUPS, 64, NT), BF16),
            pltpu.VMEM((ROWS, COLS, HALF), F32),
            pltpu.VMEM((ROWS, COLS), jnp.int32),
            pltpu.VMEM((ROWS, 512), jnp.int32),
            pltpu.VMEM((2, 16, HALF), F32),
            pltpu.VMEM((BLOCK, 256), F32),
            pltpu.VMEM((N_A, 8, 384), F32),
            pltpu.VMEM((N_A, 8, 384), F32),
            pltpu.VMEM((N_A, 8, 384), F32),
            pltpu.VMEM((N_B, 16, 2 * WAVES), BF16),
            pltpu.VMEM((64, 2 * WAVES), BF16),
            pltpu.VMEM((16, WAVES), F32),
            pltpu.VMEM((16, WAVES), BF16),
            pltpu.VMEM((CYCLES, 2 * WAVES, SLOTS), BF16),
            pltpu.VMEM((CYCLES, 2 * WAVES, POINTS), BF16),
            pltpu.VMEM((GROUPS, 8, SLOTS), F32),
            pltpu.VMEM((GROUPS, 8, SLOTS), F32),
            pltpu.VMEM((ROWS + 2, COLS + 16, HALF), F32),
            pltpu.VMEM((ROWS + 2, COLS + 16, HALF), F32),
            pltpu.VMEM((ROWS, COLS, HALF), F32),
            pltpu.VMEM((2, 2, ROWS, 1, HALF), F32),
            pltpu.VMEM((2, 2, ROWS, 1, HALF), F32),
            pltpu.VMEM((2, COLS, HALF), BF16),
            pltpu.VMEM((2, COLS, HALF), BF16),
            pltpu.VMEM((ROWS * COLS, 128), F32),
            pltpu.VMEM((ROWS * COLS, 128), F32),
            pltpu.VMEM((ROWS * COLS, 128), F32),
            pltpu.VMEM((2, ROWS * COLS, 128), F32),
            pltpu.VMEM((ROWS * COLS, 128), F32),
            pltpu.VMEM((8, 128), F32),
            pltpu.VMEM((8, 128), F32),
            pltpu.VMEM((384, 512), BF16),
            pltpu.VMEM((64, 64), BF16),
            dma((6,)), dma((GROUPS,)),
            dma((N_A - 1,)), dma((N_A,)),
            dma((N_A,)), dma((N_A,)),
            dma((N_B - 1,)), dma((N_B,)),
            dma((N_B - 1,)), dma((1,)),
            dma((2, 3)), dma((2, 3)),
            dma((2,)), dma((2,)),
            dma((N_B - 1,)), dma((N_B,)),
            dma((3,)),
        ],
        compiler_params=pltpu.CompilerParams(
            collective_id=0, has_side_effects=True, vmem_limit_bytes=VMEM
        ),
    )(
        cycle_points, legendre, coefficients.reshape(BLOCK, 2, 4, NT), spectra, sea_mask, wind_column,
        jnp.asarray(bin_table()),
    )
    return pl.pallas_call(
        last,
        out_shape=(winds, waves, jax.ShapeDtypeStruct((CYCLES, SLOTS), F32)),
        in_specs=[hbm] * 5,
        out_specs=(hbm, hbm, vmem),
        scratch_shapes=[
            pltpu.SMEM((32,), jnp.int32),
            pltpu.VMEM((1, CYCLES, 64, SLOTS), BF16),
            pltpu.VMEM((ROWS, COLS, HALF), F32),
            pltpu.VMEM((N_B, 8, 128), F32),
            pltpu.VMEM((CYCLES, SLOTS), jnp.int32),
            dma((8,)), dma((5,)),
        ],
        compiler_params=pltpu.CompilerParams(vmem_limit_bytes=VMEM),
    )(cycle_points, winds_done, waves_done, rough, roughness_source)


def solution(mesh):
    in_specs = (
        P("aa", None, None),
        P("comp", "aa", None, "ba", None),
        P(),
        P("aa", "ba", "comp"),
        P("aa", "ba"),
        P("aa", None),
        P("aa", "ba"),
    )
    out_specs = (P("comp", "aa", None, "ba"), P("aa", "ba", "comp"), P("aa", "ba"))
    return jax.shard_map(
        per_device, mesh=mesh, in_specs=in_specs, out_specs=out_specs, check_vma=False
    )
```
